32 devices in a mesh: survey: 2 (over x), freq: 16 (over z, y, core).
Axes of the slice: x: 2, y: 2, z: 4, core: 2. Of those that a mesh axis runs over, the one named last changes fastest.
Arguments:
- gathers: float32 [4096, 2048], P(('survey', 'freq')), parts along dimension 0, may hold values from -6 to 6
- operator: bfloat16 [64, 2, 1024, 1024], P(('survey', 'freq')), parts along dimension 0, may hold values from -0.125 to 0.125
- filters: float32 [32, 4, 9, 31], P(('survey', 'freq')), parts along dimension 0, may hold values from -0.18 to 0.18
- tile_of: int32 [32], P('survey'), parts along dimension 0, may hold values from 0 to 15, each once
- slice_len: int32 [32], P('survey'), parts along dimension 0, may hold values from 1 to 2, 20 in all
Outputs:
- primaries: float32 [4096, 2048], P(('survey', 'freq')), parts along dimension 0
The draws below stay inside these ranges and needn't reach their ends.
There are 2 independent parts, one for each index of `survey`. The reference program is written for one: setup_inputs(seed, part) draws one part's arguments, and reference() takes and returns one part's arrays. A program takes and returns all parts, laid end to end along the dimension named above; each array names one. Nothing has to cross between parts.
Inputs may be any that keep to these rules, and one draw needn't show every extreme that they name: `tile_of`: each tile is held by exactly one block of rows. `slice_len`: the entries sum to 20; the largest equals 2.
All inputs are finite; a program needn't handle non-finite values.
Results may differ from the reference program's by a relative error of at most 0.0027.
Values may be sent and summed in bfloat16 or wider, within the bound.
No kernel may reach another device: no remote copies, remote signals or barrier semaphores. Data moves between devices by JAX's collectives and lax.ppermute only.
A program may use at most 64 MiB of HBM per device.

```python
import math
import jax
import jax.numpy as jnp
import numpy as np
from jax import lax

R = 1024
NT = 2048
TRACES_DEV = 128
MOST = 2
FIRST = 40
SHOTS = 2
BAND = 32
KEPT = 20
N_FREQ = 16


def block_levels(own_key, dims, cuts, least, high):
    gain, own = 1.0, jax.random.fold_in(own_key, 6)
    for dim, shards_of in cuts:
        steps = jnp.exp(jax.random.uniform(jax.random.fold_in(own, dim), (shards_of,), jnp.float32, least / len(cuts), high / len(cuts)))
        gain = gain * jnp.repeat(steps, dims[dim] // shards_of).reshape([-1 if axis == dim else 1 for axis in range(len(dims))])
    return gain


def split_up(amount, total, most, skew):
    loads = [(1 << 20) // math.isqrt(rank ** skew) + 1 for rank in range(2, amount + 1)]
    spare, counts = total - most - (amount - 1), [1] * (amount - 1)
    while spare > 0:
        free = [i for i in range(amount - 1) if counts[i] < most]
        pool, remaining = sum([loads[i] for i in free]), spare
        for i in free:
            extra = min(most - counts[i], max(1, remaining * loads[i] // pool), spare)
            counts[i] = counts[i] + extra
            spare = spare - extra
    return np.array([most] + counts)


def uneven(rng, amount, total, reach, lean):
    if amount == 2:
        one = jax.random.randint(rng, (), max(1, total - reach), min(reach, total - 1) + 1)
        return jnp.stack([one, total - one])
    tallies = jnp.asarray(split_up(amount, total, reach, lean), jnp.int32)
    pairs = (amount - 1) // 2
    source_of, receiver = tallies[1:1 + 2 * pairs:2], tallies[2:2 + 2 * pairs:2]
    room = jnp.minimum(source_of - 1, reach - receiver)
    passed = jax.random.randint(jax.random.fold_in(rng, 1), (pairs,), 0, 1 << 20) % (room + 1)
    tallies = tallies.at[1:1 + 2 * pairs:2].set(source_of - passed).at[2:2 + 2 * pairs:2].set(receiver + passed)
    return tallies[jax.random.permutation(jax.random.fold_in(rng, 2), amount)]


def scatter_about(own_key, shape, width, bound, split=(), kind=jnp.bfloat16):
    factor_of = block_levels(own_key, shape, split, -0.22, 0.18) if split else 1.0
    drawn = jax.random.normal(own_key, shape, jnp.float32) * width * factor_of
    return jnp.minimum(jnp.maximum(drawn, -bound), bound).astype(kind)


def setup_inputs(seed: int = 0, part: int = 0) -> dict:
    keys = jax.random.split(jax.random.key(seed), 6)
    part_keys = jax.random.split(jax.random.fold_in(keys[5], part), 6)
    return {
        "gathers": scatter_about(part_keys[0], (N_FREQ * TRACES_DEV, NT), 1.0, 6.0, ((0, 16),), jnp.float32),
        "operator": scatter_about(part_keys[1], (BAND, 2, R, R), (2 * R) ** -0.5, 0.125, ((0, 16),)),
        "filters": scatter_about(part_keys[2], (N_FREQ, 4, 9, 31), 0.03, 0.18, ((0, 16),), jnp.float32),
        "tile_of": jax.random.permutation(part_keys[3], N_FREQ).astype(jnp.int32),
        "slice_len": uneven(part_keys[4], N_FREQ, KEPT, MOST, 2).astype(jnp.int32),
    }


def band_tables(first_bin, band_bins, length):
    bin_ids = first_bin + jnp.arange(band_bins, dtype=jnp.int32)
    time_ids = jnp.arange(length, dtype=jnp.int32)
    phase_ids = bin_ids[:, None] * time_ids[None, :] % length
    angles = 2.0 * math.pi / length * phase_ids.astype(jnp.float32)
    return (jnp.cos(angles), jnp.sin(angles))

def forward_table(first_bin, band_bins, length):
    cosine_rows, sine_rows = band_tables(first_bin, band_bins, length)
    return jnp.concatenate([cosine_rows, -sine_rows], axis=0) * (1.0 / math.sqrt(length))

def band_mask(slice_len, band_bins, slot_count):
    bin_ids = jnp.arange(band_bins, dtype=jnp.int32)
    device_ids = jnp.arange(slice_len.shape[0], dtype=jnp.int32)
    group_ids = bin_ids // slot_count
    kept_count = lax.optimization_barrier(jnp.sum(jnp.where(group_ids[:, None] == device_ids[None, :], slice_len[None, :], 0), axis=1))
    return (bin_ids % slot_count < kept_count).astype(jnp.float32)

def match_response(band_rows, kept, filters, first_bin, length, kept_bins):
    band_bins = band_rows.shape[0]
    traces = band_rows.shape[2] - 8
    bin_ids = first_bin + jnp.arange(band_bins, dtype=jnp.int32)
    lag_ids = jnp.arange(31, dtype=jnp.int32) - 15
    phase_ids = bin_ids[:, None] * lag_ids[None, :] % length
    angles = 2.0 * math.pi / length * phase_ids.astype(jnp.float32)
    h_real = jnp.einsum('cab,fb->caf', filters, jnp.cos(angles), precision=lax.Precision.HIGHEST)
    h_imag = jnp.einsum('cab,fb->caf', filters, jnp.sin(angles), precision=lax.Precision.HIGHEST)
    weight = bin_ids.astype(jnp.float32) / (first_bin + band_bins)
    k_real = h_real[0] + h_imag[1] - weight * h_imag[2] + weight * h_real[3]
    k_imag = h_imag[0] - h_real[1] + weight * h_real[2] + weight * h_imag[3]
    rows = band_rows.astype(jnp.float32)
    s_real = jnp.zeros((band_bins, traces), jnp.float32)
    s_imag = jnp.zeros((band_bins, traces), jnp.float32)
    for offset in range(9):
        real_rows = rows[:, 0, offset:offset + traces]
        imag_rows = rows[:, 1, offset:offset + traces]
        s_real = s_real + k_real[offset][:, None] * real_rows - k_imag[offset][:, None] * imag_rows
        s_imag = s_imag + k_real[offset][:, None] * imag_rows + k_imag[offset][:, None] * real_rows
    scale = (math.sqrt(2.0 / kept_bins) * kept)[:, None]
    stacked = jnp.concatenate([s_real * scale, s_imag * scale], axis=0)
    cosine_rows, sine_rows = band_tables(first_bin, band_bins, length)
    table = jnp.concatenate([cosine_rows, -sine_rows], axis=0)
    return lax.dot_general(stacked, table, (((0,), (0,)), ((), ())), precision=lax.Precision.HIGHEST, preferred_element_type=jnp.float32)

def predict(pair):
    spec_plane, operator_pair = pair
    contract = (((1,), (1,)), ((), ()))

    def multiply(left, right):
        return lax.dot_general(left, right, contract, preferred_element_type=jnp.float32)
    real_part = multiply(spec_plane[0], operator_pair[0]) - multiply(spec_plane[1], operator_pair[1])
    imag_part = multiply(spec_plane[0], operator_pair[1]) + multiply(spec_plane[1], operator_pair[0])
    return jnp.stack([real_part, imag_part]).astype(jnp.bfloat16)

def reference(gathers, operator, filters, tile_of, slice_len):
    per_shot = R // TRACES_DEV
    holder = jnp.argsort(tile_of).astype(jnp.int32)
    blocks = gathers.reshape(N_FREQ, TRACES_DEV, NT)
    ordered = jnp.take(blocks, holder, axis=0).reshape(SHOTS * R, NT)
    spectrum = lax.dot_general(forward_table(FIRST, BAND, NT), ordered, (((1,), (1,)), ((), ())), precision=lax.Precision.HIGHEST, preferred_element_type=jnp.float32)
    spectrum = spectrum.astype(jnp.bfloat16).reshape(2, BAND, SHOTS, R)
    predicted = lax.map(predict, (jnp.moveaxis(spectrum, 1, 0), operator))
    widened = jnp.pad(predicted, ((0, 0), (0, 0), (0, 0), (4, 4)))
    kept = band_mask(slice_len, BAND, MOST)

    def cleaned(device_index):
        tile_index = tile_of[device_index]
        shot_index = tile_index // per_shot
        start_index = tile_index % per_shot * TRACES_DEV
        anchor = jnp.zeros((), jnp.int32)
        piece = lax.dynamic_slice(widened, (anchor, anchor, shot_index, start_index), (BAND, 2, 1, TRACES_DEV + 8))[:, :, 0]
        response = match_response(piece, kept, filters[device_index], FIRST, NT, KEPT)
        return blocks[device_index] - response
    result = lax.map(cleaned, jnp.arange(N_FREQ, dtype=jnp.int32))
    return result.reshape(N_FREQ * TRACES_DEV, NT)
```

```python
import functools
import math

import jax
import jax.numpy as jnp
import ml_dtypes
import numpy as np
from jax import lax
from jax.experimental import pallas as pl
from jax.experimental.pallas import tpu as pltpu
from jax.sharding import PartitionSpec as P

FIRST = 40
REACH = 4
VMEM_LIMIT = 40 * 1024 * 1024


def split_halves(values):
    values = values.astype(np.float32)
    high = values.astype(ml_dtypes.bfloat16)
    low = (values - high.astype(np.float32)).astype(ml_dtypes.bfloat16)
    return high, low


def row_tables(band_bins, length):
    bin_ids = FIRST + np.arange(band_bins)
    angles = 2.0 * np.pi / length * (bin_ids[:, None] * np.arange(length)[None, :] % length)
    return np.stack([np.cos(angles), -np.sin(angles)], axis=1).reshape(2 * band_bins, length)


def lag_tables(band_bins, lags, length):
    bin_ids = FIRST + np.arange(band_bins)
    lag_ids = np.arange(lags) - lags // 2
    angles = 2.0 * np.pi / length * (bin_ids[:, None] * lag_ids[None, :] % length)
    cosine, sine = np.cos(angles), np.sin(angles)
    weight = (bin_ids / (FIRST + band_bins))[:, None]
    real = np.stack([cosine, sine, -weight * sine, weight * cosine])
    imag = np.stack([sine, -cosine, weight * cosine, weight * sine])
    own = np.stack([real, real], axis=2).reshape(4, 2 * band_bins, lags)
    partner = np.stack([-imag, imag], axis=2).reshape(4, 2 * band_bins, lags)
    return np.concatenate([own, partner], axis=1).astype(np.float32)


def split_array(values):
    high = values.astype(jnp.bfloat16)
    low = (values - high.astype(jnp.float32)).astype(jnp.bfloat16)
    return high, low


def swap_pairs(values):
    rows = values.shape[0]
    parity = lax.broadcasted_iota(jnp.int32, values.shape, 0) % 2
    return jnp.where(
        parity == 0, pltpu.roll(values, rows - 1, 0), pltpu.roll(values, 1, 0)
    )


def spectrum_kernel(gathers_ref, high_ref, low_ref, out_ref):
    nt = (((1,), (1,)), ((), ()))
    high, low = split_array(gathers_ref[...])
    dot = functools.partial(
        lax.dot_general, dimension_numbers=nt, preferred_element_type=jnp.float32
    )
    total = dot(high_ref[...], high) + (dot(high_ref[...], low) + dot(low_ref[...], high))
    out_ref[...] = total.astype(jnp.bfloat16).reshape(out_ref.shape)


def coefficient_kernel(kept_bins, slots, slice_ref, filters_ref, table_ref, out_ref):
    rows = out_ref.shape[1]
    offsets = filters_ref.shape[2]
    width = out_ref.shape[2]
    total = jnp.zeros((2 * rows, offsets), jnp.float32)
    for part in range(filters_ref.shape[1]):
        total = total + lax.dot_general(
            table_ref[part],
            filters_ref[0, part],
            (((1,), (1,)), ((), ())),
            precision=lax.Precision.HIGHEST,
            preferred_element_type=jnp.float32,
        )
    row_ids = lax.broadcasted_iota(jnp.int32, (rows, width), 0)
    group = row_ids // (2 * slots)
    slot = row_ids // 2 % slots
    count = jnp.zeros((rows, width), jnp.int32)
    for device in range(rows // (2 * slots)):
        count = jnp.where(group == device, slice_ref[device], count)
    scale = jnp.where(slot < count, math.sqrt(2.0 / kept_bins), 0.0)
    for offset in range(offsets):
        out_ref[offset] = total[:rows, offset : offset + 1] * scale
        out_ref[offsets + offset] = total[rows:, offset : offset + 1] * scale


def predict_kernel(tile_ref, incoming_ref, operator_ref, out_ref, holder_ref, tiles_ref):
    devices, group_rows, traces = incoming_ref.shape
    slots, _, receivers, _ = operator_ref.shape
    per_shot = receivers // traces
    shots = devices // per_shot
    for k in range(devices):
        holder_ref[tile_ref[k]] = k
    columns = []
    for q in range(per_shot):
        parts = [
            incoming_ref[holder_ref[s * per_shot + q]].astype(jnp.float32) for s in range(shots)
        ]
        columns.append(jnp.concatenate(parts, axis=0))
    spectrum = jnp.concatenate(columns, axis=1).astype(jnp.bfloat16)
    rows = shots * group_rows
    row_ids = lax.broadcasted_iota(jnp.int32, (rows, receivers), 0)
    dot = functools.partial(
        lax.dot_general,
        dimension_numbers=(((1,), (1,)), ((), ())),
        preferred_element_type=jnp.float32,
    )
    predicted = jnp.zeros((rows, receivers), jnp.float32)
    for slot in range(slots):
        by_real = dot(spectrum, operator_ref[slot, 0])
        by_imag = swap_pairs(dot(spectrum, operator_ref[slot, 1]))
        product = jnp.where(row_ids % 2 == 0, by_real - by_imag, by_real + by_imag)
        predicted = jnp.where(row_ids // 2 % slots == slot, product, predicted)
    for s in range(shots):
        for q in range(per_shot):
            tiles_ref[s * per_shot + q] = predicted[
                s * group_rows : (s + 1) * group_rows, q * traces : (q + 1) * traces
            ]
    lane_ids = lax.broadcasted_iota(jnp.int32, (group_rows, traces), 1)
    for k in range(devices):
        tile = tile_ref[k]
        place = tile % per_shot
        before = tiles_ref[jnp.maximum(tile - 1, 0)]
        after = tiles_ref[jnp.minimum(tile + 1, devices - 1)]
        first_lanes = jnp.where(place < per_shot - 1, REACH, 0)
        last_lanes = jnp.where(place > 0, traces - REACH, traces)
        halo = jnp.where(lane_ids < first_lanes, after, 0.0)
        halo = jnp.where(lane_ids >= last_lanes, before, halo)
        both = jnp.concatenate([tiles_ref[tile], halo], axis=1)
        out_ref[k] = both.astype(jnp.bfloat16)


def subtract_kernel(returned_ref, coefficient_ref, table_ref, gathers_ref, out_ref):
    devices, group_rows, width = returned_ref.shape
    rows = devices * group_rows
    traces = gathers_ref.shape[0]
    own = returned_ref[...].astype(jnp.float32).reshape(rows, width)
    partner = swap_pairs(own)
    offsets = coefficient_ref.shape[0] // 2
    total = jnp.zeros((rows, traces), jnp.float32)
    for offset in range(offsets):
        shift = (offsets // 2 - offset) % width
        moved = pltpu.roll(own, shift, 1)[:, :traces]
        moved_partner = pltpu.roll(partner, shift, 1)[:, :traces]
        total = total + coefficient_ref[offset] * moved
        total = total + coefficient_ref[offsets + offset] * moved_partner
    high, low = split_array(jnp.transpose(total))
    stacked = jnp.concatenate([high, low, high], axis=1)
    response = jnp.dot(stacked, table_ref[...], preferred_element_type=jnp.float32)
    out_ref[...] = gathers_ref[...] - response


def vmem_spec():
    return pl.BlockSpec(memory_space=pltpu.VMEM)


def smem_spec():
    return pl.BlockSpec(memory_space=pltpu.SMEM)


def local(gathers, operator, filters, tile_of, slice_len):
    devices = lax.axis_size("freq")
    traces, length = gathers.shape
    slots, _, receivers, _ = operator.shape
    band_bins = slots * devices
    rows = 2 * band_bins
    group_rows = 2 * slots
    kept_bins = 5 * devices // 4
    offsets, lags = filters.shape[2], filters.shape[3]
    params = pltpu.CompilerParams(vmem_limit_bytes=VMEM_LIMIT)
    table = row_tables(band_bins, length)
    forward_high, forward_low = split_halves(table / math.sqrt(length))
    back_high, back_low = split_halves(table)
    back_table = np.concatenate([back_high, back_high, back_low], axis=0)

    with jax.named_scope("spectrum"):
        outgoing = pl.pallas_call(
            spectrum_kernel,
            out_shape=jax.ShapeDtypeStruct((devices, group_rows, traces), jnp.bfloat16),
            in_specs=[vmem_spec()] * 3,
            out_specs=vmem_spec(),
            compiler_params=params,
            name="spectrum",
        )(gathers, jnp.asarray(forward_high), jnp.asarray(forward_low))
    incoming = lax.all_to_all(outgoing, "freq", split_axis=0, concat_axis=0, tiled=True)
    with jax.named_scope("coefficients"):
        coefficients = pl.pallas_call(
            functools.partial(coefficient_kernel, kept_bins, slots),
            out_shape=jax.ShapeDtypeStruct((2 * offsets, rows, traces), jnp.float32),
            in_specs=[smem_spec(), vmem_spec(), vmem_spec()],
            out_specs=vmem_spec(),
            compiler_params=params,
            name="coefficients",
        )(slice_len, filters, jnp.asarray(lag_tables(band_bins, lags, length)))
    with jax.named_scope("predict"):
        sending = pl.pallas_call(
            predict_kernel,
            out_shape=jax.ShapeDtypeStruct((devices, group_rows, 2 * traces), jnp.bfloat16),
            in_specs=[smem_spec(), vmem_spec(), vmem_spec()],
            out_specs=vmem_spec(),
            scratch_shapes=[
                pltpu.SMEM((devices,), jnp.int32),
                pltpu.VMEM((devices, group_rows, traces), jnp.float32),
            ],
            compiler_params=params,
            name="predict",
        )(tile_of, incoming, operator)
    returned = lax.all_to_all(sending, "freq", split_axis=0, concat_axis=0, tiled=True)
    with jax.named_scope("subtract"):
        return pl.pallas_call(
            subtract_kernel,
            out_shape=jax.ShapeDtypeStruct((traces, length), jnp.float32),
            in_specs=[vmem_spec()] * 4,
            out_specs=vmem_spec(),
            compiler_params=params,
            name="subtract",
        )(returned, coefficients, jnp.asarray(back_table), gathers)


def solution(mesh):
    placed = (
        P(("survey", "freq"), None),
        P(("survey", "freq"), None, None, None),
        P(("survey", "freq"), None, None, None),
        P("survey"),
        P("survey"),
    )
    return jax.shard_map(
        local, mesh=mesh, in_specs=placed, out_specs=P(("survey", "freq"), None), check_vma=False
    )
```

```python
import functools
import math

import jax
import jax.numpy as jnp
import ml_dtypes
import numpy as np
from jax import lax
from jax.experimental import pallas as pl
from jax.experimental.pallas import tpu as pltpu
from jax.sharding import PartitionSpec as P

FIRST = 40
REACH = 4
VMEM_LIMIT = 40 * 1024 * 1024


def split_halves(values):
    values = values.astype(np.float32)
    high = values.astype(ml_dtypes.bfloat16)
    low = (values - high.astype(np.float32)).astype(ml_dtypes.bfloat16)
    return high, low


def row_tables(band_bins, length):
    bin_ids = FIRST + np.arange(band_bins)
    angles = 2.0 * np.pi / length * (bin_ids[:, None] * np.arange(length)[None, :] % length)
    return np.stack([np.cos(angles), -np.sin(angles)], axis=1).reshape(2 * band_bins, length)


def lag_tables(band_bins, lags, length):
    bin_ids = FIRST + np.arange(band_bins)
    lag_ids = np.arange(lags) - lags // 2
    angles = 2.0 * np.pi / length * (bin_ids[:, None] * lag_ids[None, :] % length)
    cosine, sine = np.cos(angles), np.sin(angles)
    weight = (bin_ids / (FIRST + band_bins))[:, None]
    real = np.stack([cosine, sine, -weight * sine, weight * cosine])
    imag = np.stack([sine, -cosine, weight * cosine, weight * sine])
    own = np.stack([real, real], axis=2).reshape(4, 2 * band_bins, lags)
    partner = np.stack([-imag, imag], axis=2).reshape(4, 2 * band_bins, lags)
    return np.concatenate([own, partner], axis=1).astype(np.float32)


def split_array(values):
    high = values.astype(jnp.bfloat16)
    low = (values - high.astype(jnp.float32)).astype(jnp.bfloat16)
    return high, low


def swap_pairs(values):
    rows = values.shape[0]
    parity = lax.broadcasted_iota(jnp.int32, values.shape, 0) % 2
    return jnp.where(
        parity == 0, pltpu.roll(values, rows - 1, 0), pltpu.roll(values, 1, 0)
    )


def spectrum_kernel(chunk, self_ref, gathers_ref, table_ref, *refs):
    outs, (held, table, products, sems) = refs[:-4], refs[-4:]
    devices = len(outs)
    length = gathers_ref.shape[1]
    rows = table_ref.shape[0] // 2
    copies = []
    for step in range(length // chunk):
        part = pl.ds(step * chunk, chunk)
        copies.append(
            (
                pltpu.make_async_copy(gathers_ref.at[:, part], held.at[:, part], sems.at[0, step]),
                pltpu.make_async_copy(table_ref.at[:, part], table.at[:, part], sems.at[1, step]),
            )
        )
    for pair in copies:
        for copy in pair:
            copy.start()
    dot = functools.partial(
        lax.dot_general,
        dimension_numbers=(((1,), (1,)), ((), ())),
        preferred_element_type=jnp.float32,
    )
    total = jnp.zeros((rows, held.shape[0]), jnp.float32)
    for step, pair in enumerate(copies):
        for copy in pair:
            copy.wait()
        part = pl.ds(step * chunk, chunk)
        high, low = split_array(held[:, part])
        weights = table[:, part]
        both = dot(weights, high)
        total = total + both[:rows] + (both[rows:] + dot(weights[:rows], low))
    products[...] = total.reshape(products.shape)
    me = self_ref[0]
    for r in range(devices):
        outs[r][...] = products[me ^ r].astype(jnp.bfloat16)


def prepare_kernel(
    kept_bins, slots, slice_ref, after_ref, filters_ref, table_ref, operator_ref, out_ref, held_ref, sem
):
    copy = pltpu.make_async_copy(operator_ref, held_ref, sem)
    copy.start()
    rows = out_ref.shape[1]
    offsets = filters_ref.shape[2]
    width = out_ref.shape[2]
    total = jnp.zeros((2 * rows, offsets), jnp.float32)
    for part in range(filters_ref.shape[1]):
        total = total + lax.dot_general(
            table_ref[part],
            filters_ref[0, part],
            (((1,), (1,)), ((), ())),
            precision=lax.Precision.HIGHEST,
            preferred_element_type=jnp.float32,
        )
    row_ids = lax.broadcasted_iota(jnp.int32, (rows, width), 0)
    group = row_ids // (2 * slots)
    slot = row_ids // 2 % slots
    count = jnp.zeros((rows, width), jnp.int32)
    for device in range(rows // (2 * slots)):
        count = jnp.where(group == device, slice_ref[device], count)
    scale = jnp.where(slot < count, math.sqrt(2.0 / kept_bins), 0.0)
    for offset in range(offsets):
        out_ref[offset] = total[:rows, offset : offset + 1] * scale
        out_ref[offsets + offset] = total[rows:, offset : offset + 1] * scale
    copy.wait()


def predict_kernel(devices, self_ref, tile_ref, *refs):
    incoming, (operator_ref, out_ref, spectra) = refs[:devices], refs[devices:]
    group_rows, traces = incoming[0].shape
    slots, _, receivers, _ = operator_ref.shape
    per_shot = receivers // traces
    shots = devices // per_shot
    me = self_ref[0]
    for r in range(devices):
        spectra[tile_ref[me ^ r]] = incoming[r][...].astype(jnp.float32)
    columns = []
    for q in range(per_shot):
        parts = [spectra[s * per_shot + q] for s in range(shots)]
        columns.append(jnp.concatenate(parts, axis=0))
    spectrum = jnp.concatenate(columns, axis=1).astype(jnp.bfloat16)
    rows = shots * group_rows
    row_ids = lax.broadcasted_iota(jnp.int32, (rows, receivers), 0)
    dot = functools.partial(
        lax.dot_general,
        dimension_numbers=(((1,), (1,)), ((), ())),
        preferred_element_type=jnp.float32,
    )
    predicted = jnp.zeros((rows, receivers), jnp.float32)
    for slot in range(slots):
        by_real = dot(spectrum, operator_ref[slot, 0])
        by_imag = swap_pairs(dot(spectrum, operator_ref[slot, 1]))
        product = jnp.where(row_ids % 2 == 0, by_real - by_imag, by_real + by_imag)
        predicted = jnp.where(row_ids // 2 % slots == slot, product, predicted)
    for s in range(shots):
        for q in range(per_shot):
            out_ref[s * per_shot + q] = predicted[
                s * group_rows : (s + 1) * group_rows, q * traces : (q + 1) * traces
            ].astype(jnp.bfloat16)


def subtract_kernel(per_shot, tile_ref, returned_ref, coefficient_ref, table_ref, gathers_ref, out_ref):
    devices, tiles, group_rows, traces = returned_ref.shape
    rows = devices * group_rows
    width = 2 * traces
    tile = tile_ref[0]
    place = tile % per_shot

    def held(index):
        return returned_ref[:, index].astype(jnp.float32).reshape(rows, traces)

    lane_ids = lax.broadcasted_iota(jnp.int32, (rows, traces), 1)
    first_lanes = jnp.where(place < per_shot - 1, REACH, 0)
    last_lanes = jnp.where(place > 0, traces - REACH, traces)
    halo = jnp.where(lane_ids < first_lanes, held(jnp.minimum(tile + 1, tiles - 1)), 0.0)
    halo = jnp.where(lane_ids >= last_lanes, held(jnp.maximum(tile - 1, 0)), halo)
    own = jnp.concatenate([held(tile), halo], axis=1)
    partner = swap_pairs(own)
    offsets = coefficient_ref.shape[0] // 2
    total = jnp.zeros((rows, traces), jnp.float32)
    for offset in range(offsets):
        shift = (offsets // 2 - offset) % width
        moved = pltpu.roll(own, shift, 1)[:, :traces]
        moved_partner = pltpu.roll(partner, shift, 1)[:, :traces]
        total = total + coefficient_ref[offset] * moved
        total = total + coefficient_ref[offsets + offset] * moved_partner
    high, low = split_array(jnp.transpose(total))
    stacked = jnp.concatenate([high, low, high], axis=1)
    response = jnp.dot(stacked, table_ref[...], preferred_element_type=jnp.float32)
    out_ref[...] = gathers_ref[...] - response


def vmem_spec():
    return pl.BlockSpec(memory_space=pltpu.VMEM)


def smem_spec():
    return pl.BlockSpec(memory_space=pltpu.SMEM)


def hbm_spec():
    return pl.BlockSpec(memory_space=pltpu.HBM)


def in_hbm(values):
    return pltpu.with_memory_space_constraint(values, pltpu.HBM)


def local(gathers, operator, filters, tile_of, slice_len):
    devices = lax.axis_size("freq")
    traces, length = gathers.shape
    slots, _, receivers, _ = operator.shape
    band_bins = slots * devices
    rows = 2 * band_bins
    group_rows = 2 * slots
    kept_bins = 5 * devices // 4
    offsets, lags = filters.shape[2], filters.shape[3]
    chunk = length // 4
    params = pltpu.CompilerParams(vmem_limit_bytes=VMEM_LIMIT)
    table = row_tables(band_bins, length)
    forward_table = np.concatenate(split_halves(table / math.sqrt(length)), axis=0)
    back_high, back_low = split_halves(table)
    back_table = np.concatenate([back_high, back_high, back_low], axis=0)
    me = lax.axis_index("freq").astype(jnp.int32)
    place = me.reshape(1)

    with jax.named_scope("spectrum"):
        outgoing = pl.pallas_call(
            functools.partial(spectrum_kernel, chunk),
            out_shape=[jax.ShapeDtypeStruct((group_rows, traces), jnp.bfloat16)] * devices,
            in_specs=[smem_spec(), hbm_spec(), hbm_spec()],
            out_specs=[vmem_spec()] * devices,
            scratch_shapes=[
                pltpu.VMEM((traces, length), jnp.float32),
                pltpu.VMEM((2 * rows, length), jnp.bfloat16),
                pltpu.VMEM((devices, group_rows, traces), jnp.float32),
                pltpu.SemaphoreType.DMA((2, length // chunk)),
            ],
            compiler_params=params,
            name="spectrum",
        )(place, in_hbm(gathers), in_hbm(jnp.asarray(forward_table)))
    incoming = [outgoing[0]]
    for r in range(1, devices):
        pairs = [(i, i ^ r) for i in range(devices)]
        incoming.append(lax.ppermute(outgoing[r], "freq", pairs))
    with jax.named_scope("prepare"):
        coefficients, held = pl.pallas_call(
            functools.partial(prepare_kernel, kept_bins, slots),
            out_shape=[
                jax.ShapeDtypeStruct((2 * offsets, rows, traces), jnp.float32),
                pltpu.VMEM(operator.shape, operator.dtype),
            ],
            in_specs=[smem_spec(), pl.BlockSpec(memory_space=pl.ANY), vmem_spec(), vmem_spec(), hbm_spec()],
            out_specs=[vmem_spec(), vmem_spec()],
            scratch_shapes=[pltpu.SemaphoreType.DMA],
            compiler_params=params,
            name="prepare",
        )(
            slice_len,
            outgoing[0],
            filters,
            jnp.asarray(lag_tables(band_bins, lags, length)),
            in_hbm(operator),
        )
    with jax.named_scope("predict"):
        sending = pl.pallas_call(
            functools.partial(predict_kernel, devices),
            out_shape=jax.ShapeDtypeStruct((devices, group_rows, traces), jnp.bfloat16),
            in_specs=[smem_spec(), smem_spec()] + [vmem_spec()] * (devices + 1),
            out_specs=vmem_spec(),
            scratch_shapes=[pltpu.VMEM((devices, group_rows, traces), jnp.float32)],
            compiler_params=params,
            name="predict",
        )(place, tile_of, *incoming, held)
    returned = lax.all_gather(sending, "freq", axis=0, tiled=False)
    with jax.named_scope("subtract"):
        return pl.pallas_call(
            functools.partial(subtract_kernel, receivers // traces),
            out_shape=jax.ShapeDtypeStruct((traces, length), jnp.float32),
            in_specs=[smem_spec()] + [vmem_spec()] * 4,
            out_specs=vmem_spec(),
            compiler_params=params,
            name="subtract",
        )(
            lax.dynamic_slice(tile_of, (me,), (1,)),
            returned,
            coefficients,
            jnp.asarray(back_table),
            gathers,
        )


def solution(mesh):
    placed = (
        P(("survey", "freq"), None),
        P(("survey", "freq"), None, None, None),
        P(("survey", "freq"), None, None, None),
        P("survey"),
        P("survey"),
    )
    return jax.shard_map(
        local, mesh=mesh, in_specs=placed, out_specs=P(("survey", "freq"), None), check_vma=False
    )
```

```python
import functools
import math

import jax
import jax.numpy as jnp
import ml_dtypes
import numpy as np
from jax import lax
from jax.experimental import pallas as pl
from jax.experimental.pallas import tpu as pltpu
from jax.sharding import PartitionSpec as P

FIRST = 40
REACH = 4
VMEM_LIMIT = 40 * 1024 * 1024


def split_halves(values):
    values = values.astype(np.float32)
    high = values.astype(ml_dtypes.bfloat16)
    low = (values - high.astype(np.float32)).astype(ml_dtypes.bfloat16)
    return high, low


def row_tables(band_bins, length):
    bin_ids = FIRST + np.arange(band_bins)
    angles = 2.0 * np.pi / length * (bin_ids[:, None] * np.arange(length)[None, :] % length)
    return np.stack([np.cos(angles), -np.sin(angles)], axis=1).reshape(2 * band_bins, length)


def lag_tables(band_bins, lags, length):
    bin_ids = FIRST + np.arange(band_bins)
    lag_ids = np.arange(lags) - lags // 2
    angles = 2.0 * np.pi / length * (bin_ids[:, None] * lag_ids[None, :] % length)
    cosine, sine = np.cos(angles), np.sin(angles)
    weight = (bin_ids / (FIRST + band_bins))[:, None]
    real = np.stack([cosine, sine, -weight * sine, weight * cosine])
    imag = np.stack([sine, -cosine, weight * cosine, weight * sine])
    own = np.stack([real, real], axis=2).reshape(4, 2 * band_bins, lags)
    partner = np.stack([-imag, imag], axis=2).reshape(4, 2 * band_bins, lags)
    return np.concatenate([own, partner], axis=1).astype(np.float32)


def split_array(values):
    high = values.astype(jnp.bfloat16)
    low = (values - high.astype(jnp.float32)).astype(jnp.bfloat16)
    return high, low


def swap_pairs(values):
    rows = values.shape[0]
    parity = lax.broadcasted_iota(jnp.int32, values.shape, 0) % 2
    return jnp.where(
        parity == 0, pltpu.roll(values, rows - 1, 0), pltpu.roll(values, 1, 0)
    )


def spectrum_kernel(chunk, gathers_ref, table_ref, out_ref, held, table, sems):
    length = gathers_ref.shape[1]
    rows = table_ref.shape[0] // 2
    copies = []
    for step in range(length // chunk):
        part = pl.ds(step * chunk, chunk)
        copies.append(
            (
                pltpu.make_async_copy(gathers_ref.at[:, part], held.at[:, part], sems.at[0, step]),
                pltpu.make_async_copy(table_ref.at[:, part], table.at[:, part], sems.at[1, step]),
            )
        )
    for pair in copies:
        for copy in pair:
            copy.start()
    dot = functools.partial(
        lax.dot_general,
        dimension_numbers=(((1,), (1,)), ((), ())),
        preferred_element_type=jnp.float32,
    )
    total = jnp.zeros((rows, held.shape[0]), jnp.float32)
    for step, pair in enumerate(copies):
        for copy in pair:
            copy.wait()
        part = pl.ds(step * chunk, chunk)
        high, low = split_array(held[:, part])
        weights = table[:, part]
        both = dot(weights, high)
        total = total + both[:rows] + (both[rows:] + dot(weights[:rows], low))
    out_ref[...] = total.astype(jnp.bfloat16).reshape(out_ref.shape)


def prepare_kernel(
    kept_bins,
    slots,
    after_ref,
    slice_ref,
    filters_ref,
    table_ref,
    operator_ref,
    out_ref,
    held_ref,
    counts,
    filters,
    table,
    sems,
):
    pairs = ((slice_ref, counts), (filters_ref, filters), (table_ref, table), (operator_ref, held_ref))
    copies = [
        pltpu.make_async_copy(source, target, sems.at[i])
        for i, (source, target) in enumerate(pairs)
    ]
    for copy in copies:
        copy.start()
    rows = out_ref.shape[1]
    offsets, components, _ = filters.shape
    width = out_ref.shape[2]
    for copy in copies[:-1]:
        copy.wait()
    total = jnp.zeros((2 * rows, offsets), jnp.float32)
    for part in range(components):
        total = total + lax.dot_general(
            table[part],
            filters[:, part],
            (((1,), (1,)), ((), ())),
            precision=lax.Precision.HIGHEST,
            preferred_element_type=jnp.float32,
        )
    row_ids = lax.broadcasted_iota(jnp.int32, (rows, width), 0)
    group = row_ids // (2 * slots)
    slot = row_ids // 2 % slots
    count = jnp.zeros((rows, width), jnp.int32)
    for device in range(rows // (2 * slots)):
        count = jnp.where(group == device, counts[device], count)
    scale = jnp.where(slot < count, math.sqrt(2.0 / kept_bins), 0.0)
    for offset in range(offsets):
        out_ref[offset] = total[:rows, offset : offset + 1] * scale
        out_ref[offsets + offset] = total[rows:, offset : offset + 1] * scale
    copies[-1].wait()


def predict_kernel(self_ref, tile_ref, incoming_ref, operator_ref, keep_ref, send_ref, spectra, tiles):
    devices, group_rows, traces = incoming_ref.shape
    slots, _, receivers, _ = operator_ref.shape
    per_shot = receivers // traces
    shots = devices // per_shot
    me = self_ref[0]
    for k in range(devices):
        spectra[tile_ref[k]] = incoming_ref[k].astype(jnp.float32)
    columns = []
    for q in range(per_shot):
        parts = [spectra[s * per_shot + q] for s in range(shots)]
        columns.append(jnp.concatenate(parts, axis=0))
    spectrum = jnp.concatenate(columns, axis=1).astype(jnp.bfloat16)
    rows = shots * group_rows
    row_ids = lax.broadcasted_iota(jnp.int32, (rows, receivers), 0)
    dot = functools.partial(
        lax.dot_general,
        dimension_numbers=(((1,), (1,)), ((), ())),
        preferred_element_type=jnp.float32,
    )
    predicted = jnp.zeros((rows, receivers), jnp.float32)
    for slot in range(slots):
        by_real = dot(spectrum, operator_ref[slot, 0])
        by_imag = swap_pairs(dot(spectrum, operator_ref[slot, 1]))
        product = jnp.where(row_ids % 2 == 0, by_real - by_imag, by_real + by_imag)
        predicted = jnp.where(row_ids // 2 % slots == slot, product, predicted)
    for s in range(shots):
        for q in range(per_shot):
            tiles[s * per_shot + q] = predicted[
                s * group_rows : (s + 1) * group_rows, q * traces : (q + 1) * traces
            ]
    lane_ids = lax.broadcasted_iota(jnp.int32, (group_rows, traces), 1)
    half = devices // 2
    for q in range(devices):
        tile = tile_ref[me ^ q]
        place = tile % per_shot
        before = tiles[jnp.maximum(tile - 1, 0)]
        after = tiles[jnp.minimum(tile + 1, devices - 1)]
        first_lanes = jnp.where(place < per_shot - 1, REACH, 0)
        last_lanes = jnp.where(place > 0, traces - REACH, traces)
        halo = jnp.where(lane_ids < first_lanes, after, 0.0)
        halo = jnp.where(lane_ids >= last_lanes, before, halo)
        both = jnp.concatenate([tiles[tile], halo], axis=1).astype(jnp.bfloat16)
        if q < half:
            keep_ref[q] = both
        else:
            send_ref[q - half] = both


def pack_kernel(places, *refs):
    for index, (piece, place) in enumerate(places):
        refs[-1][index] = refs[piece][place]


def subtract_kernel(places, self_ref, *refs):
    count = len(refs) - 5
    pieces, (coefficient_ref, table_ref, gathers_ref, out_ref, returned) = refs[:count], refs[count:]
    devices, group_rows, width = returned.shape
    rows = devices * group_rows
    traces = gathers_ref.shape[0]
    me = self_ref[0]
    for q, (piece, index) in enumerate(places):
        returned[me ^ q] = pieces[piece][index].astype(jnp.float32)
    own = returned[...].reshape(rows, width)
    partner = swap_pairs(own)
    offsets = coefficient_ref.shape[0] // 2
    total = jnp.zeros((rows, traces), jnp.float32)
    for offset in range(offsets):
        shift = (offsets // 2 - offset) % width
        moved = pltpu.roll(own, shift, 1)[:, :traces]
        moved_partner = pltpu.roll(partner, shift, 1)[:, :traces]
        total = total + coefficient_ref[offset] * moved
        total = total + coefficient_ref[offsets + offset] * moved_partner
    high, low = split_array(jnp.transpose(total))
    stacked = jnp.concatenate([high, low, high], axis=1)
    response = jnp.dot(stacked, table_ref[...], preferred_element_type=jnp.float32)
    out_ref[...] = gathers_ref[...] - response


def vmem_spec():
    return pl.BlockSpec(memory_space=pltpu.VMEM)


def smem_spec():
    return pl.BlockSpec(memory_space=pltpu.SMEM)


def hbm_spec():
    return pl.BlockSpec(memory_space=pltpu.HBM)


def in_hbm(values):
    return pltpu.with_memory_space_constraint(values, pltpu.HBM)


def exchange(keep, send, devices):
    half = devices // 2
    pieces = [keep]
    places = [(0, q) for q in range(half)] + [None] * half
    bit = half
    while bit:
        ids = [q for q in range(devices) if q & bit]
        if bit < half:
            send = pl.pallas_call(
                functools.partial(pack_kernel, [places[q] for q in ids]),
                out_shape=jax.ShapeDtypeStruct(send.shape, send.dtype),
                in_specs=[vmem_spec()] * len(pieces),
                out_specs=vmem_spec(),
                name="pack",
            )(*pieces)
        pairs = [(i, i ^ bit) for i in range(devices)]
        pieces.append(lax.ppermute(send, "freq", pairs))
        for index, q in enumerate(ids):
            places[q] = (len(pieces) - 1, index)
        bit //= 2
    return pieces, places


def local(gathers, operator, filters, tile_of, slice_len):
    devices = lax.axis_size("freq")
    traces, length = gathers.shape
    slots, _, receivers, _ = operator.shape
    band_bins = slots * devices
    rows = 2 * band_bins
    group_rows = 2 * slots
    kept_bins = 5 * devices // 4
    offsets, lags = filters.shape[2], filters.shape[3]
    chunk = length // 4
    params = pltpu.CompilerParams(vmem_limit_bytes=VMEM_LIMIT)
    table = row_tables(band_bins, length)
    forward_table = np.concatenate(split_halves(table / math.sqrt(length)), axis=0)
    back_high, back_low = split_halves(table)
    back_table = np.concatenate([back_high, back_high, back_low], axis=0)
    me = lax.axis_index("freq").astype(jnp.int32).reshape(1)
    half = devices // 2

    with jax.named_scope("spectrum"):
        outgoing = pl.pallas_call(
            functools.partial(spectrum_kernel, chunk),
            out_shape=jax.ShapeDtypeStruct((devices, group_rows, traces), jnp.bfloat16),
            in_specs=[hbm_spec()] * 2,
            out_specs=vmem_spec(),
            scratch_shapes=[
                pltpu.VMEM((traces, length), jnp.float32),
                pltpu.VMEM((2 * rows, length), jnp.bfloat16),
                pltpu.SemaphoreType.DMA((2, length // chunk)),
            ],
            compiler_params=params,
            name="spectrum",
        )(in_hbm(gathers), in_hbm(jnp.asarray(forward_table)))
    incoming = lax.all_to_all(outgoing, "freq", split_axis=0, concat_axis=0, tiled=True)
    with jax.named_scope("prepare"):
        tables = lag_tables(band_bins, lags, length)
        coefficients, held = pl.pallas_call(
            functools.partial(prepare_kernel, kept_bins, slots),
            out_shape=[
                jax.ShapeDtypeStruct((2 * offsets, rows, traces), jnp.float32),
                pltpu.VMEM(operator.shape, operator.dtype),
            ],
            in_specs=[pl.BlockSpec(memory_space=pl.ANY)] + [hbm_spec()] * 4,
            out_specs=[vmem_spec(), vmem_spec()],
            scratch_shapes=[
                pltpu.SMEM(slice_len.shape, jnp.int32),
                pltpu.VMEM((offsets, filters.shape[1], lags), jnp.float32),
                pltpu.VMEM(tables.shape, jnp.float32),
                pltpu.SemaphoreType.DMA((4,)),
            ],
            compiler_params=params,
            name="prepare",
        )(
            outgoing,
            in_hbm(slice_len),
            in_hbm(jnp.transpose(filters[0], (1, 0, 2))),
            in_hbm(jnp.asarray(tables)),
            in_hbm(operator),
        )
    with jax.named_scope("predict"):
        block = jax.ShapeDtypeStruct((half, group_rows, 2 * traces), jnp.bfloat16)
        keep, send = pl.pallas_call(
            predict_kernel,
            out_shape=[block, block],
            in_specs=[smem_spec(), smem_spec(), vmem_spec(), vmem_spec()],
            out_specs=[vmem_spec(), vmem_spec()],
            scratch_shapes=[pltpu.VMEM((devices, group_rows, traces), jnp.float32)] * 2,
            compiler_params=params,
            name="predict",
        )(me, tile_of, incoming, held)
    with jax.named_scope("exchange"):
        pieces, places = exchange(keep, send, devices)
    with jax.named_scope("subtract"):
        return pl.pallas_call(
            functools.partial(subtract_kernel, places),
            out_shape=jax.ShapeDtypeStruct((traces, length), jnp.float32),
            in_specs=[smem_spec()] + [vmem_spec()] * (len(pieces) + 3),
            out_specs=vmem_spec(),
            scratch_shapes=[pltpu.VMEM((devices, group_rows, 2 * traces), jnp.float32)],
            compiler_params=params,
            name="subtract",
        )(me, *pieces, coefficients, jnp.asarray(back_table), gathers)


def solution(mesh):
    placed = (
        P(("survey", "freq"), None),
        P(("survey", "freq"), None, None, None),
        P(("survey", "freq"), None, None, None),
        P("survey"),
        P("survey"),
    )
    return jax.shard_map(
        local, mesh=mesh, in_specs=placed, out_specs=P(("survey", "freq"), None), check_vma=False
    )
```

```python
import functools
import math

import jax
import jax.numpy as jnp
import ml_dtypes
import numpy as np
from jax import lax
from jax.experimental import pallas as pl
from jax.experimental.pallas import tpu as pltpu
from jax.sharding import PartitionSpec as P

FIRST = 40
REACH = 4
VMEM_LIMIT = 40 * 1024 * 1024


def split_halves(values):
    values = values.astype(np.float32)
    high = values.astype(ml_dtypes.bfloat16)
    low = (values - high.astype(np.float32)).astype(ml_dtypes.bfloat16)
    return high, low


def row_tables(band_bins, length):
    bin_ids = FIRST + np.arange(band_bins)
    angles = 2.0 * np.pi / length * (bin_ids[:, None] * np.arange(length)[None, :] % length)
    return np.stack([np.cos(angles), -np.sin(angles)], axis=1).reshape(2 * band_bins, length)


def lag_tables(band_bins, lags, length):
    bin_ids = FIRST + np.arange(band_bins)
    lag_ids = np.arange(lags) - lags // 2
    angles = 2.0 * np.pi / length * (bin_ids[:, None] * lag_ids[None, :] % length)
    cosine, sine = np.cos(angles), np.sin(angles)
    weight = (bin_ids / (FIRST + band_bins))[:, None]
    real = np.stack([cosine, sine, -weight * sine, weight * cosine])
    imag = np.stack([sine, -cosine, weight * cosine, weight * sine])
    own = np.stack([real, real], axis=2).reshape(4, 2 * band_bins, lags)
    partner = np.stack([-imag, imag], axis=2).reshape(4, 2 * band_bins, lags)
    return np.concatenate([own, partner], axis=1).astype(np.float32)


def split_array(values):
    high = values.astype(jnp.bfloat16)
    low = (values - high.astype(jnp.float32)).astype(jnp.bfloat16)
    return high, low


def swap_pairs(values):
    rows = values.shape[0]
    parity = lax.broadcasted_iota(jnp.int32, values.shape, 0) % 2
    return jnp.where(
        parity == 0, pltpu.roll(values, rows - 1, 0), pltpu.roll(values, 1, 0)
    )


def spectrum_kernel(chunk, gathers_ref, table_ref, out_ref, held, table, sems):
    length = gathers_ref.shape[1]
    rows = table_ref.shape[0] // 2
    copies = []
    for step in range(length // chunk):
        part = pl.ds(step * chunk, chunk)
        copies.append(
            (
                pltpu.make_async_copy(gathers_ref.at[:, part], held.at[:, part], sems.at[0, step]),
                pltpu.make_async_copy(table_ref.at[:, part], table.at[:, part], sems.at[1, step]),
            )
        )
    for pair in copies:
        for copy in pair:
            copy.start()
    dot = functools.partial(
        lax.dot_general,
        dimension_numbers=(((1,), (1,)), ((), ())),
        preferred_element_type=jnp.float32,
    )
    total = jnp.zeros((rows, held.shape[0]), jnp.float32)
    for step, pair in enumerate(copies):
        for copy in pair:
            copy.wait()
        part = pl.ds(step * chunk, chunk)
        high, low = split_array(held[:, part])
        weights = table[:, part]
        both = dot(weights, high)
        total = total + both[:rows] + (both[rows:] + dot(weights[:rows], low))
    out_ref[...] = total.astype(jnp.bfloat16).reshape(out_ref.shape)


def fill_coefficients(kept_bins, slots, counts, filters, table, out_ref):
    offsets, components, _ = filters.shape
    _, rows, width = out_ref.shape
    total = jnp.zeros((2 * rows, offsets), jnp.float32)
    for part in range(components):
        total = total + lax.dot_general(
            table[part],
            filters[:, part],
            (((1,), (1,)), ((), ())),
            precision=lax.Precision.HIGHEST,
            preferred_element_type=jnp.float32,
        )
    row_ids = lax.broadcasted_iota(jnp.int32, (rows, width), 0)
    group = row_ids // (2 * slots)
    slot = row_ids // 2 % slots
    count = jnp.zeros((rows, width), jnp.int32)
    for device in range(rows // (2 * slots)):
        count = jnp.where(group == device, counts[device], count)
    scale = jnp.where(slot < count, math.sqrt(2.0 / kept_bins), 0.0)
    for offset in range(offsets):
        out_ref[offset] = total[:rows, offset : offset + 1] * scale
        out_ref[offsets + offset] = total[rows:, offset : offset + 1] * scale


def predict_kernel(
    kept_bins,
    pieces,
    incoming_ref,
    tile_ref,
    slice_ref,
    filters_ref,
    lag_ref,
    operator_ref,
    out_ref,
    coefficient_ref,
    tile_of,
    counts,
    filters,
    lags,
    operator,
    spectra,
    tiles,
    small_sems,
    sems,
):
    devices, group_rows, traces = incoming_ref.shape
    slots, _, receivers, _ = operator_ref.shape
    per_shot = receivers // traces
    shots = devices // per_shot
    rows = shots * group_rows
    span = receivers // pieces
    pairs = ((tile_ref, tile_of), (slice_ref, counts), (filters_ref, filters), (lag_ref, lags))
    small = [
        pltpu.make_async_copy(source, target, small_sems.at[i])
        for i, (source, target) in enumerate(pairs)
    ]
    for copy in small:
        copy.start()
    copies = {}
    for slot in range(slots):
        for piece in range(pieces):
            for part in range(2):
                where = (slot, part, pl.ds(piece * span, span))
                copies[slot, piece, part] = pltpu.make_async_copy(
                    operator_ref.at[where], operator.at[where], sems.at[slot, piece, part]
                )
                copies[slot, piece, part].start()
    for copy in small:
        copy.wait()
    for k in range(devices):
        spectra[tile_of[k]] = incoming_ref[k].astype(jnp.float32)
    columns = []
    for q in range(per_shot):
        parts = [spectra[s * per_shot + q] for s in range(shots)]
        columns.append(jnp.concatenate(parts, axis=0))
    spectrum = jnp.concatenate(columns, axis=1).astype(jnp.bfloat16)
    fill_coefficients(kept_bins, slots, counts, filters, lags, coefficient_ref)
    row_ids = lax.broadcasted_iota(jnp.int32, (rows, span), 0)
    dot = functools.partial(
        lax.dot_general,
        dimension_numbers=(((1,), (1,)), ((), ())),
        preferred_element_type=jnp.float32,
    )
    kept = {}
    for slot in range(slots):
        for piece in range(pieces):
            where = pl.ds(piece * span, span)
            copies[slot, piece, 0].wait()
            by_real = dot(spectrum, operator[slot, 0, where])
            copies[slot, piece, 1].wait()
            by_imag = swap_pairs(dot(spectrum, operator[slot, 1, where]))
            product = jnp.where(row_ids % 2 == 0, by_real - by_imag, by_real + by_imag)
            if slot:
                product = jnp.where(row_ids // 2 % slots == slot, product, kept[piece])
            kept[piece] = product
            if slot == slots - 1:
                for s in range(shots):
                    for q in range(span // traces):
                        tiles[s * per_shot + piece * span // traces + q] = product[
                            s * group_rows : (s + 1) * group_rows, q * traces : (q + 1) * traces
                        ]
    lane_ids = lax.broadcasted_iota(jnp.int32, (group_rows, traces), 1)
    for k in range(devices):
        tile = tile_of[k]
        place = tile % per_shot
        before = tiles[jnp.maximum(tile - 1, 0)]
        after = tiles[jnp.minimum(tile + 1, devices - 1)]
        first_lanes = jnp.where(place < per_shot - 1, REACH, 0)
        last_lanes = jnp.where(place > 0, traces - REACH, traces)
        halo = jnp.where(lane_ids < first_lanes, after, 0.0)
        halo = jnp.where(lane_ids >= last_lanes, before, halo)
        out_ref[k] = jnp.concatenate([tiles[tile], halo], axis=1).astype(jnp.bfloat16)


def subtract_kernel(chunk, returned_ref, coefficient_ref, table_ref, gathers_ref, out_ref, result, sems):
    devices, group_rows, width = returned_ref.shape
    rows = devices * group_rows
    traces, length = gathers_ref.shape
    own = returned_ref[...].astype(jnp.float32).reshape(rows, width)
    partner = swap_pairs(own)
    offsets = coefficient_ref.shape[0] // 2
    total = jnp.zeros((rows, traces), jnp.float32)
    for offset in range(offsets):
        shift = (offsets // 2 - offset) % width
        moved = pltpu.roll(own, shift, 1)[:, :traces]
        moved_partner = pltpu.roll(partner, shift, 1)[:, :traces]
        total = total + coefficient_ref[offset] * moved
        total = total + coefficient_ref[offsets + offset] * moved_partner
    high, low = split_array(jnp.transpose(total))
    stacked = jnp.concatenate([high, low, high], axis=1)
    copies = []
    for step in range(length // chunk):
        part = pl.ds(step * chunk, chunk)
        response = jnp.dot(stacked, table_ref[:, part], preferred_element_type=jnp.float32)
        result[:, part] = gathers_ref[:, part] - response
        copy = pltpu.make_async_copy(result.at[:, part], out_ref.at[:, part], sems.at[step])
        copy.start()
        copies.append(copy)
    for copy in copies:
        copy.wait()


def vmem_spec():
    return pl.BlockSpec(memory_space=pltpu.VMEM)


def hbm_spec():
    return pl.BlockSpec(memory_space=pltpu.HBM)


def in_hbm(values):
    return pltpu.with_memory_space_constraint(values, pltpu.HBM)


def local(gathers, operator, filters, tile_of, slice_len):
    devices = lax.axis_size("freq")
    traces, length = gathers.shape
    slots, _, receivers, _ = operator.shape
    band_bins = slots * devices
    rows = 2 * band_bins
    group_rows = 2 * slots
    kept_bins = 5 * devices // 4
    offsets, lags = filters.shape[2], filters.shape[3]
    chunk = length // 4
    params = pltpu.CompilerParams(vmem_limit_bytes=VMEM_LIMIT)
    table = row_tables(band_bins, length)
    forward_table = np.concatenate(split_halves(table / math.sqrt(length)), axis=0)
    back_high, back_low = split_halves(table)
    back_table = np.concatenate([back_high, back_high, back_low], axis=0)
    with jax.named_scope("spectrum"):
        outgoing = pl.pallas_call(
            functools.partial(spectrum_kernel, chunk),
            out_shape=jax.ShapeDtypeStruct((devices, group_rows, traces), jnp.bfloat16),
            in_specs=[hbm_spec()] * 2,
            out_specs=vmem_spec(),
            scratch_shapes=[
                pltpu.VMEM((traces, length), jnp.float32),
                pltpu.VMEM((2 * rows, length), jnp.bfloat16),
                pltpu.SemaphoreType.DMA((2, length // chunk)),
            ],
            compiler_params=params,
            name="spectrum",
        )(in_hbm(gathers), in_hbm(jnp.asarray(forward_table)))
    incoming = lax.all_to_all(outgoing, "freq", split_axis=0, concat_axis=0, tiled=True)
    with jax.named_scope("predict"):
        tables = lag_tables(band_bins, lags, length)
        pieces = 2
        sending, coefficients = pl.pallas_call(
            functools.partial(predict_kernel, kept_bins, pieces),
            out_shape=[
                jax.ShapeDtypeStruct((devices, group_rows, 2 * traces), jnp.bfloat16),
                jax.ShapeDtypeStruct((2 * offsets, rows, traces), jnp.float32),
            ],
            in_specs=[vmem_spec()] + [hbm_spec()] * 5,
            out_specs=[vmem_spec(), vmem_spec()],
            scratch_shapes=[
                pltpu.SMEM(tile_of.shape, jnp.int32),
                pltpu.SMEM(slice_len.shape, jnp.int32),
                pltpu.VMEM((offsets, filters.shape[1], lags), jnp.float32),
                pltpu.VMEM(tables.shape, jnp.float32),
                pltpu.VMEM(operator.shape, operator.dtype),
                pltpu.VMEM((devices, group_rows, traces), jnp.float32),
                pltpu.VMEM((devices, group_rows, traces), jnp.float32),
                pltpu.SemaphoreType.DMA((4,)),
                pltpu.SemaphoreType.DMA((slots, pieces, 2)),
            ],
            compiler_params=params,
            name="predict",
        )(
            incoming,
            in_hbm(tile_of),
            in_hbm(slice_len),
            in_hbm(jnp.transpose(filters[0], (1, 0, 2))),
            in_hbm(jnp.asarray(tables)),
            in_hbm(operator),
        )
    returned = lax.all_to_all(sending, "freq", split_axis=0, concat_axis=0, tiled=True)
    with jax.named_scope("subtract"):
        return pl.pallas_call(
            functools.partial(subtract_kernel, chunk),
            out_shape=jax.ShapeDtypeStruct((traces, length), jnp.float32),
            in_specs=[vmem_spec()] * 4,
            out_specs=hbm_spec(),
            scratch_shapes=[
                pltpu.VMEM((traces, length), jnp.float32),
                pltpu.SemaphoreType.DMA((length // chunk,)),
            ],
            compiler_params=params,
            name="subtract",
        )(returned, coefficients, jnp.asarray(back_table), gathers)


def solution(mesh):
    placed = (
        P(("survey", "freq"), None),
        P(("survey", "freq"), None, None, None),
        P(("survey", "freq"), None, None, None),
        P("survey"),
        P("survey"),
    )
    return jax.shard_map(
        local, mesh=mesh, in_specs=placed, out_specs=P(("survey", "freq"), None), check_vma=False
    )
```

```python
import functools
import math

import jax
import jax.numpy as jnp
import ml_dtypes
import numpy as np
from jax import lax
from jax.experimental import pallas as pl
from jax.experimental.pallas import tpu as pltpu
from jax.sharding import PartitionSpec as P

FIRST = 40
REACH = 4
IN_FLIGHT = 2
VMEM_LIMIT = 40 * 1024 * 1024


def split_halves(values):
    values = values.astype(np.float32)
    high = values.astype(ml_dtypes.bfloat16)
    low = (values - high.astype(np.float32)).astype(ml_dtypes.bfloat16)
    return high, low


def row_tables(band_bins, length):
    bin_ids = FIRST + np.arange(band_bins)
    angles = 2.0 * np.pi / length * (bin_ids[:, None] * np.arange(length)[None, :] % length)
    return np.stack([np.cos(angles), -np.sin(angles)], axis=1).reshape(2 * band_bins, length)


def lag_tables(band_bins, lags, length):
    bin_ids = FIRST + np.arange(band_bins)
    lag_ids = np.arange(lags) - lags // 2
    angles = 2.0 * np.pi / length * (bin_ids[:, None] * lag_ids[None, :] % length)
    cosine, sine = np.cos(angles), np.sin(angles)
    weight = (bin_ids / (FIRST + band_bins))[:, None]
    real = np.stack([cosine, sine, -weight * sine, weight * cosine])
    imag = np.stack([sine, -cosine, weight * cosine, weight * sine])
    own = np.stack([real, real], axis=2).reshape(4, 2 * band_bins, lags)
    partner = np.stack([-imag, imag], axis=2).reshape(4, 2 * band_bins, lags)
    return np.concatenate([own, partner], axis=1).astype(np.float32)


def split_array(values):
    high = values.astype(jnp.bfloat16)
    low = (values - high.astype(jnp.float32)).astype(jnp.bfloat16)
    return high, low


def swap_pairs(values):
    rows = values.shape[0]
    parity = lax.broadcasted_iota(jnp.int32, values.shape, 0) % 2
    return jnp.where(
        parity == 0, pltpu.roll(values, rows - 1, 0), pltpu.roll(values, 1, 0)
    )


def spectrum_kernel(chunk, gathers_ref, table_ref, out_ref, held, table, sems):
    length = gathers_ref.shape[1]
    rows = table_ref.shape[0] // 2
    copies = []
    for step in range(length // chunk):
        part = pl.ds(step * chunk, chunk)
        copies.append(
            (
                pltpu.make_async_copy(gathers_ref.at[:, part], held.at[:, part], sems.at[0, step]),
                pltpu.make_async_copy(table_ref.at[:, part], table.at[:, part], sems.at[1, step]),
            )
        )
    for pair in copies[:IN_FLIGHT]:
        for copy in pair:
            copy.start()
    dot = functools.partial(
        lax.dot_general,
        dimension_numbers=(((1,), (1,)), ((), ())),
        preferred_element_type=jnp.float32,
    )
    total = jnp.zeros((rows, held.shape[0]), jnp.float32)
    for step, pair in enumerate(copies):
        for copy in pair:
            copy.wait()
        for copy in copies[step + IN_FLIGHT] if step + IN_FLIGHT < len(copies) else ():
            copy.start()
        part = pl.ds(step * chunk, chunk)
        high, low = split_array(held[:, part])
        weights = table[:, part]
        both = dot(weights, high)
        total = total + both[:rows] + (both[rows:] + dot(weights[:rows], low))
    out_ref[...] = total.astype(jnp.bfloat16).reshape(out_ref.shape)


def fill_coefficients(kept_bins, slots, counts, filters, table, out_ref):
    offsets, components, _ = filters.shape
    _, rows, width = out_ref.shape
    total = jnp.zeros((2 * rows, offsets), jnp.float32)
    for part in range(components):
        total = total + lax.dot_general(
            table[part],
            filters[:, part],
            (((1,), (1,)), ((), ())),
            precision=lax.Precision.HIGHEST,
            preferred_element_type=jnp.float32,
        )
    row_ids = lax.broadcasted_iota(jnp.int32, (rows, width), 0)
    group = row_ids // (2 * slots)
    slot = row_ids // 2 % slots
    count = jnp.zeros((rows, width), jnp.int32)
    for device in range(rows // (2 * slots)):
        count = jnp.where(group == device, counts[device], count)
    scale = jnp.where(slot < count, math.sqrt(2.0 / kept_bins), 0.0)
    for offset in range(offsets):
        out_ref[offset] = total[:rows, offset : offset + 1] * scale
        out_ref[offsets + offset] = total[rows:, offset : offset + 1] * scale


def predict_kernel(
    kept_bins,
    pieces,
    incoming_ref,
    tile_ref,
    slice_ref,
    filters_ref,
    lag_ref,
    operator_ref,
    out_ref,
    coefficient_ref,
    tile_of,
    counts,
    filters,
    lags,
    operator,
    spectra,
    tiles,
    small_sems,
    sems,
):
    devices, group_rows, traces = incoming_ref.shape
    slots, _, receivers, _ = operator_ref.shape
    per_shot = receivers // traces
    shots = devices // per_shot
    rows = shots * group_rows
    span = receivers // pieces
    pairs = ((tile_ref, tile_of), (slice_ref, counts), (filters_ref, filters), (lag_ref, lags))
    small = [
        pltpu.make_async_copy(source, target, small_sems.at[i])
        for i, (source, target) in enumerate(pairs)
    ]
    for copy in small:
        copy.start()
    order = [
        (slot, part, pl.ds(piece * span, span))
        for slot in range(slots)
        for piece in range(pieces)
        for part in range(2)
    ]
    copies = [
        pltpu.make_async_copy(operator_ref.at[where], operator.at[where], sems.at[i])
        for i, where in enumerate(order)
    ]
    for copy in copies[:IN_FLIGHT]:
        copy.start()

    def arrived(index):
        copies[index].wait()
        if index + IN_FLIGHT < len(copies):
            copies[index + IN_FLIGHT].start()
        return operator[order[index]]

    for copy in small:
        copy.wait()
    for k in range(devices):
        spectra[tile_of[k]] = incoming_ref[k].astype(jnp.float32)
    columns = []
    for q in range(per_shot):
        parts = [spectra[s * per_shot + q] for s in range(shots)]
        columns.append(jnp.concatenate(parts, axis=0))
    spectrum = jnp.concatenate(columns, axis=1).astype(jnp.bfloat16)
    fill_coefficients(kept_bins, slots, counts, filters, lags, coefficient_ref)
    row_ids = lax.broadcasted_iota(jnp.int32, (rows, span), 0)
    dot = functools.partial(
        lax.dot_general,
        dimension_numbers=(((1,), (1,)), ((), ())),
        preferred_element_type=jnp.float32,
    )
    kept = {}
    for slot in range(slots):
        for piece in range(pieces):
            index = 2 * (slot * pieces + piece)
            by_real = dot(spectrum, arrived(index))
            by_imag = swap_pairs(dot(spectrum, arrived(index + 1)))
            product = jnp.where(row_ids % 2 == 0, by_real - by_imag, by_real + by_imag)
            if slot:
                product = jnp.where(row_ids // 2 % slots == slot, product, kept[piece])
            kept[piece] = product
            if slot == slots - 1:
                for s in range(shots):
                    for q in range(span // traces):
                        tiles[s * per_shot + piece * span // traces + q] = product[
                            s * group_rows : (s + 1) * group_rows, q * traces : (q + 1) * traces
                        ]
    lane_ids = lax.broadcasted_iota(jnp.int32, (group_rows, traces), 1)
    for k in range(devices):
        tile = tile_of[k]
        place = tile % per_shot
        before = tiles[jnp.maximum(tile - 1, 0)]
        after = tiles[jnp.minimum(tile + 1, devices - 1)]
        first_lanes = jnp.where(place < per_shot - 1, REACH, 0)
        last_lanes = jnp.where(place > 0, traces - REACH, traces)
        halo = jnp.where(lane_ids < first_lanes, after, 0.0)
        halo = jnp.where(lane_ids >= last_lanes, before, halo)
        out_ref[k] = jnp.concatenate([tiles[tile], halo], axis=1).astype(jnp.bfloat16)


def subtract_kernel(chunk, returned_ref, coefficient_ref, table_ref, gathers_ref, out_ref, result, sems):
    devices, group_rows, width = returned_ref.shape
    rows = devices * group_rows
    traces, length = gathers_ref.shape
    own = returned_ref[...].astype(jnp.float32).reshape(rows, width)
    partner = swap_pairs(own)
    offsets = coefficient_ref.shape[0] // 2
    total = jnp.zeros((rows, traces), jnp.float32)
    for offset in range(offsets):
        shift = (offsets // 2 - offset) % width
        moved = pltpu.roll(own, shift, 1)[:, :traces]
        moved_partner = pltpu.roll(partner, shift, 1)[:, :traces]
        total = total + coefficient_ref[offset] * moved
        total = total + coefficient_ref[offsets + offset] * moved_partner
    high, low = split_array(jnp.transpose(total))
    stacked = jnp.concatenate([high, low, high], axis=1)
    copies = []
    for step in range(length // chunk):
        part = pl.ds(step * chunk, chunk)
        response = jnp.dot(stacked, table_ref[:, part], preferred_element_type=jnp.float32)
        result[:, part] = gathers_ref[:, part] - response
        copy = pltpu.make_async_copy(result.at[:, part], out_ref.at[:, part], sems.at[step])
        copy.start()
        copies.append(copy)
    for copy in copies:
        copy.wait()


def vmem_spec():
    return pl.BlockSpec(memory_space=pltpu.VMEM)


def hbm_spec():
    return pl.BlockSpec(memory_space=pltpu.HBM)


def in_hbm(values):
    return pltpu.with_memory_space_constraint(values, pltpu.HBM)


def exchange(chunks, devices):
    inner = 1 << (devices.bit_length() - 1) // 2
    outer = devices // inner
    shape = chunks.shape[1:]
    near = [[o * inner + i for i in range(inner)] for o in range(outer)]
    far = [[o * inner + i for o in range(outer)] for i in range(inner)]
    by_inner = jnp.swapaxes(chunks.reshape(outer, inner, *shape), 0, 1)
    held = lax.all_to_all(by_inner, "freq", 0, 0, axis_index_groups=near, tiled=True)
    by_outer = jnp.swapaxes(held, 0, 1)
    came = lax.all_to_all(by_outer, "freq", 0, 0, axis_index_groups=far, tiled=True)
    return came.reshape(devices, *shape)


def local(gathers, operator, filters, tile_of, slice_len):
    devices = lax.axis_size("freq")
    traces, length = gathers.shape
    slots, _, receivers, _ = operator.shape
    band_bins = slots * devices
    rows = 2 * band_bins
    group_rows = 2 * slots
    kept_bins = 5 * devices // 4
    offsets, lags = filters.shape[2], filters.shape[3]
    chunk = length // 4
    params = pltpu.CompilerParams(vmem_limit_bytes=VMEM_LIMIT)
    table = row_tables(band_bins, length)
    forward_table = np.concatenate(split_halves(table / math.sqrt(length)), axis=0)
    back_high, back_low = split_halves(table)
    back_table = np.concatenate([back_high, back_high, back_low], axis=0)
    with jax.named_scope("spectrum"):
        outgoing = pl.pallas_call(
            functools.partial(spectrum_kernel, chunk),
            out_shape=jax.ShapeDtypeStruct((devices, group_rows, traces), jnp.bfloat16),
            in_specs=[hbm_spec()] * 2,
            out_specs=vmem_spec(),
            scratch_shapes=[
                pltpu.VMEM((traces, length), jnp.float32),
                pltpu.VMEM((2 * rows, length), jnp.bfloat16),
                pltpu.SemaphoreType.DMA((2, length // chunk)),
            ],
            compiler_params=params,
            name="spectrum",
        )(in_hbm(gathers), in_hbm(jnp.asarray(forward_table)))
    incoming = exchange(outgoing, devices)
    with jax.named_scope("predict"):
        tables = lag_tables(band_bins, lags, length)
        pieces = 2
        sending, coefficients = pl.pallas_call(
            functools.partial(predict_kernel, kept_bins, pieces),
            out_shape=[
                jax.ShapeDtypeStruct((devices, group_rows, 2 * traces), jnp.bfloat16),
                jax.ShapeDtypeStruct((2 * offsets, rows, traces), jnp.float32),
            ],
            in_specs=[vmem_spec()] + [hbm_spec()] * 5,
            out_specs=[vmem_spec(), vmem_spec()],
            scratch_shapes=[
                pltpu.SMEM(tile_of.shape, jnp.int32),
                pltpu.SMEM(slice_len.shape, jnp.int32),
                pltpu.VMEM((offsets, filters.shape[1], lags), jnp.float32),
                pltpu.VMEM(tables.shape, jnp.float32),
                pltpu.VMEM(operator.shape, operator.dtype),
                pltpu.VMEM((devices, group_rows, traces), jnp.float32),
                pltpu.VMEM((devices, group_rows, traces), jnp.float32),
                pltpu.SemaphoreType.DMA((4,)),
                pltpu.SemaphoreType.DMA((slots * pieces * 2,)),
            ],
            compiler_params=params,
            name="predict",
        )(
            incoming,
            in_hbm(tile_of),
            in_hbm(slice_len),
            in_hbm(jnp.transpose(filters[0], (1, 0, 2))),
            in_hbm(jnp.asarray(tables)),
            in_hbm(operator),
        )
    returned = exchange(sending, devices)
    with jax.named_scope("subtract"):
        return pl.pallas_call(
            functools.partial(subtract_kernel, chunk),
            out_shape=jax.ShapeDtypeStruct((traces, length), jnp.float32),
            in_specs=[vmem_spec()] * 4,
            out_specs=hbm_spec(),
            scratch_shapes=[
                pltpu.VMEM((traces, length), jnp.float32),
                pltpu.SemaphoreType.DMA((length // chunk,)),
            ],
            compiler_params=params,
            name="subtract",
        )(returned, coefficients, jnp.asarray(back_table), gathers)


def solution(mesh):
    placed = (
        P(("survey", "freq"), None),
        P(("survey", "freq"), None, None, None),
        P(("survey", "freq"), None, None, None),
        P("survey"),
        P("survey"),
    )
    return jax.shard_map(
        local, mesh=mesh, in_specs=placed, out_specs=P(("survey", "freq"), None), check_vma=False
    )
```

```python
import functools
import math

import jax
import jax.numpy as jnp
import ml_dtypes
import numpy as np
from jax import lax
from jax.experimental import pallas as pl
from jax.experimental.pallas import tpu as pltpu
from jax.sharding import PartitionSpec as P

FIRST = 40
REACH = 4
COST = (10**11, 40_000_000)
VMEM_LIMIT = 32 * 1024 * 1024


def split_halves(values):
    values = values.astype(np.float32)
    high = values.astype(ml_dtypes.bfloat16)
    low = (values - high.astype(np.float32)).astype(ml_dtypes.bfloat16)
    return high, low


def row_tables(band_bins, length):
    bin_ids = FIRST + np.arange(band_bins)
    angles = 2.0 * np.pi / length * (bin_ids[:, None] * np.arange(length)[None, :] % length)
    return np.stack([np.cos(angles), -np.sin(angles)], axis=1).reshape(2 * band_bins, length)


def lag_tables(band_bins, lags, length):
    bin_ids = FIRST + np.arange(band_bins)
    lag_ids = np.arange(lags) - lags // 2
    angles = 2.0 * np.pi / length * (bin_ids[:, None] * lag_ids[None, :] % length)
    cosine, sine = np.cos(angles), np.sin(angles)
    weight = (bin_ids / (FIRST + band_bins))[:, None]
    real = np.stack([cosine, sine, -weight * sine, weight * cosine])
    imag = np.stack([sine, -cosine, weight * cosine, weight * sine])
    own = np.stack([real, real], axis=2).reshape(4, 2 * band_bins, lags)
    partner = np.stack([-imag, imag], axis=2).reshape(4, 2 * band_bins, lags)
    both = np.concatenate([own, partner], axis=1)
    return np.swapaxes(both, 0, 1).reshape(4 * band_bins, 4 * lags).astype(np.float32)


def split_array(values):
    high = values.astype(jnp.bfloat16)
    low = (values - high.astype(jnp.float32)).astype(jnp.bfloat16)
    return high, low


def swap_pairs(values):
    rows = values.shape[0]
    parity = lax.broadcasted_iota(jnp.int32, values.shape, 0) % 2
    return jnp.where(
        parity == 0, pltpu.roll(values, rows - 1, 0), pltpu.roll(values, 1, 0)
    )


def fill_coefficients(kept_bins, slots, counts, filters, table, out_ref):
    offsets, components, _ = filters.shape
    _, rows, width = out_ref.shape
    flat = jnp.concatenate([filters[:, part] for part in range(components)], axis=1)
    total = lax.dot_general(
        table[...],
        flat,
        (((1,), (1,)), ((), ())),
        precision=lax.Precision.HIGHEST,
        preferred_element_type=jnp.float32,
    )
    row_ids = lax.broadcasted_iota(jnp.int32, (rows, width), 0)
    group = row_ids // (2 * slots)
    slot = row_ids // 2 % slots
    count = jnp.zeros((rows, width), jnp.int32)
    for device in range(rows // (2 * slots)):
        count = jnp.where(group == device, counts[device], count)
    scale = jnp.where(slot < count, math.sqrt(2.0 / kept_bins), 0.0)
    for offset in range(offsets):
        out_ref[offset] = total[:rows, offset : offset + 1] * scale
        out_ref[offsets + offset] = total[rows:, offset : offset + 1] * scale


def spectrum_kernel(
    chunk,
    kept_bins,
    slots,
    slice_ref,
    filters_ref,
    lag_ref,
    gathers_ref,
    table_ref,
    out_ref,
    coefficient_ref,
    counts,
    filters,
    lags,
    held,
    table,
    small_sems,
    sems,
):
    length = gathers_ref.shape[1]
    rows = table_ref.shape[0] // 2
    pairs = ((slice_ref, counts), (filters_ref, filters), (lag_ref, lags))
    small = [
        pltpu.make_async_copy(source, target, small_sems.at[i])
        for i, (source, target) in enumerate(pairs)
    ]
    for copy in small:
        copy.start()
    copies = []
    for step in range(length // chunk):
        part = pl.ds(step * chunk, chunk)
        copies.append(
            (
                pltpu.make_async_copy(gathers_ref.at[:, part], held.at[:, part], sems.at[0, step]),
                pltpu.make_async_copy(table_ref.at[:, part], table.at[:, part], sems.at[1, step]),
            )
        )
    for pair in copies:
        for copy in pair:
            copy.start()
    for copy in small:
        copy.wait()
    fill_coefficients(kept_bins, slots, counts, filters, lags, coefficient_ref)
    dot = functools.partial(
        lax.dot_general,
        dimension_numbers=(((1,), (1,)), ((), ())),
        preferred_element_type=jnp.float32,
    )
    total = jnp.zeros((rows, held.shape[0]), jnp.float32)
    for step, pair in enumerate(copies):
        for copy in pair:
            copy.wait()
        part = pl.ds(step * chunk, chunk)
        high, low = split_array(held[:, part])
        weights = table[:, part]
        both = dot(weights, high)
        total = total + both[:rows] + (both[rows:] + dot(weights[:rows], low))
    out_ref[...] = total.astype(jnp.bfloat16).reshape(out_ref.shape)


def predict_kernel(tile_ref, incoming_ref, operator_ref, out_ref, spectra, tiles):
    devices, group_rows, traces = incoming_ref.shape
    slots, _, receivers, _ = operator_ref.shape
    per_shot = receivers // traces
    shots = devices // per_shot
    rows = shots * group_rows
    for k in range(devices):
        spectra[tile_ref[k]] = incoming_ref[k].astype(jnp.float32)
    columns = []
    for q in range(per_shot):
        parts = [spectra[s * per_shot + q] for s in range(shots)]
        columns.append(jnp.concatenate(parts, axis=0))
    spectrum = jnp.concatenate(columns, axis=1).astype(jnp.bfloat16)
    row_ids = lax.broadcasted_iota(jnp.int32, (rows, receivers), 0)
    dot = functools.partial(
        lax.dot_general,
        dimension_numbers=(((1,), (1,)), ((), ())),
        preferred_element_type=jnp.float32,
    )
    predicted = jnp.zeros((rows, receivers), jnp.float32)
    for slot in range(slots):
        by_real = dot(spectrum, operator_ref[slot, 0])
        by_imag = swap_pairs(dot(spectrum, operator_ref[slot, 1]))
        product = jnp.where(row_ids % 2 == 0, by_real - by_imag, by_real + by_imag)
        predicted = jnp.where(row_ids // 2 % slots == slot, product, predicted)
    for s in range(shots):
        for q in range(per_shot):
            tiles[s * per_shot + q] = predicted[
                s * group_rows : (s + 1) * group_rows, q * traces : (q + 1) * traces
            ]
    lane_ids = lax.broadcasted_iota(jnp.int32, (group_rows, traces), 1)
    for k in range(devices):
        tile = tile_ref[k]
        place = tile % per_shot
        before = tiles[jnp.maximum(tile - 1, 0)]
        after = tiles[jnp.minimum(tile + 1, devices - 1)]
        first_lanes = jnp.where(place < per_shot - 1, REACH, 0)
        last_lanes = jnp.where(place > 0, traces - REACH, traces)
        halo = jnp.where(lane_ids < first_lanes, after, 0.0)
        halo = jnp.where(lane_ids >= last_lanes, before, halo)
        out_ref[k] = jnp.concatenate([tiles[tile], halo], axis=1).astype(jnp.bfloat16)


def subtract_kernel(chunk, returned_ref, coefficient_ref, table_ref, gathers_ref, out_ref, result, sems):
    devices, group_rows, width = returned_ref.shape
    rows = devices * group_rows
    traces, length = gathers_ref.shape
    own = returned_ref[...].astype(jnp.float32).reshape(rows, width)
    partner = swap_pairs(own)
    offsets = coefficient_ref.shape[0] // 2
    total = jnp.zeros((rows, traces), jnp.float32)
    for offset in range(offsets):
        shift = (offsets // 2 - offset) % width
        moved = pltpu.roll(own, shift, 1)[:, :traces]
        moved_partner = pltpu.roll(partner, shift, 1)[:, :traces]
        total = total + coefficient_ref[offset] * moved
        total = total + coefficient_ref[offsets + offset] * moved_partner
    high, low = split_array(jnp.transpose(total))
    stacked = jnp.concatenate([high, low, high], axis=1)
    copies = []
    for step in range(length // chunk):
        part = pl.ds(step * chunk, chunk)
        response = jnp.dot(stacked, table_ref[:, part], preferred_element_type=jnp.float32)
        result[:, part] = gathers_ref[:, part] - response
        copy = pltpu.make_async_copy(result.at[:, part], out_ref.at[:, part], sems.at[step])
        copy.start()
        copies.append(copy)
    for copy in copies:
        copy.wait()


def vmem_spec():
    return pl.BlockSpec(memory_space=pltpu.VMEM)


def hbm_spec():
    return pl.BlockSpec(memory_space=pltpu.HBM)


def in_hbm(values):
    return pltpu.with_memory_space_constraint(values, pltpu.HBM)


def local(gathers, operator, filters, tile_of, slice_len):
    devices = lax.axis_size("freq")
    traces, length = gathers.shape
    slots, _, receivers, _ = operator.shape
    band_bins = slots * devices
    rows = 2 * band_bins
    group_rows = 2 * slots
    kept_bins = 5 * devices // 4
    offsets, lags = filters.shape[2], filters.shape[3]
    chunk = length // 4
    params = pltpu.CompilerParams(vmem_limit_bytes=VMEM_LIMIT)
    table = row_tables(band_bins, length)
    forward_table = np.concatenate(split_halves(table / math.sqrt(length)), axis=0)
    back_high, back_low = split_halves(table)
    back_table = np.concatenate([back_high, back_high, back_low], axis=0)
    tables = lag_tables(band_bins, lags, length)
    with jax.named_scope("spectrum"):
        outgoing, coefficients = pl.pallas_call(
            functools.partial(spectrum_kernel, chunk, kept_bins, slots),
            out_shape=[
                jax.ShapeDtypeStruct((devices, group_rows, traces), jnp.bfloat16),
                jax.ShapeDtypeStruct((2 * offsets, rows, traces), jnp.float32),
            ],
            in_specs=[hbm_spec()] * 5,
            out_specs=[vmem_spec()] * 2,
            scratch_shapes=[
                pltpu.SMEM(slice_len.shape, jnp.int32),
                pltpu.VMEM((offsets, filters.shape[1], lags), jnp.float32),
                pltpu.VMEM(tables.shape, jnp.float32),
                pltpu.VMEM((traces, length), jnp.float32),
                pltpu.VMEM((2 * rows, length), jnp.bfloat16),
                pltpu.SemaphoreType.DMA((3,)),
                pltpu.SemaphoreType.DMA((2, length // chunk)),
            ],
            compiler_params=params,
            cost_estimate=pl.CostEstimate(flops=COST[0], bytes_accessed=COST[1], transcendentals=0),
            name="spectrum",
        )(
            in_hbm(slice_len),
            in_hbm(jnp.transpose(filters[0], (1, 0, 2))),
            in_hbm(jnp.asarray(tables)),
            in_hbm(gathers),
            in_hbm(jnp.asarray(forward_table)),
        )
    incoming = lax.all_to_all(outgoing, "freq", split_axis=0, concat_axis=0, tiled=True)
    with jax.named_scope("predict"):
        sending = pl.pallas_call(
            predict_kernel,
            out_shape=jax.ShapeDtypeStruct((devices, group_rows, 2 * traces), jnp.bfloat16),
            in_specs=[pl.BlockSpec(memory_space=pltpu.SMEM), vmem_spec(), vmem_spec()],
            out_specs=vmem_spec(),
            scratch_shapes=[pltpu.VMEM((devices, group_rows, traces), jnp.float32)] * 2,
            compiler_params=params,
            name="predict",
        )(tile_of, incoming, operator)
    returned = lax.all_to_all(sending, "freq", split_axis=0, concat_axis=0, tiled=True)
    with jax.named_scope("subtract"):
        return pl.pallas_call(
            functools.partial(subtract_kernel, chunk),
            out_shape=jax.ShapeDtypeStruct((traces, length), jnp.float32),
            in_specs=[vmem_spec()] * 4,
            out_specs=hbm_spec(),
            scratch_shapes=[
                pltpu.VMEM((traces, length), jnp.float32),
                pltpu.SemaphoreType.DMA((length // chunk,)),
            ],
            compiler_params=params,
            name="subtract",
        )(returned, coefficients, jnp.asarray(back_table), gathers)


def solution(mesh):
    placed = (
        P(("survey", "freq"), None),
        P(("survey", "freq"), None, None, None),
        P(("survey", "freq"), None, None, None),
        P("survey"),
        P("survey"),
    )
    return jax.shard_map(
        local, mesh=mesh, in_specs=placed, out_specs=P(("survey", "freq"), None), check_vma=False
    )
```

```python
import functools
import math

import jax
import jax.numpy as jnp
import ml_dtypes
import numpy as np
from jax import lax
from jax.experimental import pallas as pl
from jax.experimental.pallas import tpu as pltpu
from jax.sharding import PartitionSpec as P

FIRST = 40
REACH = 4
COST = (10**11, 40_000_000)
VMEM_LIMIT = 32 * 1024 * 1024


def split_halves(values):
    values = values.astype(np.float32)
    high = values.astype(ml_dtypes.bfloat16)
    low = (values - high.astype(np.float32)).astype(ml_dtypes.bfloat16)
    return high, low


def row_tables(band_bins, length):
    bin_ids = FIRST + np.arange(band_bins)
    angles = 2.0 * np.pi / length * (bin_ids[:, None] * np.arange(length)[None, :] % length)
    return np.stack([np.cos(angles), -np.sin(angles)], axis=1).reshape(2 * band_bins, length)


def lag_tables(band_bins, lags, length):
    bin_ids = FIRST + np.arange(band_bins)
    lag_ids = np.arange(lags) - lags // 2
    angles = 2.0 * np.pi / length * (bin_ids[:, None] * lag_ids[None, :] % length)
    cosine, sine = np.cos(angles), np.sin(angles)
    weight = (bin_ids / (FIRST + band_bins))[:, None]
    real = np.stack([cosine, sine, -weight * sine, weight * cosine])
    imag = np.stack([sine, -cosine, weight * cosine, weight * sine])
    own = np.stack([real, real], axis=2).reshape(4, 2 * band_bins, lags)
    partner = np.stack([-imag, imag], axis=2).reshape(4, 2 * band_bins, lags)
    both = np.concatenate([own, partner], axis=1)
    return np.swapaxes(both, 1, 2).reshape(4 * lags, 4 * band_bins).astype(np.float32)


def split_array(values):
    high = values.astype(jnp.bfloat16)
    low = (values - high.astype(jnp.float32)).astype(jnp.bfloat16)
    return high, low


def swap_pairs(values):
    rows = values.shape[0]
    parity = lax.broadcasted_iota(jnp.int32, values.shape, 0) % 2
    return jnp.where(
        parity == 0, pltpu.roll(values, rows - 1, 0), pltpu.roll(values, 1, 0)
    )


def filter_lanes(kept_bins, slots, slice_ref, filters_ref, lag_ref):
    _, components, _ = filters_ref.shape
    lanes = lag_ref.shape[1]
    rows = lanes // 2
    flat = jnp.concatenate([filters_ref[:, part] for part in range(components)], axis=1)
    total = jnp.dot(
        flat, lag_ref[...], precision=lax.Precision.HIGHEST, preferred_element_type=jnp.float32
    )
    lane_ids = lax.broadcasted_iota(jnp.int32, (1, lanes), 1) % rows
    group = lane_ids // (2 * slots)
    slot = lane_ids // 2 % slots
    count = jnp.zeros((1, lanes), jnp.int32)
    for device in range(rows // (2 * slots)):
        count = jnp.where(group == device, slice_ref[device], count)
    return total * jnp.where(slot < count, math.sqrt(2.0 / kept_bins), 0.0)


def spectrum_kernel(chunk, gathers_ref, table_ref, out_ref, held, table, sems):
    length = gathers_ref.shape[1]
    rows = table_ref.shape[0] // 2
    copies = []
    for step in range(length // chunk):
        part = pl.ds(step * chunk, chunk)
        copies.append(
            (
                pltpu.make_async_copy(gathers_ref.at[:, part], held.at[:, part], sems.at[0, step]),
                pltpu.make_async_copy(table_ref.at[:, part], table.at[:, part], sems.at[1, step]),
            )
        )
    for pair in copies:
        for copy in pair:
            copy.start()
    dot = functools.partial(
        lax.dot_general,
        dimension_numbers=(((1,), (1,)), ((), ())),
        preferred_element_type=jnp.float32,
    )
    total = jnp.zeros((rows, held.shape[0]), jnp.float32)
    for step, pair in enumerate(copies):
        for copy in pair:
            copy.wait()
        part = pl.ds(step * chunk, chunk)
        high, low = split_array(held[:, part])
        weights = table[:, part]
        both = dot(weights, high)
        total = total + both[:rows] + (both[rows:] + dot(weights[:rows], low))
    out_ref[...] = total.astype(jnp.bfloat16).reshape(out_ref.shape)


def predict_kernel(
    kept_bins,
    tile_ref,
    slice_ref,
    filters_ref,
    lag_ref,
    incoming_ref,
    operator_ref,
    out_ref,
    coefficient_ref,
    holder,
):
    devices, group_rows, traces = incoming_ref.shape
    slots, _, receivers, _ = operator_ref.shape
    per_shot = receivers // traces
    shots = devices // per_shot
    rows = shots * group_rows
    for k in range(devices):
        holder[tile_ref[k]] = k
    columns = []
    for q in range(per_shot):
        parts = [
            incoming_ref[holder[s * per_shot + q]].astype(jnp.float32) for s in range(shots)
        ]
        columns.append(jnp.concatenate(parts, axis=0))
    spectrum = jnp.concatenate(columns, axis=1).astype(jnp.bfloat16)
    row_ids = lax.broadcasted_iota(jnp.int32, (rows, receivers), 0)
    dot = functools.partial(
        lax.dot_general,
        dimension_numbers=(((1,), (1,)), ((), ())),
        preferred_element_type=jnp.float32,
    )
    predicted = jnp.zeros((rows, receivers), jnp.float32)
    for slot in range(slots):
        by_real = dot(spectrum, operator_ref[slot, 0])
        by_imag = swap_pairs(dot(spectrum, operator_ref[slot, 1]))
        product = jnp.where(row_ids % 2 == 0, by_real - by_imag, by_real + by_imag)
        predicted = jnp.where(row_ids // 2 % slots == slot, product, predicted)
    lane_ids = lax.broadcasted_iota(jnp.int32, (rows, receivers), 1) % traces
    edge = jnp.zeros((rows, traces), jnp.float32)
    after = jnp.concatenate([predicted[:, traces:], edge], axis=1)
    before = jnp.concatenate([edge, predicted[:, :-traces]], axis=1)
    halo = jnp.where(lane_ids < REACH, after, jnp.where(lane_ids >= traces - REACH, before, 0.0))
    for s in range(shots):
        for q in range(per_shot):
            where = (slice(s * group_rows, (s + 1) * group_rows), slice(q * traces, (q + 1) * traces))
            both = jnp.concatenate([predicted[where], halo[where]], axis=1)
            out_ref[holder[s * per_shot + q]] = both.astype(jnp.bfloat16)
    coefficient_ref[...] = filter_lanes(kept_bins, slots, slice_ref, filters_ref, lag_ref)


def subtract_kernel(
    chunk, returned_ref, coefficient_ref, table_ref, gathers_ref, out_ref, spread, result, sems
):
    devices, group_rows, _ = returned_ref.shape
    rows = devices * group_rows
    traces, length = gathers_ref.shape
    offsets = coefficient_ref.shape[0]
    own = returned_ref[...].astype(jnp.float32).reshape(rows, 2 * traces)
    both = jnp.concatenate([own, swap_pairs(own)], axis=0)
    halo = jnp.transpose(both[:, traces:])
    spread[0:8] = halo[traces - 8 :]
    spread[8 : 8 + traces] = jnp.transpose(both[:, :traces])
    spread[8 + traces : 16 + traces] = halo[:8]
    total = jnp.zeros((traces, 2 * rows), jnp.float32)
    for offset in range(offsets):
        first = 8 + offset - offsets // 2
        total = total + spread[first : first + traces] * coefficient_ref[offset : offset + 1]
    total = total + pltpu.roll(total, rows, 1)
    high = total.astype(jnp.bfloat16).astype(jnp.float32)
    lane_ids = lax.broadcasted_iota(jnp.int32, total.shape, 1)
    mixed = jnp.where(lane_ids < rows, high, total - high)
    stacked = jnp.concatenate([mixed, high[:, :rows]], axis=1).astype(jnp.bfloat16)
    copies = []
    for step in range(length // chunk):
        part = pl.ds(step * chunk, chunk)
        response = jnp.dot(stacked, table_ref[:, part], preferred_element_type=jnp.float32)
        result[:, part] = gathers_ref[:, part] - response
        copy = pltpu.make_async_copy(result.at[:, part], out_ref.at[:, part], sems.at[step])
        copy.start()
        copies.append(copy)
    for copy in copies:
        copy.wait()


def vmem_spec():
    return pl.BlockSpec(memory_space=pltpu.VMEM)


def smem_spec():
    return pl.BlockSpec(memory_space=pltpu.SMEM)


def hbm_spec():
    return pl.BlockSpec(memory_space=pltpu.HBM)


def in_hbm(values):
    return pltpu.with_memory_space_constraint(values, pltpu.HBM)


def local(gathers, operator, filters, tile_of, slice_len):
    devices = lax.axis_size("freq")
    traces, length = gathers.shape
    slots, _, receivers, _ = operator.shape
    band_bins = slots * devices
    rows = 2 * band_bins
    group_rows = 2 * slots
    kept_bins = 5 * devices // 4
    offsets, lags = filters.shape[2], filters.shape[3]
    chunk = length // 4
    params = pltpu.CompilerParams(vmem_limit_bytes=VMEM_LIMIT)
    table = row_tables(band_bins, length)
    forward_table = np.concatenate(split_halves(table / math.sqrt(length)), axis=0)
    back_high, back_low = split_halves(table)
    back_table = np.concatenate([back_high, back_high, back_low], axis=0)
    tables = lag_tables(band_bins, lags, length)
    with jax.named_scope("spectrum"):
        outgoing = pl.pallas_call(
            functools.partial(spectrum_kernel, chunk),
            out_shape=jax.ShapeDtypeStruct((devices, group_rows, traces), jnp.bfloat16),
            in_specs=[hbm_spec()] * 2,
            out_specs=vmem_spec(),
            scratch_shapes=[
                pltpu.VMEM((traces, length), jnp.float32),
                pltpu.VMEM((2 * rows, length), jnp.bfloat16),
                pltpu.SemaphoreType.DMA((2, length // chunk)),
            ],
            compiler_params=params,
            cost_estimate=pl.CostEstimate(flops=COST[0], bytes_accessed=COST[1], transcendentals=0),
            name="spectrum",
        )(in_hbm(gathers), in_hbm(jnp.asarray(forward_table)))
    incoming = lax.all_to_all(outgoing, "freq", split_axis=0, concat_axis=0, tiled=True)
    with jax.named_scope("predict"):
        sending, coefficients = pl.pallas_call(
            functools.partial(predict_kernel, kept_bins),
            out_shape=[
                jax.ShapeDtypeStruct((devices, group_rows, 2 * traces), jnp.bfloat16),
                jax.ShapeDtypeStruct((offsets, 2 * rows), jnp.float32),
            ],
            in_specs=[smem_spec()] * 2 + [vmem_spec()] * 4,
            out_specs=[vmem_spec()] * 2,
            scratch_shapes=[pltpu.SMEM((devices,), jnp.int32)],
            compiler_params=params,
            name="predict",
        )(
            tile_of,
            slice_len,
            jnp.transpose(filters[0], (1, 0, 2)),
            jnp.asarray(tables),
            incoming,
            operator,
        )
    returned = lax.all_to_all(sending, "freq", split_axis=0, concat_axis=0, tiled=True)
    with jax.named_scope("subtract"):
        return pl.pallas_call(
            functools.partial(subtract_kernel, length // 8),
            out_shape=jax.ShapeDtypeStruct((traces, length), jnp.float32),
            in_specs=[vmem_spec()] * 4,
            out_specs=hbm_spec(),
            scratch_shapes=[
                pltpu.VMEM((traces + 16, 2 * rows), jnp.float32),
                pltpu.VMEM((traces, length), jnp.float32),
                pltpu.SemaphoreType.DMA((8,)),
            ],
            compiler_params=params,
            name="subtract",
        )(returned, coefficients, jnp.asarray(back_table), gathers)


def solution(mesh):
    placed = (
        P(("survey", "freq"), None),
        P(("survey", "freq"), None, None, None),
        P(("survey", "freq"), None, None, None),
        P("survey"),
        P("survey"),
    )
    return jax.shard_map(
        local, mesh=mesh, in_specs=placed, out_specs=P(("survey", "freq"), None), check_vma=False
    )
```

```python
import functools
import math

import jax
import jax.numpy as jnp
import ml_dtypes
import numpy as np
from jax import lax
from jax.experimental import pallas as pl
from jax.experimental.pallas import tpu as pltpu
from jax.sharding import PartitionSpec as P

FIRST = 40
REACH = 4
COST = (10**11, 40_000_000)
VMEM_LIMIT = 32 * 1024 * 1024


def split_halves(values):
    values = values.astype(np.float32)
    high = values.astype(ml_dtypes.bfloat16)
    low = (values - high.astype(np.float32)).astype(ml_dtypes.bfloat16)
    return high, low


def row_tables(band_bins, length):
    bin_ids = FIRST + np.arange(band_bins)
    angles = 2.0 * np.pi / length * (bin_ids[:, None] * np.arange(length)[None, :] % length)
    return np.stack([np.cos(angles), -np.sin(angles)], axis=1).reshape(2 * band_bins, length)


def lag_tables(band_bins, lags, length):
    bin_ids = FIRST + np.arange(band_bins)
    lag_ids = np.arange(lags) - lags // 2
    angles = 2.0 * np.pi / length * (bin_ids[:, None] * lag_ids[None, :] % length)
    cosine, sine = np.cos(angles), np.sin(angles)
    weight = (bin_ids / (FIRST + band_bins))[:, None]
    real = np.stack([cosine, sine, -weight * sine, weight * cosine])
    imag = np.stack([sine, -cosine, weight * cosine, weight * sine])
    own = np.stack([real, real], axis=2).reshape(4, 2 * band_bins, lags)
    partner = np.stack([-imag, imag], axis=2).reshape(4, 2 * band_bins, lags)
    both = np.concatenate([own, partner], axis=1)
    return np.swapaxes(both, 1, 2).reshape(4 * lags, 4 * band_bins).astype(np.float32)


def split_array(values):
    high = values.astype(jnp.bfloat16)
    low = (values - high.astype(jnp.float32)).astype(jnp.bfloat16)
    return high, low


def swap_pairs(values):
    rows = values.shape[0]
    parity = lax.broadcasted_iota(jnp.int32, values.shape, 0) % 2
    return jnp.where(
        parity == 0, pltpu.roll(values, rows - 1, 0), pltpu.roll(values, 1, 0)
    )


def filter_lanes(kept_bins, slots, slice_ref, filters_ref, lag_ref):
    _, components, _ = filters_ref.shape
    lanes = lag_ref.shape[1]
    rows = lanes // 2
    flat = jnp.concatenate([filters_ref[:, part] for part in range(components)], axis=1)
    total = jnp.dot(
        flat, lag_ref[...], precision=lax.Precision.HIGHEST, preferred_element_type=jnp.float32
    )
    lane_ids = lax.broadcasted_iota(jnp.int32, (1, lanes), 1) % rows
    group = lane_ids // (2 * slots)
    slot = lane_ids // 2 % slots
    count = jnp.zeros((1, lanes), jnp.int32)
    for device in range(rows // (2 * slots)):
        count = jnp.where(group == device, slice_ref[device], count)
    return total * jnp.where(slot < count, math.sqrt(2.0 / kept_bins), 0.0)


def spectrum_kernel(chunk, gathers_ref, table_ref, out_ref, held, table, sems):
    length = gathers_ref.shape[1]
    rows = table_ref.shape[0] // 2
    copies = []
    for step in range(length // chunk):
        part = pl.ds(step * chunk, chunk)
        copies.append(
            (
                pltpu.make_async_copy(gathers_ref.at[:, part], held.at[:, part], sems.at[0, step]),
                pltpu.make_async_copy(table_ref.at[:, part], table.at[:, part], sems.at[1, step]),
            )
        )
    for pair in copies:
        for copy in pair:
            copy.start()
    dot = functools.partial(
        lax.dot_general,
        dimension_numbers=(((1,), (1,)), ((), ())),
        preferred_element_type=jnp.float32,
    )
    total = jnp.zeros((rows, held.shape[0]), jnp.float32)
    for step, pair in enumerate(copies):
        for copy in pair:
            copy.wait()
        part = pl.ds(step * chunk, chunk)
        high, low = split_array(held[:, part])
        weights = table[:, part]
        both = dot(weights, high)
        total = total + both[:rows] + (both[rows:] + dot(weights[:rows], low))
    out_ref[...] = total.astype(jnp.bfloat16).reshape(out_ref.shape)


def predict_kernel(
    kept_bins,
    tile_ref,
    slice_ref,
    filters_ref,
    lag_ref,
    incoming_ref,
    operator_ref,
    out_ref,
    coefficient_ref,
    holder,
):
    devices, group_rows, traces = incoming_ref.shape
    slots, _, receivers, _ = operator_ref.shape
    per_shot = receivers // traces
    shots = devices // per_shot
    rows = shots * group_rows
    for k in range(devices):
        holder[tile_ref[k]] = k
    columns = []
    for q in range(per_shot):
        parts = [
            incoming_ref[holder[s * per_shot + q]].astype(jnp.float32) for s in range(shots)
        ]
        columns.append(jnp.concatenate(parts, axis=0))
    spectrum = jnp.concatenate(columns, axis=1)
    row_ids = lax.broadcasted_iota(jnp.int32, (rows, receivers), 0)
    partner = swap_pairs(spectrum)
    partner = jnp.where(row_ids % 2 == 0, -partner, partner)
    sides = [jnp.transpose(spectrum), jnp.transpose(partner)]
    column_ids = lax.broadcasted_iota(jnp.int32, (receivers, rows), 1)
    turned = jnp.zeros((receivers, rows), jnp.float32)
    for slot in range(slots):
        for part in range(2):
            side = jnp.where(column_ids // 2 % slots == slot, sides[part], 0.0).astype(jnp.bfloat16)
            turned = turned + jnp.dot(
                operator_ref[slot, part], side, preferred_element_type=jnp.float32
            )
    predicted = jnp.transpose(turned)
    lane_ids = lax.broadcasted_iota(jnp.int32, (rows, receivers), 1) % traces
    edge = jnp.zeros((rows, traces), jnp.float32)
    after = jnp.concatenate([predicted[:, traces:], edge], axis=1)
    before = jnp.concatenate([edge, predicted[:, :-traces]], axis=1)
    halo = jnp.where(lane_ids < REACH, after, jnp.where(lane_ids >= traces - REACH, before, 0.0))
    for s in range(shots):
        for q in range(per_shot):
            where = (slice(s * group_rows, (s + 1) * group_rows), slice(q * traces, (q + 1) * traces))
            both = jnp.concatenate([predicted[where], halo[where]], axis=1)
            out_ref[holder[s * per_shot + q]] = both.astype(jnp.bfloat16)
    coefficient_ref[...] = filter_lanes(kept_bins, slots, slice_ref, filters_ref, lag_ref)


def subtract_kernel(
    chunk, returned_ref, coefficient_ref, table_ref, gathers_ref, out_ref, spread, result, sems
):
    devices, group_rows, _ = returned_ref.shape
    rows = devices * group_rows
    traces, length = gathers_ref.shape
    offsets = coefficient_ref.shape[0]
    own = returned_ref[...].astype(jnp.float32).reshape(rows, 2 * traces)
    both = jnp.concatenate([own, swap_pairs(own)], axis=0)
    halo = jnp.transpose(both[:, traces:])
    spread[0:8] = halo[traces - 8 :]
    spread[8 : 8 + traces] = jnp.transpose(both[:, :traces])
    spread[8 + traces : 16 + traces] = halo[:8]
    total = jnp.zeros((traces, 2 * rows), jnp.float32)
    for offset in range(offsets):
        first = 8 + offset - offsets // 2
        total = total + spread[first : first + traces] * coefficient_ref[offset : offset + 1]
    total = total + pltpu.roll(total, rows, 1)
    high = total.astype(jnp.bfloat16).astype(jnp.float32)
    lane_ids = lax.broadcasted_iota(jnp.int32, total.shape, 1)
    mixed = jnp.where(lane_ids < rows, high, total - high)
    stacked = jnp.concatenate([mixed, high[:, :rows]], axis=1).astype(jnp.bfloat16)
    copies = []
    for step in range(length // chunk):
        part = pl.ds(step * chunk, chunk)
        response = jnp.dot(stacked, table_ref[:, part], preferred_element_type=jnp.float32)
        result[:, part] = gathers_ref[:, part] - response
        copy = pltpu.make_async_copy(result.at[:, part], out_ref.at[:, part], sems.at[step])
        copy.start()
        copies.append(copy)
    for copy in copies:
        copy.wait()


def vmem_spec():
    return pl.BlockSpec(memory_space=pltpu.VMEM)


def smem_spec():
    return pl.BlockSpec(memory_space=pltpu.SMEM)


def hbm_spec():
    return pl.BlockSpec(memory_space=pltpu.HBM)


def in_hbm(values):
    return pltpu.with_memory_space_constraint(values, pltpu.HBM)


def local(gathers, operator, filters, tile_of, slice_len):
    devices = lax.axis_size("freq")
    traces, length = gathers.shape
    slots, _, receivers, _ = operator.shape
    band_bins = slots * devices
    rows = 2 * band_bins
    group_rows = 2 * slots
    kept_bins = 5 * devices // 4
    offsets, lags = filters.shape[2], filters.shape[3]
    chunk = length // 8
    params = pltpu.CompilerParams(vmem_limit_bytes=VMEM_LIMIT)
    table = row_tables(band_bins, length)
    forward_table = np.concatenate(split_halves(table / math.sqrt(length)), axis=0)
    back_high, back_low = split_halves(table)
    back_table = np.concatenate([back_high, back_high, back_low], axis=0)
    tables = lag_tables(band_bins, lags, length)
    with jax.named_scope("spectrum"):
        outgoing = pl.pallas_call(
            functools.partial(spectrum_kernel, chunk),
            out_shape=jax.ShapeDtypeStruct((devices, group_rows, traces), jnp.bfloat16),
            in_specs=[hbm_spec()] * 2,
            out_specs=vmem_spec(),
            scratch_shapes=[
                pltpu.VMEM((traces, length), jnp.float32),
                pltpu.VMEM((2 * rows, length), jnp.bfloat16),
                pltpu.SemaphoreType.DMA((2, length // chunk)),
            ],
            compiler_params=params,
            cost_estimate=pl.CostEstimate(flops=COST[0], bytes_accessed=COST[1], transcendentals=0),
            name="spectrum",
        )(in_hbm(gathers), in_hbm(jnp.asarray(forward_table)))
    incoming = lax.all_to_all(outgoing, "freq", split_axis=0, concat_axis=0, tiled=True)
    with jax.named_scope("predict"):
        sending, coefficients = pl.pallas_call(
            functools.partial(predict_kernel, kept_bins),
            out_shape=[
                jax.ShapeDtypeStruct((devices, group_rows, 2 * traces), jnp.bfloat16),
                jax.ShapeDtypeStruct((offsets, 2 * rows), jnp.float32),
            ],
            in_specs=[smem_spec()] * 2 + [vmem_spec()] * 4,
            out_specs=[vmem_spec()] * 2,
            scratch_shapes=[pltpu.SMEM((devices,), jnp.int32)],
            compiler_params=params,
            name="predict",
        )(
            tile_of,
            slice_len,
            jnp.transpose(filters[0], (1, 0, 2)),
            jnp.asarray(tables),
            incoming,
            operator,
        )
    returned = lax.all_to_all(sending, "freq", split_axis=0, concat_axis=0, tiled=True)
    with jax.named_scope("subtract"):
        return pl.pallas_call(
            functools.partial(subtract_kernel, length // 4),
            out_shape=jax.ShapeDtypeStruct((traces, length), jnp.float32),
            in_specs=[vmem_spec()] * 4,
            out_specs=hbm_spec(),
            scratch_shapes=[
                pltpu.VMEM((traces + 16, 2 * rows), jnp.float32),
                pltpu.VMEM((traces, length), jnp.float32),
                pltpu.SemaphoreType.DMA((4,)),
            ],
            compiler_params=params,
            name="subtract",
        )(returned, coefficients, jnp.asarray(back_table), gathers)


def solution(mesh):
    placed = (
        P(("survey", "freq"), None),
        P(("survey", "freq"), None, None, None),
        P(("survey", "freq"), None, None, None),
        P("survey"),
        P("survey"),
    )
    return jax.shard_map(
        local, mesh=mesh, in_specs=placed, out_specs=P(("survey", "freq"), None), check_vma=False
    )
```

```python
import functools
import math

import jax
import jax.numpy as jnp
import ml_dtypes
import numpy as np
from jax import lax
from jax.experimental import pallas as pl
from jax.experimental.pallas import tpu as pltpu
from jax.sharding import PartitionSpec as P

FIRST = 40
REACH = 4
COST = (10**11, 40_000_000)
VMEM_LIMIT = 32 * 1024 * 1024


def split_halves(values):
    values = values.astype(np.float32)
    high = values.astype(ml_dtypes.bfloat16)
    low = (values - high.astype(np.float32)).astype(ml_dtypes.bfloat16)
    return high, low


def bins_in_order(band_bins, slots):
    return FIRST + np.arange(band_bins).reshape(-1, slots)[::-1].reshape(-1)


def row_tables(band_bins, slots, length):
    bin_ids = bins_in_order(band_bins, slots)
    angles = 2.0 * np.pi / length * (bin_ids[:, None] * np.arange(length)[None, :] % length)
    return np.stack([np.cos(angles), -np.sin(angles)], axis=1).reshape(2 * band_bins, length)


def lag_tables(band_bins, slots, lags, length):
    bin_ids = bins_in_order(band_bins, slots)
    lag_ids = np.arange(lags) - lags // 2
    angles = 2.0 * np.pi / length * (bin_ids[:, None] * lag_ids[None, :] % length)
    cosine, sine = np.cos(angles), np.sin(angles)
    weight = (bin_ids / (FIRST + band_bins))[:, None]
    real = np.stack([cosine, sine, -weight * sine, weight * cosine])
    imag = np.stack([sine, -cosine, weight * cosine, weight * sine])
    own = np.stack([real, real], axis=2).reshape(4, 2 * band_bins, lags)
    partner = np.stack([-imag, imag], axis=2).reshape(4, 2 * band_bins, lags)
    both = np.concatenate([own, partner], axis=1)
    return np.swapaxes(both, 1, 2).reshape(4 * lags, 4 * band_bins).astype(np.float32)


def split_array(values):
    high = values.astype(jnp.bfloat16)
    low = (values - high.astype(jnp.float32)).astype(jnp.bfloat16)
    return high, low


def swap_pairs(values):
    rows = values.shape[0]
    parity = lax.broadcasted_iota(jnp.int32, values.shape, 0) % 2
    return jnp.where(
        parity == 0, pltpu.roll(values, rows - 1, 0), pltpu.roll(values, 1, 0)
    )


def filter_lanes(kept_bins, slots, slice_ref, filters_ref, lag_ref):
    _, components, _ = filters_ref.shape
    lanes = lag_ref.shape[1]
    rows = lanes // 2
    flat = jnp.concatenate([filters_ref[:, part] for part in range(components)], axis=1)
    total = jnp.dot(
        flat, lag_ref[...], precision=lax.Precision.HIGHEST, preferred_element_type=jnp.float32
    )
    lane_ids = lax.broadcasted_iota(jnp.int32, (1, lanes), 1) % rows
    group = lane_ids // (2 * slots)
    slot = lane_ids // 2 % slots
    count = jnp.zeros((1, lanes), jnp.int32)
    devices = rows // (2 * slots)
    for device in range(devices):
        count = jnp.where(group == devices - 1 - device, slice_ref[device], count)
    return total * jnp.where(slot < count, math.sqrt(2.0 / kept_bins), 0.0)


def spectrum_kernel(chunk, gathers_ref, table_ref, out_ref, held, table, sems):
    length = gathers_ref.shape[1]
    rows = table_ref.shape[0] // 2
    copies = []
    for step in range(length // chunk):
        part = pl.ds(step * chunk, chunk)
        copies.append(
            (
                pltpu.make_async_copy(gathers_ref.at[:, part], held.at[:, part], sems.at[0, step]),
                pltpu.make_async_copy(table_ref.at[:, part], table.at[:, part], sems.at[1, step]),
            )
        )
    for pair in copies:
        for copy in pair:
            copy.start()
    dot = functools.partial(
        lax.dot_general,
        dimension_numbers=(((1,), (1,)), ((), ())),
        preferred_element_type=jnp.float32,
    )
    total = jnp.zeros((rows, held.shape[0]), jnp.float32)
    for step, pair in enumerate(copies):
        for copy in pair:
            copy.wait()
        part = pl.ds(step * chunk, chunk)
        high, low = split_array(held[:, part])
        weights = table[:, part]
        both = dot(weights, high)
        total = total + both[:rows] + (both[rows:] + dot(weights[:rows], low))
    out_ref[...] = total.astype(jnp.bfloat16).reshape(out_ref.shape)


def predict_kernel(
    kept_bins,
    tile_ref,
    slice_ref,
    filters_ref,
    lag_ref,
    incoming_ref,
    operator_ref,
    out_ref,
    coefficient_ref,
    holder,
):
    devices, group_rows, traces = incoming_ref.shape
    slots, _, receivers, _ = operator_ref.shape
    per_shot = receivers // traces
    shots = devices // per_shot
    rows = shots * group_rows
    for k in range(devices):
        holder[tile_ref[k]] = devices - 1 - k
    columns = []
    for q in range(per_shot):
        parts = [
            incoming_ref[holder[s * per_shot + q]].astype(jnp.float32) for s in range(shots)
        ]
        columns.append(jnp.concatenate(parts, axis=0))
    spectrum = jnp.concatenate(columns, axis=1).astype(jnp.bfloat16)
    row_ids = lax.broadcasted_iota(jnp.int32, (rows, receivers), 0)
    dot = functools.partial(
        lax.dot_general,
        dimension_numbers=(((1,), (1,)), ((), ())),
        preferred_element_type=jnp.float32,
    )
    predicted = jnp.zeros((rows, receivers), jnp.float32)
    for slot in range(slots):
        by_real = dot(spectrum, operator_ref[slot, 0])
        by_imag = swap_pairs(dot(spectrum, operator_ref[slot, 1]))
        product = jnp.where(row_ids % 2 == 0, by_real - by_imag, by_real + by_imag)
        predicted = jnp.where(row_ids // 2 % slots == slot, product, predicted)
    lane_ids = lax.broadcasted_iota(jnp.int32, (rows, receivers), 1) % traces
    edge = jnp.zeros((rows, traces), jnp.float32)
    after = jnp.concatenate([predicted[:, traces:], edge], axis=1)
    before = jnp.concatenate([edge, predicted[:, :-traces]], axis=1)
    halo = jnp.where(lane_ids < REACH, after, jnp.where(lane_ids >= traces - REACH, before, 0.0))
    for s in range(shots):
        for q in range(per_shot):
            where = (slice(s * group_rows, (s + 1) * group_rows), slice(q * traces, (q + 1) * traces))
            both = jnp.concatenate([predicted[where], halo[where]], axis=1)
            out_ref[holder[s * per_shot + q]] = both.astype(jnp.bfloat16)
    coefficient_ref[...] = filter_lanes(kept_bins, slots, slice_ref, filters_ref, lag_ref)


def subtract_kernel(
    chunk, returned_ref, coefficient_ref, table_ref, gathers_ref, out_ref, spread, result, sems
):
    devices, group_rows, _ = returned_ref.shape
    rows = devices * group_rows
    traces, length = gathers_ref.shape
    offsets = coefficient_ref.shape[0]
    own = returned_ref[...].astype(jnp.float32).reshape(rows, 2 * traces)
    both = jnp.concatenate([own, swap_pairs(own)], axis=0)
    halo = jnp.transpose(both[:, traces:])
    spread[0:8] = halo[traces - 8 :]
    spread[8 : 8 + traces] = jnp.transpose(both[:, :traces])
    spread[8 + traces : 16 + traces] = halo[:8]
    total = jnp.zeros((traces, 2 * rows), jnp.float32)
    for offset in range(offsets):
        first = 8 + offset - offsets // 2
        total = total + spread[first : first + traces] * coefficient_ref[offset : offset + 1]
    total = total + pltpu.roll(total, rows, 1)
    high = total.astype(jnp.bfloat16).astype(jnp.float32)
    lane_ids = lax.broadcasted_iota(jnp.int32, total.shape, 1)
    mixed = jnp.where(lane_ids < rows, high, total - high)
    stacked = jnp.concatenate([mixed, high[:, :rows]], axis=1).astype(jnp.bfloat16)
    copies = []
    for step in range(length // chunk):
        part = pl.ds(step * chunk, chunk)
        response = jnp.dot(stacked, table_ref[:, part], preferred_element_type=jnp.float32)
        result[:, part] = gathers_ref[:, part] - response
        copy = pltpu.make_async_copy(result.at[:, part], out_ref.at[:, part], sems.at[step])
        copy.start()
        copies.append(copy)
    for copy in copies:
        copy.wait()


def vmem_spec():
    return pl.BlockSpec(memory_space=pltpu.VMEM)


def smem_spec():
    return pl.BlockSpec(memory_space=pltpu.SMEM)


def hbm_spec():
    return pl.BlockSpec(memory_space=pltpu.HBM)


def in_hbm(values):
    return pltpu.with_memory_space_constraint(values, pltpu.HBM)


def exchange(chunks):
    order = list(range(chunks.shape[0]))[::-1]
    return lax.all_to_all(chunks, "freq", 0, 0, axis_index_groups=[order], tiled=True)


def local(gathers, operator, filters, tile_of, slice_len):
    devices = lax.axis_size("freq")
    traces, length = gathers.shape
    slots, _, receivers, _ = operator.shape
    band_bins = slots * devices
    rows = 2 * band_bins
    group_rows = 2 * slots
    kept_bins = 5 * devices // 4
    offsets, lags = filters.shape[2], filters.shape[3]
    chunk = length // 4
    params = pltpu.CompilerParams(vmem_limit_bytes=VMEM_LIMIT)
    table = row_tables(band_bins, slots, length)
    forward_table = np.concatenate(split_halves(table / math.sqrt(length)), axis=0)
    back_high, back_low = split_halves(table)
    back_table = np.concatenate([back_high, back_high, back_low], axis=0)
    tables = lag_tables(band_bins, slots, lags, length)
    with jax.named_scope("spectrum"):
        outgoing = pl.pallas_call(
            functools.partial(spectrum_kernel, chunk),
            out_shape=jax.ShapeDtypeStruct((devices, group_rows, traces), jnp.bfloat16),
            in_specs=[hbm_spec()] * 2,
            out_specs=vmem_spec(),
            scratch_shapes=[
                pltpu.VMEM((traces, length), jnp.float32),
                pltpu.VMEM((2 * rows, length), jnp.bfloat16),
                pltpu.SemaphoreType.DMA((2, length // chunk)),
            ],
            compiler_params=params,
            cost_estimate=pl.CostEstimate(flops=COST[0], bytes_accessed=COST[1], transcendentals=0),
            name="spectrum",
        )(in_hbm(gathers), in_hbm(jnp.asarray(forward_table)))
    incoming = exchange(outgoing)
    with jax.named_scope("predict"):
        sending, coefficients = pl.pallas_call(
            functools.partial(predict_kernel, kept_bins),
            out_shape=[
                jax.ShapeDtypeStruct((devices, group_rows, 2 * traces), jnp.bfloat16),
                jax.ShapeDtypeStruct((offsets, 2 * rows), jnp.float32),
            ],
            in_specs=[smem_spec()] * 2 + [vmem_spec()] * 4,
            out_specs=[vmem_spec()] * 2,
            scratch_shapes=[pltpu.SMEM((devices,), jnp.int32)],
            compiler_params=params,
            name="predict",
        )(
            tile_of,
            slice_len,
            jnp.transpose(filters[0], (1, 0, 2)),
            jnp.asarray(tables),
            incoming,
            operator,
        )
    returned = exchange(sending)
    with jax.named_scope("subtract"):
        return pl.pallas_call(
            functools.partial(subtract_kernel, length // 4),
            out_shape=jax.ShapeDtypeStruct((traces, length), jnp.float32),
            in_specs=[vmem_spec()] * 4,
            out_specs=hbm_spec(),
            scratch_shapes=[
                pltpu.VMEM((traces + 16, 2 * rows), jnp.float32),
                pltpu.VMEM((traces, length), jnp.float32),
                pltpu.SemaphoreType.DMA((4,)),
            ],
            compiler_params=params,
            name="subtract",
        )(returned, coefficients, jnp.asarray(back_table), gathers)


def solution(mesh):
    placed = (
        P(("survey", "freq"), None),
        P(("survey", "freq"), None, None, None),
        P(("survey", "freq"), None, None, None),
        P("survey"),
        P("survey"),
    )
    return jax.shard_map(
        local, mesh=mesh, in_specs=placed, out_specs=P(("survey", "freq"), None), check_vma=False
    )
```

```python
import functools
import math

import jax
import jax.numpy as jnp
import ml_dtypes
import numpy as np
from jax import lax
from jax.experimental import pallas as pl
from jax.experimental.pallas import tpu as pltpu
from jax.sharding import PartitionSpec as P

FIRST = 40
REACH = 4
SPAN = 256
COST = (10**11, 40_000_000)
VMEM_LIMIT = 32 * 1024 * 1024


def split_halves(values):
    values = values.astype(np.float32)
    high = values.astype(ml_dtypes.bfloat16)
    low = (values - high.astype(np.float32)).astype(ml_dtypes.bfloat16)
    return high, low


def bins_in_order(band_bins, slots):
    return FIRST + np.arange(band_bins).reshape(-1, slots)[::-1].reshape(-1)


def row_tables(band_bins, slots, length):
    bin_ids = bins_in_order(band_bins, slots)
    angles = 2.0 * np.pi / length * (bin_ids[:, None] * np.arange(length)[None, :] % length)
    return np.stack([np.cos(angles), -np.sin(angles)], axis=1).reshape(2 * band_bins, length)


def lag_tables(band_bins, slots, lags, length):
    bin_ids = bins_in_order(band_bins, slots)
    lag_ids = np.arange(lags) - lags // 2
    angles = 2.0 * np.pi / length * (bin_ids[:, None] * lag_ids[None, :] % length)
    cosine, sine = np.cos(angles), np.sin(angles)
    weight = (bin_ids / (FIRST + band_bins))[:, None]
    real = np.stack([cosine, sine, -weight * sine, weight * cosine])
    imag = np.stack([sine, -cosine, weight * cosine, weight * sine])
    own = np.stack([real, real], axis=2).reshape(4, 2 * band_bins, lags)
    partner = np.stack([-imag, imag], axis=2).reshape(4, 2 * band_bins, lags)
    both = np.concatenate([own, partner], axis=1)
    return np.swapaxes(both, 1, 2).reshape(4 * lags, 4 * band_bins).astype(np.float32)


def split_array(values):
    high = values.astype(jnp.bfloat16)
    low = (values - high.astype(jnp.float32)).astype(jnp.bfloat16)
    return high, low


def swap_pairs(values):
    rows = values.shape[0]
    parity = lax.broadcasted_iota(jnp.int32, values.shape, 0) % 2
    return jnp.where(
        parity == 0, pltpu.roll(values, rows - 1, 0), pltpu.roll(values, 1, 0)
    )


def filter_lanes(kept_bins, slots, slice_ref, filters_ref, lag_ref):
    _, components, _ = filters_ref.shape
    lanes = lag_ref.shape[1]
    rows = lanes // 2
    flat = jnp.concatenate([filters_ref[:, part] for part in range(components)], axis=1)
    total = jnp.dot(
        flat, lag_ref[...], precision=lax.Precision.HIGHEST, preferred_element_type=jnp.float32
    )
    lane_ids = lax.broadcasted_iota(jnp.int32, (1, lanes), 1) % rows
    group = lane_ids // (2 * slots)
    slot = lane_ids // 2 % slots
    count = jnp.zeros((1, lanes), jnp.int32)
    devices = rows // (2 * slots)
    for device in range(devices):
        count = jnp.where(group == devices - 1 - device, slice_ref[device], count)
    return total * jnp.where(slot < count, math.sqrt(2.0 / kept_bins), 0.0)


def spectrum_kernel(chunk, gathers_ref, table_ref, out_ref, held, table, sems):
    length = gathers_ref.shape[1]
    rows = table_ref.shape[0] // 2
    copies = []
    for step in range(length // chunk):
        part = pl.ds(step * chunk, chunk)
        copies.append(
            (
                pltpu.make_async_copy(gathers_ref.at[:, part], held.at[:, part], sems.at[0, step]),
                pltpu.make_async_copy(table_ref.at[:, part], table.at[:, part], sems.at[1, step]),
            )
        )
    for pair in copies:
        for copy in pair:
            copy.start()
    dot = functools.partial(
        lax.dot_general,
        dimension_numbers=(((1,), (1,)), ((), ())),
        preferred_element_type=jnp.float32,
    )
    total = jnp.zeros((rows, held.shape[0]), jnp.float32)
    for step, pair in enumerate(copies):
        for copy in pair:
            copy.wait()
        part = pl.ds(step * chunk, chunk)
        high, low = split_array(held[:, part])
        weights = table[:, part]
        both = dot(weights, high)
        total = total + both[:rows] + (both[rows:] + dot(weights[:rows], low))
    out_ref[...] = total.astype(jnp.bfloat16).reshape(out_ref.shape)


def predict_kernel(
    kept_bins,
    tile_ref,
    slice_ref,
    filters_ref,
    lag_ref,
    incoming_ref,
    operator_ref,
    out_ref,
    coefficient_ref,
    holder,
):
    devices, group_rows, traces = incoming_ref.shape
    slots, _, receivers, _ = operator_ref.shape
    per_shot = receivers // traces
    shots = devices // per_shot
    rows = shots * group_rows
    for k in range(devices):
        holder[tile_ref[k]] = devices - 1 - k
    columns = []
    for q in range(per_shot):
        parts = [
            incoming_ref[holder[s * per_shot + q]].astype(jnp.float32) for s in range(shots)
        ]
        columns.append(jnp.concatenate(parts, axis=0))
    spectrum = jnp.concatenate(columns, axis=1).astype(jnp.bfloat16)
    coefficient_ref[...] = filter_lanes(kept_bins, slots, slice_ref, filters_ref, lag_ref)
    span = SPAN
    row_ids = lax.broadcasted_iota(jnp.int32, (rows, span), 0)
    lane_ids = lax.broadcasted_iota(jnp.int32, (rows, traces), 1)
    dot = functools.partial(
        lax.dot_general,
        dimension_numbers=(((1,), (1,)), ((), ())),
        preferred_element_type=jnp.float32,
    )
    edge = jnp.zeros((rows, traces), jnp.float32)
    predicted = [edge]

    def cut(q):
        before, here, after = predicted[q : q + 3]
        halo = jnp.where(
            lane_ids < REACH, after, jnp.where(lane_ids >= traces - REACH, before, 0.0)
        )
        both = jnp.concatenate([here, halo], axis=1)
        for s in range(shots):
            piece = both[s * group_rows : (s + 1) * group_rows]
            out_ref[holder[s * per_shot + q]] = piece.astype(jnp.bfloat16)

    done = 0
    for first in range(0, receivers, span):
        where = pl.ds(first, span)
        block = jnp.zeros((rows, span), jnp.float32)
        for slot in range(slots):
            by_real = dot(spectrum, operator_ref[slot, 0, where])
            by_imag = swap_pairs(dot(spectrum, operator_ref[slot, 1, where]))
            product = jnp.where(row_ids % 2 == 0, by_real - by_imag, by_real + by_imag)
            block = jnp.where(row_ids // 2 % slots == slot, product, block)
        predicted.extend(block[:, i : i + traces] for i in range(0, span, traces))
        while done + 3 <= len(predicted):
            cut(done)
            done += 1
    predicted.append(edge)
    cut(done)


def subtract_kernel(
    chunk, returned_ref, coefficient_ref, table_ref, gathers_ref, out_ref, spread, result, sems
):
    devices, group_rows, _ = returned_ref.shape
    rows = devices * group_rows
    traces, length = gathers_ref.shape
    offsets = coefficient_ref.shape[0]
    own = returned_ref[...].astype(jnp.float32).reshape(rows, 2 * traces)
    both = jnp.concatenate([own, swap_pairs(own)], axis=0)
    halo = jnp.transpose(both[:, traces:])
    spread[0:8] = halo[traces - 8 :]
    spread[8 : 8 + traces] = jnp.transpose(both[:, :traces])
    spread[8 + traces : 16 + traces] = halo[:8]
    total = jnp.zeros((traces, 2 * rows), jnp.float32)
    for offset in range(offsets):
        first = 8 + offset - offsets // 2
        total = total + spread[first : first + traces] * coefficient_ref[offset : offset + 1]
    total = total + pltpu.roll(total, rows, 1)
    high = total.astype(jnp.bfloat16).astype(jnp.float32)
    lane_ids = lax.broadcasted_iota(jnp.int32, total.shape, 1)
    mixed = jnp.where(lane_ids < rows, high, total - high)
    stacked = jnp.concatenate([mixed, high[:, :rows]], axis=1).astype(jnp.bfloat16)
    copies = []
    for step in range(length // chunk):
        part = pl.ds(step * chunk, chunk)
        response = jnp.dot(stacked, table_ref[:, part], preferred_element_type=jnp.float32)
        result[:, part] = gathers_ref[:, part] - response
        copy = pltpu.make_async_copy(result.at[:, part], out_ref.at[:, part], sems.at[step])
        copy.start()
        copies.append(copy)
    for copy in copies:
        copy.wait()


def vmem_spec():
    return pl.BlockSpec(memory_space=pltpu.VMEM)


def smem_spec():
    return pl.BlockSpec(memory_space=pltpu.SMEM)


def hbm_spec():
    return pl.BlockSpec(memory_space=pltpu.HBM)


def in_hbm(values):
    return pltpu.with_memory_space_constraint(values, pltpu.HBM)


def exchange(chunks):
    order = list(range(chunks.shape[0]))[::-1]
    return lax.all_to_all(chunks, "freq", 0, 0, axis_index_groups=[order], tiled=True)


def local(gathers, operator, filters, tile_of, slice_len):
    devices = lax.axis_size("freq")
    traces, length = gathers.shape
    slots, _, receivers, _ = operator.shape
    band_bins = slots * devices
    rows = 2 * band_bins
    group_rows = 2 * slots
    kept_bins = 5 * devices // 4
    offsets, lags = filters.shape[2], filters.shape[3]
    chunk = length // 2
    params = pltpu.CompilerParams(vmem_limit_bytes=VMEM_LIMIT)
    table = row_tables(band_bins, slots, length)
    forward_table = np.concatenate(split_halves(table / math.sqrt(length)), axis=0)
    back_high, back_low = split_halves(table)
    back_table = np.concatenate([back_high, back_high, back_low], axis=0)
    tables = lag_tables(band_bins, slots, lags, length)
    with jax.named_scope("spectrum"):
        outgoing = pl.pallas_call(
            functools.partial(spectrum_kernel, chunk),
            out_shape=jax.ShapeDtypeStruct((devices, group_rows, traces), jnp.bfloat16),
            in_specs=[hbm_spec()] * 2,
            out_specs=vmem_spec(),
            scratch_shapes=[
                pltpu.VMEM((traces, length), jnp.float32),
                pltpu.VMEM((2 * rows, length), jnp.bfloat16),
                pltpu.SemaphoreType.DMA((2, length // chunk)),
            ],
            compiler_params=params,
            cost_estimate=pl.CostEstimate(flops=COST[0], bytes_accessed=COST[1], transcendentals=0),
            name="spectrum",
        )(in_hbm(gathers), in_hbm(jnp.asarray(forward_table)))
    incoming = exchange(outgoing)
    with jax.named_scope("predict"):
        sending, coefficients = pl.pallas_call(
            functools.partial(predict_kernel, kept_bins),
            out_shape=[
                jax.ShapeDtypeStruct((devices, group_rows, 2 * traces), jnp.bfloat16),
                jax.ShapeDtypeStruct((offsets, 2 * rows), jnp.float32),
            ],
            in_specs=[smem_spec()] * 2 + [vmem_spec()] * 4,
            out_specs=[vmem_spec()] * 2,
            scratch_shapes=[pltpu.SMEM((devices,), jnp.int32)],
            compiler_params=params,
            name="predict",
        )(
            tile_of,
            slice_len,
            jnp.transpose(filters[0], (1, 0, 2)),
            jnp.asarray(tables),
            incoming,
            operator,
        )
    returned = exchange(sending)
    with jax.named_scope("subtract"):
        return pl.pallas_call(
            functools.partial(subtract_kernel, length // 4),
            out_shape=jax.ShapeDtypeStruct((traces, length), jnp.float32),
            in_specs=[vmem_spec()] * 4,
            out_specs=hbm_spec(),
            scratch_shapes=[
                pltpu.VMEM((traces + 16, 2 * rows), jnp.float32),
                pltpu.VMEM((traces, length), jnp.float32),
                pltpu.SemaphoreType.DMA((4,)),
            ],
            compiler_params=params,
            name="subtract",
        )(returned, coefficients, jnp.asarray(back_table), gathers)


def solution(mesh):
    placed = (
        P(("survey", "freq"), None),
        P(("survey", "freq"), None, None, None),
        P(("survey", "freq"), None, None, None),
        P("survey"),
        P("survey"),
    )
    return jax.shard_map(
        local, mesh=mesh, in_specs=placed, out_specs=P(("survey", "freq"), None), check_vma=False
    )
```

```python
import functools
import math

import jax
import jax.numpy as jnp
import ml_dtypes
import numpy as np
from jax import lax
from jax.experimental import pallas as pl
from jax.experimental.pallas import tpu as pltpu
from jax.sharding import PartitionSpec as P

FIRST = 40
REACH = 4
COST = (10**11, 40_000_000)
VMEM_LIMIT = 32 * 1024 * 1024


def split_halves(values):
    values = values.astype(np.float32)
    high = values.astype(ml_dtypes.bfloat16)
    low = (values - high.astype(np.float32)).astype(ml_dtypes.bfloat16)
    return high, low


def bins_in_order(band_bins, slots):
    return FIRST + np.arange(band_bins).reshape(-1, slots)[::-1].reshape(-1)


def row_tables(band_bins, slots, length):
    bin_ids = bins_in_order(band_bins, slots)
    angles = 2.0 * np.pi / length * (bin_ids[:, None] * np.arange(length)[None, :] % length)
    return np.stack([np.cos(angles), -np.sin(angles)], axis=1).reshape(2 * band_bins, length)


def lag_tables(band_bins, slots, lags, length):
    bin_ids = bins_in_order(band_bins, slots)
    lag_ids = np.arange(lags) - lags // 2
    angles = 2.0 * np.pi / length * (bin_ids[:, None] * lag_ids[None, :] % length)
    cosine, sine = np.cos(angles), np.sin(angles)
    weight = (bin_ids / (FIRST + band_bins))[:, None]
    real = np.stack([cosine, sine, -weight * sine, weight * cosine])
    imag = np.stack([sine, -cosine, weight * cosine, weight * sine])
    own = np.stack([real, real], axis=2).reshape(4, 2 * band_bins, lags)
    partner = np.stack([-imag, imag], axis=2).reshape(4, 2 * band_bins, lags)
    both = np.concatenate([own, partner], axis=1)
    return np.swapaxes(both, 1, 2).reshape(4 * lags, 4 * band_bins).astype(np.float32)


def split_array(values):
    high = values.astype(jnp.bfloat16)
    low = (values - high.astype(jnp.float32)).astype(jnp.bfloat16)
    return high, low


def swap_pairs(values):
    rows = values.shape[0]
    parity = lax.broadcasted_iota(jnp.int32, values.shape, 0) % 2
    return jnp.where(
        parity == 0, pltpu.roll(values, rows - 1, 0), pltpu.roll(values, 1, 0)
    )


def filter_lanes(kept_bins, slots, slice_ref, filters_ref, lag_ref):
    _, components, _ = filters_ref.shape
    lanes = lag_ref.shape[1]
    rows = lanes // 2
    flat = jnp.concatenate([filters_ref[:, part] for part in range(components)], axis=1)
    total = jnp.dot(
        flat, lag_ref[...], precision=lax.Precision.HIGHEST, preferred_element_type=jnp.float32
    )
    lane_ids = lax.broadcasted_iota(jnp.int32, (1, lanes), 1) % rows
    group = lane_ids // (2 * slots)
    slot = lane_ids // 2 % slots
    count = jnp.zeros((1, lanes), jnp.int32)
    devices = rows // (2 * slots)
    for device in range(devices):
        count = jnp.where(group == devices - 1 - device, slice_ref[device], count)
    return total * jnp.where(slot < count, math.sqrt(2.0 / kept_bins), 0.0)


def spectrum_kernel(chunk, gathers_ref, table_ref, out_ref, held, table, sems):
    length = gathers_ref.shape[1]
    rows = table_ref.shape[0] // 2
    copies = []
    for step in range(length // chunk):
        part = pl.ds(step * chunk, chunk)
        copies.append(
            (
                pltpu.make_async_copy(gathers_ref.at[:, part], held.at[:, part], sems.at[0, step]),
                pltpu.make_async_copy(table_ref.at[:, part], table.at[:, part], sems.at[1, step]),
            )
        )
    for pair in copies:
        for copy in pair:
            copy.start()
    dot = functools.partial(
        lax.dot_general,
        dimension_numbers=(((1,), (1,)), ((), ())),
        preferred_element_type=jnp.float32,
    )
    total = jnp.zeros((rows, held.shape[0]), jnp.float32)
    for step, pair in enumerate(copies):
        for copy in pair:
            copy.wait()
        part = pl.ds(step * chunk, chunk)
        high, low = split_array(held[:, part])
        weights = table[:, part]
        both = dot(weights, high)
        total = total + both[:rows] + (both[rows:] + dot(weights[:rows], low))
    out_ref[...] = total.astype(jnp.bfloat16).astype(out_ref.dtype).reshape(out_ref.shape)


def predict_kernel(
    kept_bins,
    tile_ref,
    slice_ref,
    filters_ref,
    lag_ref,
    incoming_ref,
    operator_ref,
    out_ref,
    coefficient_ref,
    holder,
):
    devices, group_rows, traces = incoming_ref.shape
    slots, _, receivers, _ = operator_ref.shape
    per_shot = receivers // traces
    shots = devices // per_shot
    rows = shots * group_rows
    for k in range(devices):
        holder[tile_ref[k]] = devices - 1 - k
    columns = []
    for q in range(per_shot):
        parts = [
            incoming_ref[holder[s * per_shot + q]].astype(jnp.float32) for s in range(shots)
        ]
        columns.append(jnp.concatenate(parts, axis=0))
    spectrum = jnp.concatenate(columns, axis=1).astype(jnp.bfloat16)
    row_ids = lax.broadcasted_iota(jnp.int32, (rows, receivers), 0)
    dot = functools.partial(
        lax.dot_general,
        dimension_numbers=(((1,), (1,)), ((), ())),
        preferred_element_type=jnp.float32,
    )
    predicted = jnp.zeros((rows, receivers), jnp.float32)
    for slot in range(slots):
        by_real = dot(spectrum, operator_ref[slot, 0])
        by_imag = swap_pairs(dot(spectrum, operator_ref[slot, 1]))
        product = jnp.where(row_ids % 2 == 0, by_real - by_imag, by_real + by_imag)
        predicted = jnp.where(row_ids // 2 % slots == slot, product, predicted)
    lane_ids = lax.broadcasted_iota(jnp.int32, (rows, receivers), 1) % traces
    edge = jnp.zeros((rows, traces), jnp.float32)
    after = jnp.concatenate([predicted[:, traces:], edge], axis=1)
    before = jnp.concatenate([edge, predicted[:, :-traces]], axis=1)
    halo = jnp.where(lane_ids < REACH, after, jnp.where(lane_ids >= traces - REACH, before, 0.0))
    for s in range(shots):
        for q in range(per_shot):
            where = (slice(s * group_rows, (s + 1) * group_rows), slice(q * traces, (q + 1) * traces))
            both = jnp.concatenate([predicted[where], halo[where]], axis=0)
            out_ref[holder[s * per_shot + q]] = both.astype(jnp.bfloat16)
    coefficient_ref[...] = filter_lanes(kept_bins, slots, slice_ref, filters_ref, lag_ref)


def subtract_kernel(
    chunk, returned_ref, coefficient_ref, table_ref, gathers_ref, out_ref, spread, result, sems
):
    devices, group_rows, _ = returned_ref.shape
    group_rows = group_rows // 2
    rows = devices * group_rows
    traces, length = gathers_ref.shape
    offsets = coefficient_ref.shape[0]
    came = returned_ref[...].astype(jnp.float32)
    own = came[:, :group_rows].reshape(rows, traces)
    edges = came[:, group_rows:].reshape(rows, traces)
    halo = jnp.transpose(jnp.concatenate([edges, swap_pairs(edges)], axis=0))
    spread[0:8] = halo[traces - 8 :]
    spread[8 : 8 + traces] = jnp.transpose(jnp.concatenate([own, swap_pairs(own)], axis=0))
    spread[8 + traces : 16 + traces] = halo[:8]
    total = jnp.zeros((traces, 2 * rows), jnp.float32)
    for offset in range(offsets):
        first = 8 + offset - offsets // 2
        total = total + spread[first : first + traces] * coefficient_ref[offset : offset + 1]
    total = total + pltpu.roll(total, rows, 1)
    high = total.astype(jnp.bfloat16).astype(jnp.float32)
    lane_ids = lax.broadcasted_iota(jnp.int32, total.shape, 1)
    mixed = jnp.where(lane_ids < rows, high, total - high)
    stacked = jnp.concatenate([mixed, high[:, :rows]], axis=1).astype(jnp.bfloat16)
    copies = []
    for step in range(length // chunk):
        part = pl.ds(step * chunk, chunk)
        response = jnp.dot(stacked, table_ref[:, part], preferred_element_type=jnp.float32)
        result[:, part] = gathers_ref[:, part] - response
        copy = pltpu.make_async_copy(result.at[:, part], out_ref.at[:, part], sems.at[step])
        copy.start()
        copies.append(copy)
    for copy in copies:
        copy.wait()


def vmem_spec():
    return pl.BlockSpec(memory_space=pltpu.VMEM)


def smem_spec():
    return pl.BlockSpec(memory_space=pltpu.SMEM)


def hbm_spec():
    return pl.BlockSpec(memory_space=pltpu.HBM)


def in_hbm(values):
    return pltpu.with_memory_space_constraint(values, pltpu.HBM)


def exchange(chunks):
    order = list(range(chunks.shape[0]))[::-1]
    return lax.all_to_all(chunks, "freq", 0, 0, axis_index_groups=[order], tiled=True)


def local(gathers, operator, filters, tile_of, slice_len):
    devices = lax.axis_size("freq")
    traces, length = gathers.shape
    slots, _, receivers, _ = operator.shape
    band_bins = slots * devices
    rows = 2 * band_bins
    group_rows = 2 * slots
    kept_bins = 5 * devices // 4
    offsets, lags = filters.shape[2], filters.shape[3]
    chunk = length
    params = pltpu.CompilerParams(vmem_limit_bytes=VMEM_LIMIT)
    table = row_tables(band_bins, slots, length)
    forward_table = np.concatenate(split_halves(table / math.sqrt(length)), axis=0)
    back_high, back_low = split_halves(table)
    back_table = np.concatenate([back_high, back_high, back_low], axis=0)
    tables = lag_tables(band_bins, slots, lags, length)
    with jax.named_scope("spectrum"):
        outgoing = pl.pallas_call(
            functools.partial(spectrum_kernel, chunk),
            out_shape=jax.ShapeDtypeStruct((devices, group_rows, traces), jnp.float32),
            in_specs=[hbm_spec()] * 2,
            out_specs=vmem_spec(),
            scratch_shapes=[
                pltpu.VMEM((traces, length), jnp.float32),
                pltpu.VMEM((2 * rows, length), jnp.bfloat16),
                pltpu.SemaphoreType.DMA((2, length // chunk)),
            ],
            compiler_params=params,
            cost_estimate=pl.CostEstimate(flops=COST[0], bytes_accessed=COST[1], transcendentals=0),
            name="spectrum",
        )(in_hbm(gathers), in_hbm(jnp.asarray(forward_table)))
    incoming = exchange(outgoing)
    with jax.named_scope("predict"):
        sending, coefficients = pl.pallas_call(
            functools.partial(predict_kernel, kept_bins),
            out_shape=[
                jax.ShapeDtypeStruct((devices, 2 * group_rows, traces), jnp.bfloat16),
                jax.ShapeDtypeStruct((offsets, 2 * rows), jnp.float32),
            ],
            in_specs=[smem_spec()] * 2 + [vmem_spec()] * 4,
            out_specs=[vmem_spec()] * 2,
            scratch_shapes=[pltpu.SMEM((devices,), jnp.int32)],
            compiler_params=params,
            name="predict",
        )(
            tile_of,
            slice_len,
            jnp.transpose(filters[0], (1, 0, 2)),
            jnp.asarray(tables),
            incoming,
            operator,
        )
    returned = exchange(sending)
    with jax.named_scope("subtract"):
        return pl.pallas_call(
            functools.partial(subtract_kernel, length // 4),
            out_shape=jax.ShapeDtypeStruct((traces, length), jnp.float32),
            in_specs=[vmem_spec()] * 4,
            out_specs=hbm_spec(),
            scratch_shapes=[
                pltpu.VMEM((traces + 16, 2 * rows), jnp.float32),
                pltpu.VMEM((traces, length), jnp.float32),
                pltpu.SemaphoreType.DMA((4,)),
            ],
            compiler_params=params,
            name="subtract",
        )(returned, coefficients, jnp.asarray(back_table), gathers)


def solution(mesh):
    placed = (
        P(("survey", "freq"), None),
        P(("survey", "freq"), None, None, None),
        P(("survey", "freq"), None, None, None),
        P("survey"),
        P("survey"),
    )
    return jax.shard_map(
        local, mesh=mesh, in_specs=placed, out_specs=P(("survey", "freq"), None), check_vma=False
    )
```

```python
import functools
import math

import jax
import jax.numpy as jnp
import ml_dtypes
import numpy as np
from jax import lax
from jax.experimental import pallas as pl
from jax.experimental.pallas import tpu as pltpu
from jax.sharding import PartitionSpec as P

FIRST = 40
REACH = 4
COST = (10**11, 40_000_000)
VMEM_LIMIT = 32 * 1024 * 1024


def split_halves(values):
    values = values.astype(np.float32)
    high = values.astype(ml_dtypes.bfloat16)
    low = (values - high.astype(np.float32)).astype(ml_dtypes.bfloat16)
    return high, low


def exchange_order(devices):
    return [device ^ 1 for device in range(devices)][::-1]


def bins_in_order(band_bins, slots):
    groups = FIRST + np.arange(band_bins).reshape(-1, slots)
    return groups[exchange_order(band_bins // slots)].reshape(-1)


def row_tables(band_bins, slots, length):
    bin_ids = bins_in_order(band_bins, slots)
    angles = 2.0 * np.pi / length * (bin_ids[:, None] * np.arange(length)[None, :] % length)
    return np.stack([np.cos(angles), -np.sin(angles)], axis=1).reshape(2 * band_bins, length)


def lag_tables(band_bins, slots, lags, length):
    bin_ids = bins_in_order(band_bins, slots)
    lag_ids = np.arange(lags) - lags // 2
    angles = 2.0 * np.pi / length * (bin_ids[:, None] * lag_ids[None, :] % length)
    cosine, sine = np.cos(angles), np.sin(angles)
    weight = (bin_ids / (FIRST + band_bins))[:, None]
    real = np.stack([cosine, sine, -weight * sine, weight * cosine])
    imag = np.stack([sine, -cosine, weight * cosine, weight * sine])
    own = np.stack([real, real], axis=2).reshape(4, 2 * band_bins, lags)
    partner = np.stack([-imag, imag], axis=2).reshape(4, 2 * band_bins, lags)
    both = np.concatenate([own, partner], axis=1)
    return np.swapaxes(both, 1, 2).reshape(4 * lags, 4 * band_bins).astype(np.float32)


def split_array(values):
    high = values.astype(jnp.bfloat16)
    low = (values - high.astype(jnp.float32)).astype(jnp.bfloat16)
    return high, low


def swap_pairs(values):
    rows = values.shape[0]
    parity = lax.broadcasted_iota(jnp.int32, values.shape, 0) % 2
    return jnp.where(
        parity == 0, pltpu.roll(values, rows - 1, 0), pltpu.roll(values, 1, 0)
    )


def filter_lanes(kept_bins, slots, slice_ref, filters_ref, lag_ref):
    _, components, _ = filters_ref.shape
    lanes = lag_ref.shape[1]
    rows = lanes // 2
    flat = jnp.concatenate([filters_ref[:, part] for part in range(components)], axis=1)
    total = jnp.dot(
        flat, lag_ref[...], precision=lax.Precision.HIGHEST, preferred_element_type=jnp.float32
    )
    lane_ids = lax.broadcasted_iota(jnp.int32, (1, lanes), 1) % rows
    group = lane_ids // (2 * slots)
    slot = lane_ids // 2 % slots
    count = jnp.zeros((1, lanes), jnp.int32)
    devices = rows // (2 * slots)
    for place, device in enumerate(exchange_order(devices)):
        count = jnp.where(group == place, slice_ref[device], count)
    return total * jnp.where(slot < count, math.sqrt(2.0 / kept_bins), 0.0)


def spectrum_kernel(chunk, gathers_ref, table_ref, out_ref, held, table, sems):
    length = gathers_ref.shape[1]
    rows = table_ref.shape[0] // 2
    copies = []
    for step in range(length // chunk):
        part = pl.ds(step * chunk, chunk)
        copies.append(
            (
                pltpu.make_async_copy(gathers_ref.at[:, part], held.at[:, part], sems.at[0, step]),
                pltpu.make_async_copy(table_ref.at[:, part], table.at[:, part], sems.at[1, step]),
            )
        )
    for pair in copies:
        for copy in pair:
            copy.start()
    dot = functools.partial(
        lax.dot_general,
        dimension_numbers=(((1,), (1,)), ((), ())),
        preferred_element_type=jnp.float32,
    )
    total = jnp.zeros((rows, held.shape[0]), jnp.float32)
    for step, pair in enumerate(copies):
        for copy in pair:
            copy.wait()
        part = pl.ds(step * chunk, chunk)
        high, low = split_array(held[:, part])
        weights = table[:, part]
        both = dot(weights, high)
        total = total + both[:rows] + (both[rows:] + dot(weights[:rows], low))
    out_ref[...] = total.astype(jnp.bfloat16).astype(out_ref.dtype).reshape(out_ref.shape)


def predict_kernel(
    kept_bins,
    tile_ref,
    slice_ref,
    filters_ref,
    lag_ref,
    incoming_ref,
    operator_ref,
    out_ref,
    coefficient_ref,
    holder,
):
    devices, group_rows, traces = incoming_ref.shape
    slots, _, receivers, _ = operator_ref.shape
    per_shot = receivers // traces
    shots = devices // per_shot
    rows = shots * group_rows
    for place, device in enumerate(exchange_order(devices)):
        holder[tile_ref[device]] = place
    columns = []
    for q in range(per_shot):
        parts = [
            incoming_ref[holder[s * per_shot + q]].astype(jnp.float32) for s in range(shots)
        ]
        columns.append(jnp.concatenate(parts, axis=0))
    spectrum = jnp.concatenate(columns, axis=1).astype(jnp.bfloat16)
    row_ids = lax.broadcasted_iota(jnp.int32, (rows, receivers), 0)
    dot = functools.partial(
        lax.dot_general,
        dimension_numbers=(((1,), (1,)), ((), ())),
        preferred_element_type=jnp.float32,
    )
    predicted = jnp.zeros((rows, receivers), jnp.float32)
    for slot in range(slots):
        by_real = dot(spectrum, operator_ref[slot, 0])
        by_imag = swap_pairs(dot(spectrum, operator_ref[slot, 1]))
        product = jnp.where(row_ids % 2 == 0, by_real - by_imag, by_real + by_imag)
        predicted = jnp.where(row_ids // 2 % slots == slot, product, predicted)
    lane_ids = lax.broadcasted_iota(jnp.int32, (rows, receivers), 1) % traces
    edge = jnp.zeros((rows, traces), jnp.float32)
    after = jnp.concatenate([predicted[:, traces:], edge], axis=1)
    before = jnp.concatenate([edge, predicted[:, :-traces]], axis=1)
    halo = jnp.where(lane_ids < REACH, after, jnp.where(lane_ids >= traces - REACH, before, 0.0))
    for s in range(shots):
        for q in range(per_shot):
            where = (slice(s * group_rows, (s + 1) * group_rows), slice(q * traces, (q + 1) * traces))
            both = jnp.concatenate([predicted[where], halo[where]], axis=0)
            out_ref[holder[s * per_shot + q]] = both.astype(jnp.bfloat16)
    coefficient_ref[...] = filter_lanes(kept_bins, slots, slice_ref, filters_ref, lag_ref)


def subtract_kernel(
    chunk, returned_ref, coefficient_ref, table_ref, gathers_ref, out_ref, spread, result, sems
):
    devices, group_rows, _ = returned_ref.shape
    group_rows = group_rows // 2
    rows = devices * group_rows
    traces, length = gathers_ref.shape
    offsets = coefficient_ref.shape[0]
    came = returned_ref[...].astype(jnp.float32)
    own = came[:, :group_rows].reshape(rows, traces)
    edges = came[:, group_rows:].reshape(rows, traces)
    halo = jnp.transpose(jnp.concatenate([edges, swap_pairs(edges)], axis=0))
    spread[0:8] = halo[traces - 8 :]
    spread[8 : 8 + traces] = jnp.transpose(jnp.concatenate([own, swap_pairs(own)], axis=0))
    spread[8 + traces : 16 + traces] = halo[:8]
    total = jnp.zeros((traces, 2 * rows), jnp.float32)
    for offset in range(offsets):
        first = 8 + offset - offsets // 2
        total = total + spread[first : first + traces] * coefficient_ref[offset : offset + 1]
    total = total + pltpu.roll(total, rows, 1)
    high = total.astype(jnp.bfloat16).astype(jnp.float32)
    lane_ids = lax.broadcasted_iota(jnp.int32, total.shape, 1)
    mixed = jnp.where(lane_ids < rows, high, total - high)
    stacked = jnp.concatenate([mixed, high[:, :rows]], axis=1).astype(jnp.bfloat16)
    copies = []
    for step in range(length // chunk):
        part = pl.ds(step * chunk, chunk)
        response = jnp.dot(stacked, table_ref[:, part], preferred_element_type=jnp.float32)
        result[:, part] = gathers_ref[:, part] - response
        copy = pltpu.make_async_copy(result.at[:, part], out_ref.at[:, part], sems.at[step])
        copy.start()
        copies.append(copy)
    for copy in copies:
        copy.wait()


def vmem_spec():
    return pl.BlockSpec(memory_space=pltpu.VMEM)


def smem_spec():
    return pl.BlockSpec(memory_space=pltpu.SMEM)


def hbm_spec():
    return pl.BlockSpec(memory_space=pltpu.HBM)


def in_hbm(values):
    return pltpu.with_memory_space_constraint(values, pltpu.HBM)


def exchange(chunks):
    groups = [exchange_order(chunks.shape[0])]
    return lax.all_to_all(chunks, "freq", 0, 0, axis_index_groups=groups, tiled=True)


def local(gathers, operator, filters, tile_of, slice_len):
    devices = lax.axis_size("freq")
    traces, length = gathers.shape
    slots, _, receivers, _ = operator.shape
    band_bins = slots * devices
    rows = 2 * band_bins
    group_rows = 2 * slots
    kept_bins = 5 * devices // 4
    offsets, lags = filters.shape[2], filters.shape[3]
    chunk = length
    params = pltpu.CompilerParams(vmem_limit_bytes=VMEM_LIMIT)
    table = row_tables(band_bins, slots, length)
    forward_table = np.concatenate(split_halves(table / math.sqrt(length)), axis=0)
    back_high, back_low = split_halves(table)
    back_table = np.concatenate([back_high, back_high, back_low], axis=0)
    tables = lag_tables(band_bins, slots, lags, length)
    with jax.named_scope("spectrum"):
        outgoing = pl.pallas_call(
            functools.partial(spectrum_kernel, chunk),
            out_shape=jax.ShapeDtypeStruct((devices, group_rows, traces), jnp.float32),
            in_specs=[hbm_spec()] * 2,
            out_specs=vmem_spec(),
            scratch_shapes=[
                pltpu.VMEM((traces, length), jnp.float32),
                pltpu.VMEM((2 * rows, length), jnp.bfloat16),
                pltpu.SemaphoreType.DMA((2, length // chunk)),
            ],
            compiler_params=params,
            cost_estimate=pl.CostEstimate(flops=COST[0], bytes_accessed=COST[1], transcendentals=0),
            name="spectrum",
        )(in_hbm(gathers), in_hbm(jnp.asarray(forward_table)))
    incoming = exchange(outgoing)
    with jax.named_scope("predict"):
        sending, coefficients = pl.pallas_call(
            functools.partial(predict_kernel, kept_bins),
            out_shape=[
                jax.ShapeDtypeStruct((devices, 2 * group_rows, traces), jnp.bfloat16),
                jax.ShapeDtypeStruct((offsets, 2 * rows), jnp.float32),
            ],
            in_specs=[smem_spec()] * 2 + [vmem_spec()] * 4,
            out_specs=[vmem_spec()] * 2,
            scratch_shapes=[pltpu.SMEM((devices,), jnp.int32)],
            compiler_params=params,
            name="predict",
        )(
            tile_of,
            slice_len,
            jnp.transpose(filters[0], (1, 0, 2)),
            jnp.asarray(tables),
            incoming,
            operator,
        )
    returned = exchange(sending)
    with jax.named_scope("subtract"):
        return pl.pallas_call(
            functools.partial(subtract_kernel, length // 4),
            out_shape=jax.ShapeDtypeStruct((traces, length), jnp.float32),
            in_specs=[vmem_spec()] * 4,
            out_specs=hbm_spec(),
            scratch_shapes=[
                pltpu.VMEM((traces + 16, 2 * rows), jnp.float32),
                pltpu.VMEM((traces, length), jnp.float32),
                pltpu.SemaphoreType.DMA((4,)),
            ],
            compiler_params=params,
            name="subtract",
        )(returned, coefficients, jnp.asarray(back_table), gathers)


def solution(mesh):
    placed = (
        P(("survey", "freq"), None),
        P(("survey", "freq"), None, None, None),
        P(("survey", "freq"), None, None, None),
        P("survey"),
        P("survey"),
    )
    return jax.shard_map(
        local, mesh=mesh, in_specs=placed, out_specs=P(("survey", "freq"), None), check_vma=False
    )
```

```python
import functools
import math

import jax
import jax.numpy as jnp
import ml_dtypes
import numpy as np
from jax import lax
from jax.experimental import pallas as pl
from jax.experimental.pallas import tpu as pltpu
from jax.sharding import PartitionSpec as P

FIRST = 40
REACH = 4
COST = (10**11, 40_000_000)
VMEM_LIMIT = 32 * 1024 * 1024


def split_halves(values):
    values = values.astype(np.float32)
    high = values.astype(ml_dtypes.bfloat16)
    low = (values - high.astype(np.float32)).astype(ml_dtypes.bfloat16)
    return high, low


def order_out(devices):
    return list(range(devices))[::-1]


def order_back(devices):
    return [devices - 1] + list(range(devices - 1))


def bins_in_order(order, slots):
    return (FIRST + np.array(order)[:, None] * slots + np.arange(slots)).reshape(-1)


def row_tables(bin_ids, length):
    band_bins = len(bin_ids)
    angles = 2.0 * np.pi / length * (bin_ids[:, None] * np.arange(length)[None, :] % length)
    return np.stack([np.cos(angles), -np.sin(angles)], axis=1).reshape(2 * band_bins, length)


def lag_tables(bin_ids, lags, length):
    band_bins = len(bin_ids)
    lag_ids = np.arange(lags) - lags // 2
    angles = 2.0 * np.pi / length * (bin_ids[:, None] * lag_ids[None, :] % length)
    cosine, sine = np.cos(angles), np.sin(angles)
    weight = (bin_ids / (FIRST + band_bins))[:, None]
    real = np.stack([cosine, sine, -weight * sine, weight * cosine])
    imag = np.stack([sine, -cosine, weight * cosine, weight * sine])
    own = np.stack([real, real], axis=2).reshape(4, 2 * band_bins, lags)
    partner = np.stack([-imag, imag], axis=2).reshape(4, 2 * band_bins, lags)
    both = np.concatenate([own, partner], axis=1)
    return np.swapaxes(both, 1, 2).reshape(4 * lags, 4 * band_bins).astype(np.float32)


def split_array(values):
    high = values.astype(jnp.bfloat16)
    low = (values - high.astype(jnp.float32)).astype(jnp.bfloat16)
    return high, low


def swap_pairs(values):
    rows = values.shape[0]
    parity = lax.broadcasted_iota(jnp.int32, values.shape, 0) % 2
    return jnp.where(
        parity == 0, pltpu.roll(values, rows - 1, 0), pltpu.roll(values, 1, 0)
    )


def filter_lanes(kept_bins, slots, slice_ref, filters_ref, lag_ref):
    _, components, _ = filters_ref.shape
    lanes = lag_ref.shape[1]
    rows = lanes // 2
    flat = jnp.concatenate([filters_ref[:, part] for part in range(components)], axis=1)
    total = jnp.dot(
        flat, lag_ref[...], precision=lax.Precision.HIGHEST, preferred_element_type=jnp.float32
    )
    lane_ids = lax.broadcasted_iota(jnp.int32, (1, lanes), 1) % rows
    group = lane_ids // (2 * slots)
    slot = lane_ids // 2 % slots
    count = jnp.zeros((1, lanes), jnp.int32)
    devices = rows // (2 * slots)
    for place, device in enumerate(order_back(devices)):
        count = jnp.where(group == place, slice_ref[device], count)
    return total * jnp.where(slot < count, math.sqrt(2.0 / kept_bins), 0.0)


def spectrum_kernel(chunk, gathers_ref, table_ref, out_ref, held, table, sems):
    length = gathers_ref.shape[1]
    rows = table_ref.shape[0] // 2
    copies = []
    for step in range(length // chunk):
        part = pl.ds(step * chunk, chunk)
        copies.append(
            (
                pltpu.make_async_copy(gathers_ref.at[:, part], held.at[:, part], sems.at[0, step]),
                pltpu.make_async_copy(table_ref.at[:, part], table.at[:, part], sems.at[1, step]),
            )
        )
    for pair in copies:
        for copy in pair:
            copy.start()
    dot = functools.partial(
        lax.dot_general,
        dimension_numbers=(((1,), (1,)), ((), ())),
        preferred_element_type=jnp.float32,
    )
    total = jnp.zeros((rows, held.shape[0]), jnp.float32)
    for step, pair in enumerate(copies):
        for copy in pair:
            copy.wait()
        part = pl.ds(step * chunk, chunk)
        high, low = split_array(held[:, part])
        weights = table[:, part]
        both = dot(weights, high)
        total = total + both[:rows] + (both[rows:] + dot(weights[:rows], low))
    out_ref[...] = total.astype(jnp.bfloat16).astype(out_ref.dtype).reshape(out_ref.shape)


def predict_kernel(
    kept_bins,
    tile_ref,
    slice_ref,
    filters_ref,
    lag_ref,
    incoming_ref,
    operator_ref,
    out_ref,
    coefficient_ref,
    holder,
):
    devices, group_rows, traces = incoming_ref.shape
    slots, _, receivers, _ = operator_ref.shape
    per_shot = receivers // traces
    shots = devices // per_shot
    rows = shots * group_rows
    for place, device in enumerate(order_out(devices)):
        holder[0, tile_ref[device]] = place
    for place, device in enumerate(order_back(devices)):
        holder[1, tile_ref[device]] = place
    columns = []
    for q in range(per_shot):
        parts = [
            incoming_ref[holder[0, s * per_shot + q]].astype(jnp.float32) for s in range(shots)
        ]
        columns.append(jnp.concatenate(parts, axis=0))
    spectrum = jnp.concatenate(columns, axis=1).astype(jnp.bfloat16)
    row_ids = lax.broadcasted_iota(jnp.int32, (rows, receivers), 0)
    dot = functools.partial(
        lax.dot_general,
        dimension_numbers=(((1,), (1,)), ((), ())),
        preferred_element_type=jnp.float32,
    )
    predicted = jnp.zeros((rows, receivers), jnp.float32)
    for slot in range(slots):
        by_real = dot(spectrum, operator_ref[slot, 0])
        by_imag = swap_pairs(dot(spectrum, operator_ref[slot, 1]))
        product = jnp.where(row_ids % 2 == 0, by_real - by_imag, by_real + by_imag)
        predicted = jnp.where(row_ids // 2 % slots == slot, product, predicted)
    lane_ids = lax.broadcasted_iota(jnp.int32, (rows, receivers), 1) % traces
    edge = jnp.zeros((rows, traces), jnp.float32)
    after = jnp.concatenate([predicted[:, traces:], edge], axis=1)
    before = jnp.concatenate([edge, predicted[:, :-traces]], axis=1)
    halo = jnp.where(lane_ids < REACH, after, jnp.where(lane_ids >= traces - REACH, before, 0.0))
    for s in range(shots):
        for q in range(per_shot):
            where = (slice(s * group_rows, (s + 1) * group_rows), slice(q * traces, (q + 1) * traces))
            both = jnp.concatenate([predicted[where], halo[where]], axis=0)
            out_ref[holder[1, s * per_shot + q]] = both.astype(jnp.bfloat16)
    coefficient_ref[...] = filter_lanes(kept_bins, slots, slice_ref, filters_ref, lag_ref)


def subtract_kernel(
    chunk, returned_ref, coefficient_ref, table_ref, gathers_ref, out_ref, spread, result, sems
):
    devices, group_rows, _ = returned_ref.shape
    group_rows = group_rows // 2
    rows = devices * group_rows
    traces, length = gathers_ref.shape
    offsets = coefficient_ref.shape[0]
    came = returned_ref[...].astype(jnp.float32)
    own = came[:, :group_rows].reshape(rows, traces)
    edges = came[:, group_rows:].reshape(rows, traces)
    halo = jnp.transpose(jnp.concatenate([edges, swap_pairs(edges)], axis=0))
    spread[0:8] = halo[traces - 8 :]
    spread[8 : 8 + traces] = jnp.transpose(jnp.concatenate([own, swap_pairs(own)], axis=0))
    spread[8 + traces : 16 + traces] = halo[:8]
    total = jnp.zeros((traces, 2 * rows), jnp.float32)
    for offset in range(offsets):
        first = 8 + offset - offsets // 2
        total = total + spread[first : first + traces] * coefficient_ref[offset : offset + 1]
    total = total + pltpu.roll(total, rows, 1)
    high = total.astype(jnp.bfloat16).astype(jnp.float32)
    lane_ids = lax.broadcasted_iota(jnp.int32, total.shape, 1)
    mixed = jnp.where(lane_ids < rows, high, total - high)
    stacked = jnp.concatenate([mixed, high[:, :rows]], axis=1).astype(jnp.bfloat16)
    copies = []
    for step in range(length // chunk):
        part = pl.ds(step * chunk, chunk)
        response = jnp.dot(stacked, table_ref[:, part], preferred_element_type=jnp.float32)
        result[:, part] = gathers_ref[:, part] - response
        copy = pltpu.make_async_copy(result.at[:, part], out_ref.at[:, part], sems.at[step])
        copy.start()
        copies.append(copy)
    for copy in copies:
        copy.wait()


def vmem_spec():
    return pl.BlockSpec(memory_space=pltpu.VMEM)


def smem_spec():
    return pl.BlockSpec(memory_space=pltpu.SMEM)


def hbm_spec():
    return pl.BlockSpec(memory_space=pltpu.HBM)


def in_hbm(values):
    return pltpu.with_memory_space_constraint(values, pltpu.HBM)


def exchange(chunks, order):
    return lax.all_to_all(chunks, "freq", 0, 0, axis_index_groups=[order], tiled=True)


def local(gathers, operator, filters, tile_of, slice_len):
    devices = lax.axis_size("freq")
    traces, length = gathers.shape
    slots, _, receivers, _ = operator.shape
    band_bins = slots * devices
    rows = 2 * band_bins
    group_rows = 2 * slots
    kept_bins = 5 * devices // 4
    offsets, lags = filters.shape[2], filters.shape[3]
    chunk = length
    params = pltpu.CompilerParams(vmem_limit_bytes=VMEM_LIMIT)
    bins_out = bins_in_order(order_out(devices), slots)
    bins_back = bins_in_order(order_back(devices), slots)
    forward = row_tables(bins_out, length) / math.sqrt(length)
    forward_table = np.concatenate(split_halves(forward), axis=0)
    back_high, back_low = split_halves(row_tables(bins_back, length))
    back_table = np.concatenate([back_high, back_high, back_low], axis=0)
    tables = lag_tables(bins_back, lags, length)
    with jax.named_scope("spectrum"):
        outgoing = pl.pallas_call(
            functools.partial(spectrum_kernel, chunk),
            out_shape=jax.ShapeDtypeStruct((devices, group_rows, traces), jnp.float32),
            in_specs=[hbm_spec()] * 2,
            out_specs=vmem_spec(),
            scratch_shapes=[
                pltpu.VMEM((traces, length), jnp.float32),
                pltpu.VMEM((2 * rows, length), jnp.bfloat16),
                pltpu.SemaphoreType.DMA((2, length // chunk)),
            ],
            compiler_params=params,
            cost_estimate=pl.CostEstimate(flops=COST[0], bytes_accessed=COST[1], transcendentals=0),
            name="spectrum",
        )(in_hbm(gathers), in_hbm(jnp.asarray(forward_table)))
    incoming = exchange(outgoing, order_out(devices))
    with jax.named_scope("predict"):
        sending, coefficients = pl.pallas_call(
            functools.partial(predict_kernel, kept_bins),
            out_shape=[
                jax.ShapeDtypeStruct((devices, 2 * group_rows, traces), jnp.bfloat16),
                jax.ShapeDtypeStruct((offsets, 2 * rows), jnp.float32),
            ],
            in_specs=[smem_spec()] * 2 + [vmem_spec()] * 4,
            out_specs=[vmem_spec()] * 2,
            scratch_shapes=[pltpu.SMEM((2, devices), jnp.int32)],
            compiler_params=params,
            name="predict",
        )(
            tile_of,
            slice_len,
            jnp.transpose(filters[0], (1, 0, 2)),
            jnp.asarray(tables),
            incoming,
            operator,
        )
    returned = exchange(sending, order_back(devices))
    with jax.named_scope("subtract"):
        return pl.pallas_call(
            functools.partial(subtract_kernel, length // 4),
            out_shape=jax.ShapeDtypeStruct((traces, length), jnp.float32),
            in_specs=[vmem_spec()] * 4,
            out_specs=hbm_spec(),
            scratch_shapes=[
                pltpu.VMEM((traces + 16, 2 * rows), jnp.float32),
                pltpu.VMEM((traces, length), jnp.float32),
                pltpu.SemaphoreType.DMA((4,)),
            ],
            compiler_params=params,
            name="subtract",
        )(returned, coefficients, jnp.asarray(back_table), gathers)


def solution(mesh):
    placed = (
        P(("survey", "freq"), None),
        P(("survey", "freq"), None, None, None),
        P(("survey", "freq"), None, None, None),
        P("survey"),
        P("survey"),
    )
    return jax.shard_map(
        local, mesh=mesh, in_specs=placed, out_specs=P(("survey", "freq"), None), check_vma=False
    )
```

```python
import functools
import math

import jax
import jax.numpy as jnp
import ml_dtypes
import numpy as np
from jax import lax
from jax.experimental import pallas as pl
from jax.experimental.pallas import tpu as pltpu
from jax.sharding import PartitionSpec as P

FIRST = 40
REACH = 4
SPAN = 256
COST = (10**11, 40_000_000)
VMEM_LIMIT = 32 * 1024 * 1024


def split_halves(values):
    values = values.astype(np.float32)
    high = values.astype(ml_dtypes.bfloat16)
    low = (values - high.astype(np.float32)).astype(ml_dtypes.bfloat16)
    return high, low


def bins_in_order(band_bins, slots):
    return FIRST + np.arange(band_bins).reshape(-1, slots)[::-1].reshape(-1)


def row_tables(band_bins, slots, length):
    bin_ids = bins_in_order(band_bins, slots)
    angles = 2.0 * np.pi / length * (bin_ids[:, None] * np.arange(length)[None, :] % length)
    return np.stack([np.cos(angles), -np.sin(angles)], axis=1).reshape(2 * band_bins, length)


def lag_tables(band_bins, slots, lags, length):
    bin_ids = bins_in_order(band_bins, slots)
    lag_ids = np.arange(lags) - lags // 2
    angles = 2.0 * np.pi / length * (bin_ids[:, None] * lag_ids[None, :] % length)
    cosine, sine = np.cos(angles), np.sin(angles)
    weight = (bin_ids / (FIRST + band_bins))[:, None]
    real = np.stack([cosine, sine, -weight * sine, weight * cosine])
    imag = np.stack([sine, -cosine, weight * cosine, weight * sine])
    own = np.stack([real, real], axis=2).reshape(4, 2 * band_bins, lags)
    partner = np.stack([-imag, imag], axis=2).reshape(4, 2 * band_bins, lags)
    both = np.concatenate([own, partner], axis=1)
    return np.swapaxes(both, 1, 2).reshape(4 * lags, 4 * band_bins).astype(np.float32)


def split_array(values):
    high = values.astype(jnp.bfloat16)
    low = (values - high.astype(jnp.float32)).astype(jnp.bfloat16)
    return high, low


def swap_pairs(values):
    rows = values.shape[0]
    parity = lax.broadcasted_iota(jnp.int32, values.shape, 0) % 2
    return jnp.where(
        parity == 0, pltpu.roll(values, rows - 1, 0), pltpu.roll(values, 1, 0)
    )


def filter_lanes(kept_bins, slots, slice_ref, filters_ref, lag_ref):
    _, components, _ = filters_ref.shape
    lanes = lag_ref.shape[1]
    rows = lanes // 2
    flat = jnp.concatenate([filters_ref[:, part] for part in range(components)], axis=1)
    total = jnp.dot(
        flat, lag_ref[...], precision=lax.Precision.HIGHEST, preferred_element_type=jnp.float32
    )
    lane_ids = lax.broadcasted_iota(jnp.int32, (1, lanes), 1) % rows
    group = lane_ids // (2 * slots)
    slot = lane_ids // 2 % slots
    count = jnp.zeros((1, lanes), jnp.int32)
    devices = rows // (2 * slots)
    for device in range(devices):
        count = jnp.where(group == devices - 1 - device, slice_ref[device], count)
    return total * jnp.where(slot < count, math.sqrt(2.0 / kept_bins), 0.0)


def spectrum_kernel(chunk, gathers_ref, table_ref, out_ref, held, table, sems):
    length = gathers_ref.shape[1]
    rows = table_ref.shape[0] // 2
    copies = []
    for step in range(length // chunk):
        part = pl.ds(step * chunk, chunk)
        copies.append(
            (
                pltpu.make_async_copy(gathers_ref.at[:, part], held.at[:, part], sems.at[0, step]),
                pltpu.make_async_copy(table_ref.at[:, part], table.at[:, part], sems.at[1, step]),
            )
        )
    for pair in copies:
        for copy in pair:
            copy.start()
    dot = functools.partial(
        lax.dot_general,
        dimension_numbers=(((1,), (1,)), ((), ())),
        preferred_element_type=jnp.float32,
    )
    total = jnp.zeros((rows, held.shape[0]), jnp.float32)
    for step, pair in enumerate(copies):
        for copy in pair:
            copy.wait()
        part = pl.ds(step * chunk, chunk)
        high, low = split_array(held[:, part])
        weights = table[:, part]
        both = dot(weights, high)
        total = total + both[:rows] + (both[rows:] + dot(weights[:rows], low))
    out_ref[...] = total.astype(jnp.bfloat16).astype(out_ref.dtype).reshape(out_ref.shape)


def predict_kernel(
    kept_bins,
    tile_ref,
    slice_ref,
    filters_ref,
    lag_ref,
    incoming_ref,
    operator_ref,
    out_ref,
    coefficient_ref,
    holder,
):
    devices, group_rows, traces = incoming_ref.shape
    slots, _, receivers, _ = operator_ref.shape
    per_shot = receivers // traces
    shots = devices // per_shot
    rows = shots * group_rows
    for k in range(devices):
        holder[tile_ref[k]] = devices - 1 - k
    columns = []
    for q in range(per_shot):
        parts = [
            incoming_ref[holder[s * per_shot + q]].astype(jnp.float32) for s in range(shots)
        ]
        columns.append(jnp.concatenate(parts, axis=0))
    spectrum = jnp.concatenate(columns, axis=1)
    row_ids = lax.broadcasted_iota(jnp.int32, (rows, receivers), 0)
    partner = swap_pairs(spectrum)
    partner = jnp.where(row_ids % 2 == 0, -partner, partner)
    flat = [spectrum.astype(jnp.bfloat16), partner.astype(jnp.bfloat16)]
    turned = [jnp.transpose(side).astype(jnp.bfloat16) for side in (spectrum, partner)]
    block_ids = lax.broadcasted_iota(jnp.int32, (rows, SPAN), 0)
    blocks = []
    for first in range(0, receivers, SPAN):
        where = pl.ds(first, SPAN)
        block = jnp.zeros((rows, SPAN), jnp.float32)
        for slot in range(slots):
            real, imag = operator_ref[slot, 0, where], operator_ref[slot, 1, where]
            if slot % 2:
                product = jnp.dot(real, turned[0], preferred_element_type=jnp.float32)
                product += jnp.dot(imag, turned[1], preferred_element_type=jnp.float32)
                product = jnp.transpose(product)
            else:
                dot = functools.partial(
                    lax.dot_general,
                    dimension_numbers=(((1,), (1,)), ((), ())),
                    preferred_element_type=jnp.float32,
                )
                product = dot(flat[0], real) + dot(flat[1], imag)
            block = jnp.where(block_ids // 2 % slots == slot, product, block)
        blocks.append(block)
    predicted = jnp.concatenate(blocks, axis=1)
    lane_ids = lax.broadcasted_iota(jnp.int32, (rows, receivers), 1) % traces
    edge = jnp.zeros((rows, traces), jnp.float32)
    after = jnp.concatenate([predicted[:, traces:], edge], axis=1)
    before = jnp.concatenate([edge, predicted[:, :-traces]], axis=1)
    halo = jnp.where(lane_ids < REACH, after, jnp.where(lane_ids >= traces - REACH, before, 0.0))
    for s in range(shots):
        for q in range(per_shot):
            where = (slice(s * group_rows, (s + 1) * group_rows), slice(q * traces, (q + 1) * traces))
            both = jnp.concatenate([predicted[where], halo[where]], axis=0)
            out_ref[holder[s * per_shot + q]] = both.astype(jnp.bfloat16)
    coefficient_ref[...] = filter_lanes(kept_bins, slots, slice_ref, filters_ref, lag_ref)


def subtract_kernel(
    chunk, returned_ref, coefficient_ref, table_ref, gathers_ref, out_ref, spread, result, sems
):
    devices, group_rows, _ = returned_ref.shape
    group_rows = group_rows // 2
    rows = devices * group_rows
    traces, length = gathers_ref.shape
    offsets = coefficient_ref.shape[0]
    came = returned_ref[...].astype(jnp.float32)
    own = came[:, :group_rows].reshape(rows, traces)
    edges = came[:, group_rows:].reshape(rows, traces)
    halo = jnp.transpose(jnp.concatenate([edges, swap_pairs(edges)], axis=0))
    spread[0:8] = halo[traces - 8 :]
    spread[8 : 8 + traces] = jnp.transpose(jnp.concatenate([own, swap_pairs(own)], axis=0))
    spread[8 + traces : 16 + traces] = halo[:8]
    total = jnp.zeros((traces, 2 * rows), jnp.float32)
    for offset in range(offsets):
        first = 8 + offset - offsets // 2
        total = total + spread[first : first + traces] * coefficient_ref[offset : offset + 1]
    total = total + pltpu.roll(total, rows, 1)
    high = total.astype(jnp.bfloat16).astype(jnp.float32)
    lane_ids = lax.broadcasted_iota(jnp.int32, total.shape, 1)
    mixed = jnp.where(lane_ids < rows, high, total - high)
    stacked = jnp.concatenate([mixed, high[:, :rows]], axis=1).astype(jnp.bfloat16)
    copies = []
    for step in range(length // chunk):
        part = pl.ds(step * chunk, chunk)
        response = jnp.dot(stacked, table_ref[:, part], preferred_element_type=jnp.float32)
        result[:, part] = gathers_ref[:, part] - response
        copy = pltpu.make_async_copy(result.at[:, part], out_ref.at[:, part], sems.at[step])
        copy.start()
        copies.append(copy)
    for copy in copies:
        copy.wait()


def vmem_spec():
    return pl.BlockSpec(memory_space=pltpu.VMEM)


def smem_spec():
    return pl.BlockSpec(memory_space=pltpu.SMEM)


def hbm_spec():
    return pl.BlockSpec(memory_space=pltpu.HBM)


def in_hbm(values):
    return pltpu.with_memory_space_constraint(values, pltpu.HBM)


def exchange(chunks):
    order = list(range(chunks.shape[0]))[::-1]
    return lax.all_to_all(chunks, "freq", 0, 0, axis_index_groups=[order], tiled=True)


def local(gathers, operator, filters, tile_of, slice_len):
    devices = lax.axis_size("freq")
    traces, length = gathers.shape
    slots, _, receivers, _ = operator.shape
    band_bins = slots * devices
    rows = 2 * band_bins
    group_rows = 2 * slots
    kept_bins = 5 * devices // 4
    offsets, lags = filters.shape[2], filters.shape[3]
    chunk = length
    params = pltpu.CompilerParams(vmem_limit_bytes=VMEM_LIMIT)
    table = row_tables(band_bins, slots, length)
    forward_table = np.concatenate(split_halves(table / math.sqrt(length)), axis=0)
    back_high, back_low = split_halves(table)
    back_table = np.concatenate([back_high, back_high, back_low], axis=0)
    tables = lag_tables(band_bins, slots, lags, length)
    with jax.named_scope("spectrum"):
        outgoing = pl.pallas_call(
            functools.partial(spectrum_kernel, chunk),
            out_shape=jax.ShapeDtypeStruct((devices, group_rows, traces), jnp.float32),
            in_specs=[hbm_spec()] * 2,
            out_specs=vmem_spec(),
            scratch_shapes=[
                pltpu.VMEM((traces, length), jnp.float32),
                pltpu.VMEM((2 * rows, length), jnp.bfloat16),
                pltpu.SemaphoreType.DMA((2, length // chunk)),
            ],
            compiler_params=params,
            cost_estimate=pl.CostEstimate(flops=COST[0], bytes_accessed=COST[1], transcendentals=0),
            name="spectrum",
        )(in_hbm(gathers), in_hbm(jnp.asarray(forward_table)))
    incoming = exchange(outgoing)
    with jax.named_scope("predict"):
        sending, coefficients = pl.pallas_call(
            functools.partial(predict_kernel, kept_bins),
            out_shape=[
                jax.ShapeDtypeStruct((devices, 2 * group_rows, traces), jnp.bfloat16),
                jax.ShapeDtypeStruct((offsets, 2 * rows), jnp.float32),
            ],
            in_specs=[smem_spec()] * 2 + [vmem_spec()] * 4,
            out_specs=[vmem_spec()] * 2,
            scratch_shapes=[pltpu.SMEM((devices,), jnp.int32)],
            compiler_params=params,
            name="predict",
        )(
            tile_of,
            slice_len,
            jnp.transpose(filters[0], (1, 0, 2)),
            jnp.asarray(tables),
            incoming,
            operator,
        )
    returned = exchange(sending)
    with jax.named_scope("subtract"):
        return pl.pallas_call(
            functools.partial(subtract_kernel, length // 4),
            out_shape=jax.ShapeDtypeStruct((traces, length), jnp.float32),
            in_specs=[vmem_spec()] * 4,
            out_specs=hbm_spec(),
            scratch_shapes=[
                pltpu.VMEM((traces + 16, 2 * rows), jnp.float32),
                pltpu.VMEM((traces, length), jnp.float32),
                pltpu.SemaphoreType.DMA((4,)),
            ],
            compiler_params=params,
            name="subtract",
        )(returned, coefficients, jnp.asarray(back_table), gathers)


def solution(mesh):
    placed = (
        P(("survey", "freq"), None),
        P(("survey", "freq"), None, None, None),
        P(("survey", "freq"), None, None, None),
        P("survey"),
        P("survey"),
    )
    return jax.shard_map(
        local, mesh=mesh, in_specs=placed, out_specs=P(("survey", "freq"), None), check_vma=False
    )
```

```python
import functools
import math

import jax
import jax.numpy as jnp
import ml_dtypes
import numpy as np
from jax import lax
from jax.experimental import pallas as pl
from jax.experimental.pallas import tpu as pltpu
from jax.sharding import PartitionSpec as P

FIRST = 40
REACH = 4
SPAN = 256
COST = (10**11, 40_000_000)
VMEM_LIMIT = 32 * 1024 * 1024


def split_halves(values):
    values = values.astype(np.float32)
    high = values.astype(ml_dtypes.bfloat16)
    low = (values - high.astype(np.float32)).astype(ml_dtypes.bfloat16)
    return high, low


def bins_in_order(band_bins, slots):
    return FIRST + np.arange(band_bins).reshape(-1, slots)[::-1].reshape(-1)


def row_tables(band_bins, slots, length):
    bin_ids = bins_in_order(band_bins, slots)
    angles = 2.0 * np.pi / length * (bin_ids[:, None] * np.arange(length)[None, :] % length)
    return np.stack([np.cos(angles), -np.sin(angles)], axis=1).reshape(2 * band_bins, length)


def lag_tables(band_bins, slots, lags, length):
    bin_ids = bins_in_order(band_bins, slots)
    lag_ids = np.arange(lags) - lags // 2
    angles = 2.0 * np.pi / length * (bin_ids[:, None] * lag_ids[None, :] % length)
    cosine, sine = np.cos(angles), np.sin(angles)
    weight = (bin_ids / (FIRST + band_bins))[:, None]
    real = np.stack([cosine, sine, -weight * sine, weight * cosine])
    imag = np.stack([sine, -cosine, weight * cosine, weight * sine])
    own = np.stack([real, real], axis=2).reshape(4, 2 * band_bins, lags)
    partner = np.stack([-imag, imag], axis=2).reshape(4, 2 * band_bins, lags)
    both = np.concatenate([own, partner], axis=1)
    return np.swapaxes(both, 1, 2).reshape(4 * lags, 4 * band_bins).astype(np.float32)


def split_array(values):
    high = values.astype(jnp.bfloat16)
    low = (values - high.astype(jnp.float32)).astype(jnp.bfloat16)
    return high, low


def swap_pairs(values):
    rows = values.shape[0]
    parity = lax.broadcasted_iota(jnp.int32, values.shape, 0) % 2
    return jnp.where(
        parity == 0, pltpu.roll(values, rows - 1, 0), pltpu.roll(values, 1, 0)
    )


def filter_lanes(kept_bins, slots, slice_ref, filters_ref, lag_ref):
    _, components, _ = filters_ref.shape
    lanes = lag_ref.shape[1]
    rows = lanes // 2
    flat = jnp.concatenate([filters_ref[:, part] for part in range(components)], axis=1)
    total = jnp.dot(
        flat, lag_ref[...], precision=lax.Precision.HIGHEST, preferred_element_type=jnp.float32
    )
    lane_ids = lax.broadcasted_iota(jnp.int32, (1, lanes), 1) % rows
    group = lane_ids // (2 * slots)
    slot = lane_ids // 2 % slots
    count = jnp.zeros((1, lanes), jnp.int32)
    devices = rows // (2 * slots)
    for device in range(devices):
        count = jnp.where(group == devices - 1 - device, slice_ref[device], count)
    return total * jnp.where(slot < count, math.sqrt(2.0 / kept_bins), 0.0)


def spectrum_kernel(chunk, gathers_ref, table_ref, out_ref, held, table, sems):
    length = gathers_ref.shape[1]
    rows = table_ref.shape[0] // 2
    copies = [
        pltpu.make_async_copy(gathers_ref, held, sems.at[0]),
        pltpu.make_async_copy(table_ref, table, sems.at[1]),
    ]
    for copy in copies:
        copy.start()
    for copy in copies:
        copy.wait()
    dot = functools.partial(
        lax.dot_general,
        dimension_numbers=(((1,), (1,)), ((), ())),
        preferred_element_type=jnp.float32,
    )

    def add(step, total):
        part = pl.ds(pl.multiple_of(step * chunk, chunk), chunk)
        high, low = split_array(held[:, part])
        weights = table[:, part]
        both = dot(weights, high)
        return total + both[:rows] + (both[rows:] + dot(weights[:rows], low))

    total = lax.fori_loop(
        0, length // chunk, add, jnp.zeros((rows, held.shape[0]), jnp.float32)
    )
    out_ref[...] = total.astype(jnp.bfloat16).astype(out_ref.dtype).reshape(out_ref.shape)


def predict_kernel(
    kept_bins,
    tile_ref,
    slice_ref,
    filters_ref,
    lag_ref,
    incoming_ref,
    operator_ref,
    out_ref,
    coefficient_ref,
    holder,
    blocks,
):
    devices, group_rows, traces = incoming_ref.shape
    slots, _, receivers, _ = operator_ref.shape
    per_shot = receivers // traces
    shots = devices // per_shot
    rows = shots * group_rows
    for k in range(devices):
        holder[tile_ref[k]] = devices - 1 - k
    columns = []
    for q in range(per_shot):
        parts = [
            incoming_ref[holder[s * per_shot + q]].astype(jnp.float32) for s in range(shots)
        ]
        columns.append(jnp.concatenate(parts, axis=0))
    spectrum = jnp.concatenate(columns, axis=1).astype(jnp.bfloat16)
    row_ids = lax.broadcasted_iota(jnp.int32, (rows, SPAN), 0)
    dot = functools.partial(
        lax.dot_general,
        dimension_numbers=(((1,), (1,)), ((), ())),
        preferred_element_type=jnp.float32,
    )

    @pl.loop(0, receivers // SPAN)
    def _(index):
        where = pl.ds(pl.multiple_of(index * SPAN, SPAN), SPAN)
        block = jnp.zeros((rows, SPAN), jnp.float32)
        for slot in range(slots):
            by_real = dot(spectrum, operator_ref[slot, 0, where])
            by_imag = swap_pairs(dot(spectrum, operator_ref[slot, 1, where]))
            product = jnp.where(row_ids % 2 == 0, by_real - by_imag, by_real + by_imag)
            block = jnp.where(row_ids // 2 % slots == slot, product, block)
        blocks[index] = block

    predicted = jnp.concatenate([blocks[i] for i in range(receivers // SPAN)], axis=1)
    lane_ids = lax.broadcasted_iota(jnp.int32, (rows, receivers), 1) % traces
    edge = jnp.zeros((rows, traces), jnp.float32)
    after = jnp.concatenate([predicted[:, traces:], edge], axis=1)
    before = jnp.concatenate([edge, predicted[:, :-traces]], axis=1)
    halo = jnp.where(lane_ids < REACH, after, jnp.where(lane_ids >= traces - REACH, before, 0.0))
    for s in range(shots):
        for q in range(per_shot):
            where = (slice(s * group_rows, (s + 1) * group_rows), slice(q * traces, (q + 1) * traces))
            both = jnp.concatenate([predicted[where], halo[where]], axis=0)
            out_ref[holder[s * per_shot + q]] = both.astype(jnp.bfloat16)
    coefficient_ref[...] = filter_lanes(kept_bins, slots, slice_ref, filters_ref, lag_ref)


def subtract_kernel(
    chunk, returned_ref, coefficient_ref, table_ref, gathers_ref, out_ref, spread, result, sems
):
    devices, group_rows, _ = returned_ref.shape
    group_rows = group_rows // 2
    rows = devices * group_rows
    traces, length = gathers_ref.shape
    offsets = coefficient_ref.shape[0]
    came = returned_ref[...].astype(jnp.float32)
    own = came[:, :group_rows].reshape(rows, traces)
    edges = came[:, group_rows:].reshape(rows, traces)
    halo = jnp.transpose(jnp.concatenate([edges, swap_pairs(edges)], axis=0))
    spread[0:8] = halo[traces - 8 :]
    spread[8 : 8 + traces] = jnp.transpose(jnp.concatenate([own, swap_pairs(own)], axis=0))
    spread[8 + traces : 16 + traces] = halo[:8]
    total = jnp.zeros((traces, 2 * rows), jnp.float32)
    for offset in range(offsets):
        first = 8 + offset - offsets // 2
        total = total + spread[first : first + traces] * coefficient_ref[offset : offset + 1]
    total = total + pltpu.roll(total, rows, 1)
    high = total.astype(jnp.bfloat16).astype(jnp.float32)
    lane_ids = lax.broadcasted_iota(jnp.int32, total.shape, 1)
    mixed = jnp.where(lane_ids < rows, high, total - high)
    stacked = jnp.concatenate([mixed, high[:, :rows]], axis=1).astype(jnp.bfloat16)

    def copy_out(step):
        part = pl.ds(pl.multiple_of(step * chunk, chunk), chunk)
        return pltpu.make_async_copy(result.at[:, part], out_ref.at[:, part], sems.at[step])

    @pl.loop(0, length // chunk)
    def _(step):
        part = pl.ds(pl.multiple_of(step * chunk, chunk), chunk)
        response = jnp.dot(stacked, table_ref[:, part], preferred_element_type=jnp.float32)
        result[:, part] = gathers_ref[:, part] - response
        copy_out(step).start()

    for step in range(length // chunk):
        copy_out(step).wait()


def vmem_spec():
    return pl.BlockSpec(memory_space=pltpu.VMEM)


def smem_spec():
    return pl.BlockSpec(memory_space=pltpu.SMEM)


def hbm_spec():
    return pl.BlockSpec(memory_space=pltpu.HBM)


def in_hbm(values):
    return pltpu.with_memory_space_constraint(values, pltpu.HBM)


def exchange(chunks):
    order = list(range(chunks.shape[0]))[::-1]
    return lax.all_to_all(chunks, "freq", 0, 0, axis_index_groups=[order], tiled=True)


def local(gathers, operator, filters, tile_of, slice_len):
    devices = lax.axis_size("freq")
    traces, length = gathers.shape
    slots, _, receivers, _ = operator.shape
    band_bins = slots * devices
    rows = 2 * band_bins
    group_rows = 2 * slots
    kept_bins = 5 * devices // 4
    offsets, lags = filters.shape[2], filters.shape[3]
    chunk = length // 4
    params = pltpu.CompilerParams(vmem_limit_bytes=VMEM_LIMIT)
    table = row_tables(band_bins, slots, length)
    forward_table = np.concatenate(split_halves(table / math.sqrt(length)), axis=0)
    back_high, back_low = split_halves(table)
    back_table = np.concatenate([back_high, back_high, back_low], axis=0)
    tables = lag_tables(band_bins, slots, lags, length)
    with jax.named_scope("spectrum"):
        outgoing = pl.pallas_call(
            functools.partial(spectrum_kernel, chunk),
            out_shape=jax.ShapeDtypeStruct((devices, group_rows, traces), jnp.float32),
            in_specs=[hbm_spec()] * 2,
            out_specs=vmem_spec(),
            scratch_shapes=[
                pltpu.VMEM((traces, length), jnp.float32),
                pltpu.VMEM((2 * rows, length), jnp.bfloat16),
                pltpu.SemaphoreType.DMA((2,)),
            ],
            compiler_params=params,
            cost_estimate=pl.CostEstimate(flops=COST[0], bytes_accessed=COST[1], transcendentals=0),
            name="spectrum",
        )(in_hbm(gathers), in_hbm(jnp.asarray(forward_table)))
    incoming = exchange(outgoing)
    with jax.named_scope("predict"):
        sending, coefficients = pl.pallas_call(
            functools.partial(predict_kernel, kept_bins),
            out_shape=[
                jax.ShapeDtypeStruct((devices, 2 * group_rows, traces), jnp.bfloat16),
                jax.ShapeDtypeStruct((offsets, 2 * rows), jnp.float32),
            ],
            in_specs=[smem_spec()] * 2 + [vmem_spec()] * 4,
            out_specs=[vmem_spec()] * 2,
            scratch_shapes=[
                pltpu.SMEM((devices,), jnp.int32),
                pltpu.VMEM(
                    (receivers // SPAN, devices * traces // receivers * group_rows, SPAN), jnp.float32
                ),
            ],
            compiler_params=params,
            name="predict",
        )(
            tile_of,
            slice_len,
            jnp.transpose(filters[0], (1, 0, 2)),
            jnp.asarray(tables),
            incoming,
            operator,
        )
    returned = exchange(sending)
    with jax.named_scope("subtract"):
        return pl.pallas_call(
            functools.partial(subtract_kernel, length // 4),
            out_shape=jax.ShapeDtypeStruct((traces, length), jnp.float32),
            in_specs=[vmem_spec()] * 4,
            out_specs=hbm_spec(),
            scratch_shapes=[
                pltpu.VMEM((traces + 16, 2 * rows), jnp.float32),
                pltpu.VMEM((traces, length), jnp.float32),
                pltpu.SemaphoreType.DMA((4,)),
            ],
            compiler_params=params,
            name="subtract",
        )(returned, coefficients, jnp.asarray(back_table), gathers)


def solution(mesh):
    placed = (
        P(("survey", "freq"), None),
        P(("survey", "freq"), None, None, None),
        P(("survey", "freq"), None, None, None),
        P("survey"),
        P("survey"),
    )
    return jax.shard_map(
        local, mesh=mesh, in_specs=placed, out_specs=P(("survey", "freq"), None), check_vma=False
    )
```

```python
import functools
import math

import jax
import jax.numpy as jnp
import ml_dtypes
import numpy as np
from jax import lax
from jax.experimental import pallas as pl
from jax.experimental.pallas import tpu as pltpu
from jax.sharding import PartitionSpec as P

FIRST = 40
REACH = 4
COST = (10**11, 40_000_000)
VMEM_LIMIT = 32 * 1024 * 1024


def split_halves(values):
    values = values.astype(np.float32)
    high = values.astype(ml_dtypes.bfloat16)
    low = (values - high.astype(np.float32)).astype(ml_dtypes.bfloat16)
    return high, low


def bins_by_parity(devices, slots):
    groups = FIRST + np.arange(devices * slots).reshape(devices, slots)[::-1]
    return np.stack([groups[:, groups[0] % 2 == parity].reshape(-1) for parity in range(2)])


def half_tables(bin_ids, length):
    angles = 2.0 * np.pi / length * (bin_ids[:, None] * np.arange(length // 2)[None, :] % length)
    return np.stack([np.cos(angles), -np.sin(angles)], axis=1).reshape(-1, length // 2)


def lag_tables(bin_ids, lags, length):
    band_bins = len(bin_ids)
    lag_ids = np.arange(lags) - lags // 2
    angles = 2.0 * np.pi / length * (bin_ids[:, None] * lag_ids[None, :] % length)
    cosine, sine = np.cos(angles), np.sin(angles)
    weight = (bin_ids / (FIRST + band_bins))[:, None]
    real = np.stack([cosine, sine, -weight * sine, weight * cosine])
    imag = np.stack([sine, -cosine, weight * cosine, weight * sine])
    own = np.stack([real, real], axis=2).reshape(4, 2 * band_bins, lags)
    partner = np.stack([-imag, imag], axis=2).reshape(4, 2 * band_bins, lags)
    both = np.concatenate([own, partner], axis=1)
    return np.swapaxes(both, 1, 2).reshape(4 * lags, 4 * band_bins).astype(np.float32)


def split_array(values):
    high = values.astype(jnp.bfloat16)
    low = (values - high.astype(jnp.float32)).astype(jnp.bfloat16)
    return high, low


def swap_pairs(values):
    rows = values.shape[0]
    parity = lax.broadcasted_iota(jnp.int32, values.shape, 0) % 2
    return jnp.where(
        parity == 0, pltpu.roll(values, rows - 1, 0), pltpu.roll(values, 1, 0)
    )


def filter_lanes(kept_bins, slots, slice_ref, filters_ref, lag_ref):
    _, components, _ = filters_ref.shape
    lanes = lag_ref.shape[1]
    rows = lanes // 2
    flat = jnp.concatenate([filters_ref[:, part] for part in range(components)], axis=1)
    total = jnp.dot(
        flat, lag_ref[...], precision=lax.Precision.HIGHEST, preferred_element_type=jnp.float32
    )
    lane_ids = lax.broadcasted_iota(jnp.int32, (1, lanes), 1) % rows
    parity = lane_ids // (rows // 2)
    place = lane_ids % (rows // 2)
    group = place // slots
    slot = place % slots // 2 * 2 + (parity + FIRST) % 2
    count = jnp.zeros((1, lanes), jnp.int32)
    devices = rows // (2 * slots)
    for device in range(devices):
        count = jnp.where(group == devices - 1 - device, slice_ref[device], count)
    return total * jnp.where(slot < count, math.sqrt(2.0 / kept_bins), 0.0)


def spectrum_kernel(gathers_ref, table_ref, out_ref, held, table, sems):
    traces, length = gathers_ref.shape
    rows = table_ref.shape[0] // 2
    devices, group_rows, _ = out_ref.shape
    copies = [
        pltpu.make_async_copy(gathers_ref, held, sems.at[0]),
        pltpu.make_async_copy(table_ref, table, sems.at[1]),
    ]
    for copy in copies:
        copy.start()
    for copy in copies:
        copy.wait()
    dot = functools.partial(
        lax.dot_general,
        dimension_numbers=(((1,), (1,)), ((), ())),
        preferred_element_type=jnp.float32,
    )
    early, late = held[:, : length // 2], held[:, length // 2 :]
    pieces = []
    for parity, folded in enumerate((early + late, early - late)):
        high, low = split_array(folded)
        weights = table[parity * rows : (parity + 1) * rows]
        both = dot(weights, high)
        total = both[: rows // 2] + (both[rows // 2 :] + dot(weights[: rows // 2], low))
        total = total.astype(jnp.bfloat16).astype(out_ref.dtype)
        pieces.append(total.reshape(devices, group_rows // 2, traces))
    out_ref[...] = jnp.concatenate(pieces, axis=1)


def place_of(slot, slots):
    return (slot + FIRST) % 2 * (slots // 2) + slot // 2


def predict_kernel(
    kept_bins,
    tile_ref,
    slice_ref,
    filters_ref,
    lag_ref,
    incoming_ref,
    operator_ref,
    out_ref,
    coefficient_ref,
    holder,
):
    devices, group_rows, traces = incoming_ref.shape
    slots, _, receivers, _ = operator_ref.shape
    per_shot = receivers // traces
    shots = devices // per_shot
    rows = shots * group_rows
    for k in range(devices):
        holder[tile_ref[k]] = devices - 1 - k
    columns = []
    for q in range(per_shot):
        parts = [
            incoming_ref[holder[s * per_shot + q]].astype(jnp.float32) for s in range(shots)
        ]
        columns.append(jnp.concatenate(parts, axis=0))
    spectrum = jnp.concatenate(columns, axis=1).astype(jnp.bfloat16)
    row_ids = lax.broadcasted_iota(jnp.int32, (rows, receivers), 0)
    dot = functools.partial(
        lax.dot_general,
        dimension_numbers=(((1,), (1,)), ((), ())),
        preferred_element_type=jnp.float32,
    )
    predicted = jnp.zeros((rows, receivers), jnp.float32)
    for slot in range(slots):
        by_real = dot(spectrum, operator_ref[slot, 0])
        by_imag = swap_pairs(dot(spectrum, operator_ref[slot, 1]))
        product = jnp.where(row_ids % 2 == 0, by_real - by_imag, by_real + by_imag)
        predicted = jnp.where(row_ids // 2 % slots == place_of(slot, slots), product, predicted)
    lane_ids = lax.broadcasted_iota(jnp.int32, (rows, receivers), 1) % traces
    edge = jnp.zeros((rows, traces), jnp.float32)
    after = jnp.concatenate([predicted[:, traces:], edge], axis=1)
    before = jnp.concatenate([edge, predicted[:, :-traces]], axis=1)
    halo = jnp.where(lane_ids < REACH, after, jnp.where(lane_ids >= traces - REACH, before, 0.0))
    for s in range(shots):
        for q in range(per_shot):
            where = (slice(s * group_rows, (s + 1) * group_rows), slice(q * traces, (q + 1) * traces))
            both = jnp.concatenate([predicted[where], halo[where]], axis=0)
            out_ref[holder[s * per_shot + q]] = both.astype(jnp.bfloat16)
    coefficient_ref[...] = filter_lanes(kept_bins, slots, slice_ref, filters_ref, lag_ref)


def subtract_kernel(
    chunk, returned_ref, coefficient_ref, table_ref, gathers_ref, out_ref, spread, result, sems
):
    devices, group_rows, _ = returned_ref.shape
    group_rows = group_rows // 2
    rows = devices * group_rows
    traces, length = gathers_ref.shape
    offsets = coefficient_ref.shape[0]
    came = returned_ref[...].astype(jnp.float32)

    def by_parity(first):
        middle, last = first + group_rows // 2, first + group_rows
        parts = (came[:, first:middle], came[:, middle:last])
        return jnp.concatenate([part.reshape(rows // 2, traces) for part in parts], axis=0)

    own, edges = by_parity(0), by_parity(group_rows)
    halo = jnp.transpose(jnp.concatenate([edges, swap_pairs(edges)], axis=0))
    spread[0:8] = halo[traces - 8 :]
    spread[8 : 8 + traces] = jnp.transpose(jnp.concatenate([own, swap_pairs(own)], axis=0))
    spread[8 + traces : 16 + traces] = halo[:8]
    total = jnp.zeros((traces, 2 * rows), jnp.float32)
    for offset in range(offsets):
        first = 8 + offset - offsets // 2
        total = total + spread[first : first + traces] * coefficient_ref[offset : offset + 1]
    total = total + pltpu.roll(total, rows, 1)
    high = total.astype(jnp.bfloat16).astype(jnp.float32)
    low = pltpu.roll(total - high, rows // 2, 1)
    block = lax.broadcasted_iota(jnp.int32, total.shape, 1) // (rows // 2)
    even = jnp.where(block == 1, low, high).astype(jnp.bfloat16)
    odd = jnp.where(block == 2, low, high).astype(jnp.bfloat16)
    copies = []
    for step in range(length // 2 // chunk):
        part = pl.ds(step * chunk, chunk)
        even_part = jnp.dot(even, table_ref[0, :, part], preferred_element_type=jnp.float32)
        odd_part = jnp.dot(odd, table_ref[1, :, part], preferred_element_type=jnp.float32)
        for later, response in enumerate((even_part + odd_part, even_part - odd_part)):
            where = pl.ds(later * (length // 2) + step * chunk, chunk)
            result[:, where] = gathers_ref[:, where] - response
            copy = pltpu.make_async_copy(
                result.at[:, where], out_ref.at[:, where], sems.at[2 * step + later]
            )
            copy.start()
            copies.append(copy)
    for copy in copies:
        copy.wait()


def vmem_spec():
    return pl.BlockSpec(memory_space=pltpu.VMEM)


def smem_spec():
    return pl.BlockSpec(memory_space=pltpu.SMEM)


def hbm_spec():
    return pl.BlockSpec(memory_space=pltpu.HBM)


def in_hbm(values):
    return pltpu.with_memory_space_constraint(values, pltpu.HBM)


def exchange(chunks):
    order = list(range(chunks.shape[0]))[::-1]
    return lax.all_to_all(chunks, "freq", 0, 0, axis_index_groups=[order], tiled=True)


def local(gathers, operator, filters, tile_of, slice_len):
    devices = lax.axis_size("freq")
    traces, length = gathers.shape
    slots, _, receivers, _ = operator.shape
    band_bins = slots * devices
    rows = 2 * band_bins
    group_rows = 2 * slots
    kept_bins = 5 * devices // 4
    offsets, lags = filters.shape[2], filters.shape[3]
    chunk = length // 4
    params = pltpu.CompilerParams(vmem_limit_bytes=VMEM_LIMIT)
    bins = bins_by_parity(devices, slots)
    halves = [half_tables(ids, length) for ids in bins]
    forward_table = np.concatenate([
        half for table in halves for half in split_halves(table / math.sqrt(length))
    ])
    blank = np.zeros((rows // 2, length // 2), ml_dtypes.bfloat16)
    (even_high, even_low), (odd_high, odd_low) = [split_halves(table) for table in halves]
    back_table = np.stack([
        np.concatenate([even_high, even_high, even_low, blank]),
        np.concatenate([blank, odd_high, odd_high, odd_low]),
    ])
    tables = lag_tables(bins.reshape(-1), lags, length)
    with jax.named_scope("spectrum"):
        outgoing = pl.pallas_call(
            spectrum_kernel,
            out_shape=jax.ShapeDtypeStruct((devices, group_rows, traces), jnp.float32),
            in_specs=[hbm_spec()] * 2,
            out_specs=vmem_spec(),
            scratch_shapes=[
                pltpu.VMEM((traces, length), jnp.float32),
                pltpu.VMEM((2 * rows, length // 2), jnp.bfloat16),
                pltpu.SemaphoreType.DMA((2,)),
            ],
            compiler_params=params,
            cost_estimate=pl.CostEstimate(flops=COST[0], bytes_accessed=COST[1], transcendentals=0),
            name="spectrum",
        )(in_hbm(gathers), in_hbm(jnp.asarray(forward_table)))
    incoming = exchange(outgoing)
    with jax.named_scope("predict"):
        sending, coefficients = pl.pallas_call(
            functools.partial(predict_kernel, kept_bins),
            out_shape=[
                jax.ShapeDtypeStruct((devices, 2 * group_rows, traces), jnp.bfloat16),
                jax.ShapeDtypeStruct((offsets, 2 * rows), jnp.float32),
            ],
            in_specs=[smem_spec()] * 2 + [vmem_spec()] * 4,
            out_specs=[vmem_spec()] * 2,
            scratch_shapes=[pltpu.SMEM((devices,), jnp.int32)],
            compiler_params=params,
            name="predict",
        )(
            tile_of,
            slice_len,
            jnp.transpose(filters[0], (1, 0, 2)),
            jnp.asarray(tables),
            incoming,
            operator,
        )
    returned = exchange(sending)
    with jax.named_scope("subtract"):
        return pl.pallas_call(
            functools.partial(subtract_kernel, chunk),
            out_shape=jax.ShapeDtypeStruct((traces, length), jnp.float32),
            in_specs=[vmem_spec()] * 4,
            out_specs=hbm_spec(),
            scratch_shapes=[
                pltpu.VMEM((traces + 16, 2 * rows), jnp.float32),
                pltpu.VMEM((traces, length), jnp.float32),
                pltpu.SemaphoreType.DMA((4,)),
            ],
            compiler_params=params,
            name="subtract",
        )(returned, coefficients, jnp.asarray(back_table), gathers)


def solution(mesh):
    placed = (
        P(("survey", "freq"), None),
        P(("survey", "freq"), None, None, None),
        P(("survey", "freq"), None, None, None),
        P("survey"),
        P("survey"),
    )
    return jax.shard_map(
        local, mesh=mesh, in_specs=placed, out_specs=P(("survey", "freq"), None), check_vma=False
    )
```

```python
import functools
import math

import jax
import jax.numpy as jnp
import ml_dtypes
import numpy as np
from jax import lax
from jax.experimental import pallas as pl
from jax.experimental.pallas import tpu as pltpu
from jax.sharding import PartitionSpec as P

FIRST = 40
REACH = 4
COST = (10**11, 40_000_000)
VMEM_LIMIT = 32 * 1024 * 1024


def split_halves(values):
    values = values.astype(np.float32)
    high = values.astype(ml_dtypes.bfloat16)
    low = (values - high.astype(np.float32)).astype(ml_dtypes.bfloat16)
    return high, low


def group_order(root, devices):
    return [root] + [device for device in range(devices)[::-1] if device != root]


def order_out(devices):
    return group_order(3 * devices // 4 - 1, devices)


def order_back(devices):
    return group_order(3 * devices // 4 - 1, devices)


def bins_in_order(order, slots):
    return (FIRST + np.array(order)[:, None] * slots + np.arange(slots)).reshape(-1)


def row_tables(bin_ids, length):
    band_bins = len(bin_ids)
    angles = 2.0 * np.pi / length * (bin_ids[:, None] * np.arange(length)[None, :] % length)
    return np.stack([np.cos(angles), -np.sin(angles)], axis=1).reshape(2 * band_bins, length)


def lag_tables(bin_ids, lags, length):
    band_bins = len(bin_ids)
    lag_ids = np.arange(lags) - lags // 2
    angles = 2.0 * np.pi / length * (bin_ids[:, None] * lag_ids[None, :] % length)
    cosine, sine = np.cos(angles), np.sin(angles)
    weight = (bin_ids / (FIRST + band_bins))[:, None]
    real = np.stack([cosine, sine, -weight * sine, weight * cosine])
    imag = np.stack([sine, -cosine, weight * cosine, weight * sine])
    own = np.stack([real, real], axis=2).reshape(4, 2 * band_bins, lags)
    partner = np.stack([-imag, imag], axis=2).reshape(4, 2 * band_bins, lags)
    both = np.concatenate([own, partner], axis=1)
    return np.swapaxes(both, 1, 2).reshape(4 * lags, 4 * band_bins).astype(np.float32)


def split_array(values):
    high = values.astype(jnp.bfloat16)
    low = (values - high.astype(jnp.float32)).astype(jnp.bfloat16)
    return high, low


def swap_pairs(values):
    rows = values.shape[0]
    parity = lax.broadcasted_iota(jnp.int32, values.shape, 0) % 2
    return jnp.where(
        parity == 0, pltpu.roll(values, rows - 1, 0), pltpu.roll(values, 1, 0)
    )


def filter_lanes(kept_bins, slots, slice_ref, filters_ref, lag_ref):
    _, components, _ = filters_ref.shape
    lanes = lag_ref.shape[1]
    rows = lanes // 2
    flat = jnp.concatenate([filters_ref[:, part] for part in range(components)], axis=1)
    total = jnp.dot(
        flat, lag_ref[...], precision=lax.Precision.HIGHEST, preferred_element_type=jnp.float32
    )
    lane_ids = lax.broadcasted_iota(jnp.int32, (1, lanes), 1) % rows
    group = lane_ids // (2 * slots)
    slot = lane_ids // 2 % slots
    count = jnp.zeros((1, lanes), jnp.int32)
    devices = rows // (2 * slots)
    for place, device in enumerate(order_back(devices)):
        count = jnp.where(group == place, slice_ref[device], count)
    return total * jnp.where(slot < count, math.sqrt(2.0 / kept_bins), 0.0)


def spectrum_kernel(chunk, gathers_ref, table_ref, out_ref, held, table, sems):
    length = gathers_ref.shape[1]
    rows = table_ref.shape[0] // 2
    copies = []
    for step in range(length // chunk):
        part = pl.ds(step * chunk, chunk)
        copies.append(
            (
                pltpu.make_async_copy(gathers_ref.at[:, part], held.at[:, part], sems.at[0, step]),
                pltpu.make_async_copy(table_ref.at[:, part], table.at[:, part], sems.at[1, step]),
            )
        )
    for pair in copies:
        for copy in pair:
            copy.start()
    dot = functools.partial(
        lax.dot_general,
        dimension_numbers=(((1,), (1,)), ((), ())),
        preferred_element_type=jnp.float32,
    )
    total = jnp.zeros((rows, held.shape[0]), jnp.float32)
    for step, pair in enumerate(copies):
        for copy in pair:
            copy.wait()
        part = pl.ds(step * chunk, chunk)
        high, low = split_array(held[:, part])
        weights = table[:, part]
        both = dot(weights, high)
        total = total + both[:rows] + (both[rows:] + dot(weights[:rows], low))
    out_ref[...] = total.astype(jnp.bfloat16).astype(out_ref.dtype).reshape(out_ref.shape)


def predict_kernel(
    kept_bins,
    tile_ref,
    slice_ref,
    filters_ref,
    lag_ref,
    incoming_ref,
    operator_ref,
    out_ref,
    coefficient_ref,
    holder,
):
    devices, group_rows, traces = incoming_ref.shape
    slots, _, receivers, _ = operator_ref.shape
    per_shot = receivers // traces
    shots = devices // per_shot
    rows = shots * group_rows
    for place, device in enumerate(order_out(devices)):
        holder[0, tile_ref[device]] = place
    for place, device in enumerate(order_back(devices)):
        holder[1, tile_ref[device]] = place
    columns = []
    for q in range(per_shot):
        parts = [
            incoming_ref[holder[0, s * per_shot + q]].astype(jnp.float32) for s in range(shots)
        ]
        columns.append(jnp.concatenate(parts, axis=0))
    spectrum = jnp.concatenate(columns, axis=1).astype(jnp.bfloat16)
    row_ids = lax.broadcasted_iota(jnp.int32, (rows, receivers), 0)
    dot = functools.partial(
        lax.dot_general,
        dimension_numbers=(((1,), (1,)), ((), ())),
        preferred_element_type=jnp.float32,
    )
    predicted = jnp.zeros((rows, receivers), jnp.float32)
    for slot in range(slots):
        by_real = dot(spectrum, operator_ref[slot, 0])
        by_imag = swap_pairs(dot(spectrum, operator_ref[slot, 1]))
        product = jnp.where(row_ids % 2 == 0, by_real - by_imag, by_real + by_imag)
        predicted = jnp.where(row_ids // 2 % slots == slot, product, predicted)
    lane_ids = lax.broadcasted_iota(jnp.int32, (rows, receivers), 1) % traces
    edge = jnp.zeros((rows, traces), jnp.float32)
    after = jnp.concatenate([predicted[:, traces:], edge], axis=1)
    before = jnp.concatenate([edge, predicted[:, :-traces]], axis=1)
    halo = jnp.where(lane_ids < REACH, after, jnp.where(lane_ids >= traces - REACH, before, 0.0))
    for s in range(shots):
        for q in range(per_shot):
            where = (slice(s * group_rows, (s + 1) * group_rows), slice(q * traces, (q + 1) * traces))
            both = jnp.concatenate([predicted[where], halo[where]], axis=0)
            out_ref[holder[1, s * per_shot + q]] = both.astype(jnp.bfloat16)
    coefficient_ref[...] = filter_lanes(kept_bins, slots, slice_ref, filters_ref, lag_ref)


def subtract_kernel(
    chunk, returned_ref, coefficient_ref, table_ref, gathers_ref, out_ref, spread, result, sems
):
    devices, group_rows, _ = returned_ref.shape
    group_rows = group_rows // 2
    rows = devices * group_rows
    traces, length = gathers_ref.shape
    offsets = coefficient_ref.shape[0]
    came = returned_ref[...].astype(jnp.float32)
    own = came[:, :group_rows].reshape(rows, traces)
    edges = came[:, group_rows:].reshape(rows, traces)
    halo = jnp.transpose(jnp.concatenate([edges, swap_pairs(edges)], axis=0))
    spread[0:8] = halo[traces - 8 :]
    spread[8 : 8 + traces] = jnp.transpose(jnp.concatenate([own, swap_pairs(own)], axis=0))
    spread[8 + traces : 16 + traces] = halo[:8]
    total = jnp.zeros((traces, 2 * rows), jnp.float32)
    for offset in range(offsets):
        first = 8 + offset - offsets // 2
        total = total + spread[first : first + traces] * coefficient_ref[offset : offset + 1]
    total = total + pltpu.roll(total, rows, 1)
    high = total.astype(jnp.bfloat16).astype(jnp.float32)
    lane_ids = lax.broadcasted_iota(jnp.int32, total.shape, 1)
    mixed = jnp.where(lane_ids < rows, high, total - high)
    stacked = jnp.concatenate([mixed, high[:, :rows]], axis=1).astype(jnp.bfloat16)
    copies = []
    for step in range(length // chunk):
        part = pl.ds(step * chunk, chunk)
        response = jnp.dot(stacked, table_ref[:, part], preferred_element_type=jnp.float32)
        result[:, part] = gathers_ref[:, part] - response
        copy = pltpu.make_async_copy(result.at[:, part], out_ref.at[:, part], sems.at[step])
        copy.start()
        copies.append(copy)
    for copy in copies:
        copy.wait()


def vmem_spec():
    return pl.BlockSpec(memory_space=pltpu.VMEM)


def smem_spec():
    return pl.BlockSpec(memory_space=pltpu.SMEM)


def hbm_spec():
    return pl.BlockSpec(memory_space=pltpu.HBM)


def in_hbm(values):
    return pltpu.with_memory_space_constraint(values, pltpu.HBM)


def exchange(chunks, order):
    return lax.all_to_all(chunks, "freq", 0, 0, axis_index_groups=[order], tiled=True)


def local(gathers, operator, filters, tile_of, slice_len):
    devices = lax.axis_size("freq")
    traces, length = gathers.shape
    slots, _, receivers, _ = operator.shape
    band_bins = slots * devices
    rows = 2 * band_bins
    group_rows = 2 * slots
    kept_bins = 5 * devices // 4
    offsets, lags = filters.shape[2], filters.shape[3]
    chunk = length
    params = pltpu.CompilerParams(vmem_limit_bytes=VMEM_LIMIT)
    bins_out = bins_in_order(order_out(devices), slots)
    bins_back = bins_in_order(order_back(devices), slots)
    forward = row_tables(bins_out, length) / math.sqrt(length)
    forward_table = np.concatenate(split_halves(forward), axis=0)
    back_high, back_low = split_halves(row_tables(bins_back, length))
    back_table = np.concatenate([back_high, back_high, back_low], axis=0)
    tables = lag_tables(bins_back, lags, length)
    with jax.named_scope("spectrum"):
        outgoing = pl.pallas_call(
            functools.partial(spectrum_kernel, chunk),
            out_shape=jax.ShapeDtypeStruct((devices, group_rows, traces), jnp.float32),
            in_specs=[hbm_spec()] * 2,
            out_specs=vmem_spec(),
            scratch_shapes=[
                pltpu.VMEM((traces, length), jnp.float32),
                pltpu.VMEM((2 * rows, length), jnp.bfloat16),
                pltpu.SemaphoreType.DMA((2, length // chunk)),
            ],
            compiler_params=params,
            cost_estimate=pl.CostEstimate(flops=COST[0], bytes_accessed=COST[1], transcendentals=0),
            name="spectrum",
        )(in_hbm(gathers), in_hbm(jnp.asarray(forward_table)))
    incoming = exchange(outgoing, order_out(devices))
    with jax.named_scope("predict"):
        sending, coefficients = pl.pallas_call(
            functools.partial(predict_kernel, kept_bins),
            out_shape=[
                jax.ShapeDtypeStruct((devices, 2 * group_rows, traces), jnp.bfloat16),
                jax.ShapeDtypeStruct((offsets, 2 * rows), jnp.float32),
            ],
            in_specs=[smem_spec()] * 2 + [vmem_spec()] * 4,
            out_specs=[vmem_spec()] * 2,
            scratch_shapes=[pltpu.SMEM((2, devices), jnp.int32)],
            compiler_params=params,
            name="predict",
        )(
            tile_of,
            slice_len,
            jnp.transpose(filters[0], (1, 0, 2)),
            jnp.asarray(tables),
            incoming,
            operator,
        )
    returned = exchange(sending, order_back(devices))
    with jax.named_scope("subtract"):
        return pl.pallas_call(
            functools.partial(subtract_kernel, length // 4),
            out_shape=jax.ShapeDtypeStruct((traces, length), jnp.float32),
            in_specs=[vmem_spec()] * 4,
            out_specs=hbm_spec(),
            scratch_shapes=[
                pltpu.VMEM((traces + 16, 2 * rows), jnp.float32),
                pltpu.VMEM((traces, length), jnp.float32),
                pltpu.SemaphoreType.DMA((4,)),
            ],
            compiler_params=params,
            name="subtract",
        )(returned, coefficients, jnp.asarray(back_table), gathers)


def solution(mesh):
    placed = (
        P(("survey", "freq"), None),
        P(("survey", "freq"), None, None, None),
        P(("survey", "freq"), None, None, None),
        P("survey"),
        P("survey"),
    )
    return jax.shard_map(
        local, mesh=mesh, in_specs=placed, out_specs=P(("survey", "freq"), None), check_vma=False
    )
```

```python
import functools
import math

import jax
import jax.numpy as jnp
import ml_dtypes
import numpy as np
from jax import lax
from jax.experimental import pallas as pl
from jax.experimental.pallas import tpu as pltpu
from jax.sharding import PartitionSpec as P

FIRST = 40
REACH = 4
COST = (10**11, 40_000_000)
VMEM_LIMIT = 32 * 1024 * 1024


def split_halves(values):
    values = values.astype(np.float32)
    high = values.astype(ml_dtypes.bfloat16)
    low = (values - high.astype(np.float32)).astype(ml_dtypes.bfloat16)
    return high, low


def group_order(root, devices):
    return [root] + [device for device in range(devices)[::-1] if device != root]


def order_out(devices):
    return group_order(3 * devices // 4 - 1, devices)


def order_back(devices):
    return group_order(3 * devices // 4 - 1, devices)


def bins_in_order(order, slots):
    return (FIRST + np.array(order)[:, None] * slots + np.arange(slots)).reshape(-1)


def row_tables(bin_ids, length):
    band_bins = len(bin_ids)
    angles = 2.0 * np.pi / length * (bin_ids[:, None] * np.arange(length)[None, :] % length)
    return np.stack([np.cos(angles), -np.sin(angles)], axis=1).reshape(2 * band_bins, length)


def lag_tables(bin_ids, lags, length):
    band_bins = len(bin_ids)
    lag_ids = np.arange(lags) - lags // 2
    angles = 2.0 * np.pi / length * (bin_ids[:, None] * lag_ids[None, :] % length)
    cosine, sine = np.cos(angles), np.sin(angles)
    weight = (bin_ids / (FIRST + band_bins))[:, None]
    real = np.stack([cosine, sine, -weight * sine, weight * cosine])
    imag = np.stack([sine, -cosine, weight * cosine, weight * sine])
    own = np.stack([real, real], axis=2).reshape(4, 2 * band_bins, lags)
    partner = np.stack([-imag, imag], axis=2).reshape(4, 2 * band_bins, lags)
    both = np.concatenate([own, partner], axis=1)
    return np.swapaxes(both, 1, 2).reshape(4 * lags, 4 * band_bins).astype(np.float32)


def split_array(values):
    high = values.astype(jnp.bfloat16)
    low = (values - high.astype(jnp.float32)).astype(jnp.bfloat16)
    return high, low


def swap_pairs(values):
    rows = values.shape[0]
    parity = lax.broadcasted_iota(jnp.int32, values.shape, 0) % 2
    return jnp.where(
        parity == 0, pltpu.roll(values, rows - 1, 0), pltpu.roll(values, 1, 0)
    )


def filter_lanes(kept_bins, slots, slice_ref, filters_ref, lag_ref):
    _, components, _ = filters_ref.shape
    lanes = lag_ref.shape[1]
    rows = lanes // 2
    flat = jnp.concatenate([filters_ref[:, part] for part in range(components)], axis=1)
    total = jnp.dot(
        flat, lag_ref[...], precision=lax.Precision.HIGHEST, preferred_element_type=jnp.float32
    )
    lane_ids = lax.broadcasted_iota(jnp.int32, (1, lanes), 1) % rows
    group = lane_ids // (2 * slots)
    slot = lane_ids // 2 % slots
    count = jnp.zeros((1, lanes), jnp.int32)
    devices = rows // (2 * slots)
    for place, device in enumerate(order_back(devices)):
        count = jnp.where(group == place, slice_ref[device], count)
    return total * jnp.where(slot < count, math.sqrt(2.0 / kept_bins), 0.0)


def spectrum_kernel(chunk, gathers_ref, table_ref, out_ref, held, table, sems):
    length = gathers_ref.shape[1]
    rows = table_ref.shape[0] // 2
    copies = []
    for step in range(length // chunk):
        part = pl.ds(step * chunk, chunk)
        copies.append(
            (
                pltpu.make_async_copy(gathers_ref.at[:, part], held.at[:, part], sems.at[0, step]),
                pltpu.make_async_copy(table_ref.at[:, part], table.at[:, part], sems.at[1, step]),
            )
        )
    for pair in copies:
        for copy in pair:
            copy.start()
    dot = functools.partial(
        lax.dot_general,
        dimension_numbers=(((1,), (1,)), ((), ())),
        preferred_element_type=jnp.float32,
    )
    total = jnp.zeros((rows, held.shape[0]), jnp.float32)
    for step, pair in enumerate(copies):
        for copy in pair:
            copy.wait()
        part = pl.ds(step * chunk, chunk)
        high, low = split_array(held[:, part])
        weights = table[:, part]
        both = dot(weights, high)
        total = total + both[:rows] + (both[rows:] + dot(weights[:rows], low))
    out_ref[...] = total.astype(jnp.bfloat16).astype(out_ref.dtype).reshape(out_ref.shape)


def predict_kernel(
    kept_bins,
    tile_ref,
    slice_ref,
    filters_ref,
    lag_ref,
    incoming_ref,
    operator_ref,
    out_ref,
    coefficient_ref,
    holder,
):
    devices, group_rows, traces = incoming_ref.shape
    slots, receivers = operator_ref.shape[0], 8 * operator_ref.shape[2]
    per_shot = receivers // traces
    shots = devices // per_shot
    rows = shots * group_rows
    for place, device in enumerate(order_out(devices)):
        holder[0, tile_ref[device]] = place
    for place, device in enumerate(order_back(devices)):
        holder[1, tile_ref[device]] = place
    columns = []
    for q in range(per_shot):
        parts = [
            incoming_ref[holder[0, s * per_shot + q]].astype(jnp.float32) for s in range(shots)
        ]
        columns.append(jnp.concatenate(parts, axis=0))
    spectrum = jnp.concatenate(columns, axis=1)
    row_ids = lax.broadcasted_iota(jnp.int32, (rows, receivers), 0)
    partner = swap_pairs(spectrum)
    partner = jnp.where(row_ids % 2 == 0, -partner, partner)
    column_ids = lax.broadcasted_iota(jnp.int32, (receivers // 2, 2 * rows), 1)
    turned = jnp.zeros((2 * receivers, 2 * rows), jnp.float32)
    for part, side in enumerate((spectrum, partner)):
        tiles = [side[:, i : i + traces] for i in range(0, receivers, traces)]
        pairs = [jnp.concatenate(tiles[half::2], axis=1) for half in range(2)]
        both = jnp.transpose(jnp.concatenate(pairs, axis=0))
        for slot in range(slots):
            weights = jnp.where(column_ids // 2 % slots == slot, both, 0.0).astype(jnp.bfloat16)
            streamed = jnp.concatenate(
                [
                    operator_ref[slot, part, :, p].reshape(2 * receivers, traces)
                    for p in range(receivers // (2 * traces))
                ],
                axis=1,
            )
            turned = turned + jnp.dot(streamed, weights, preferred_element_type=jnp.float32)
    halves = turned.reshape(receivers // 8, 2, 8, 2 * rows)
    first = halves[:, 0].reshape(receivers, 2 * rows)
    second = halves[:, 1].reshape(receivers, 2 * rows)
    predicted = jnp.transpose(first)[:rows] + jnp.transpose(second)[rows:]
    lane_ids = lax.broadcasted_iota(jnp.int32, (rows, receivers), 1) % traces
    edge = jnp.zeros((rows, traces), jnp.float32)
    after = jnp.concatenate([predicted[:, traces:], edge], axis=1)
    before = jnp.concatenate([edge, predicted[:, :-traces]], axis=1)
    halo = jnp.where(lane_ids < REACH, after, jnp.where(lane_ids >= traces - REACH, before, 0.0))
    for s in range(shots):
        for q in range(per_shot):
            where = (slice(s * group_rows, (s + 1) * group_rows), slice(q * traces, (q + 1) * traces))
            both = jnp.concatenate([predicted[where], halo[where]], axis=0)
            out_ref[holder[1, s * per_shot + q]] = both.astype(jnp.bfloat16)
    coefficient_ref[...] = filter_lanes(kept_bins, slots, slice_ref, filters_ref, lag_ref)


def subtract_kernel(
    chunk, returned_ref, coefficient_ref, table_ref, gathers_ref, out_ref, spread, result, sems
):
    devices, group_rows, _ = returned_ref.shape
    group_rows = group_rows // 2
    rows = devices * group_rows
    traces, length = gathers_ref.shape
    offsets = coefficient_ref.shape[0]
    came = returned_ref[...].astype(jnp.float32)
    own = came[:, :group_rows].reshape(rows, traces)
    edges = came[:, group_rows:].reshape(rows, traces)
    halo = jnp.transpose(jnp.concatenate([edges, swap_pairs(edges)], axis=0))
    spread[0:8] = halo[traces - 8 :]
    spread[8 : 8 + traces] = jnp.transpose(jnp.concatenate([own, swap_pairs(own)], axis=0))
    spread[8 + traces : 16 + traces] = halo[:8]
    total = jnp.zeros((traces, 2 * rows), jnp.float32)
    for offset in range(offsets):
        first = 8 + offset - offsets // 2
        total = total + spread[first : first + traces] * coefficient_ref[offset : offset + 1]
    total = total + pltpu.roll(total, rows, 1)
    high = total.astype(jnp.bfloat16).astype(jnp.float32)
    lane_ids = lax.broadcasted_iota(jnp.int32, total.shape, 1)
    mixed = jnp.where(lane_ids < rows, high, total - high)
    stacked = jnp.concatenate([mixed, high[:, :rows]], axis=1).astype(jnp.bfloat16)
    copies = []
    for step in range(length // chunk):
        part = pl.ds(step * chunk, chunk)
        response = jnp.dot(stacked, table_ref[:, part], preferred_element_type=jnp.float32)
        result[:, part] = gathers_ref[:, part] - response
        copy = pltpu.make_async_copy(result.at[:, part], out_ref.at[:, part], sems.at[step])
        copy.start()
        copies.append(copy)
    for copy in copies:
        copy.wait()


def vmem_spec():
    return pl.BlockSpec(memory_space=pltpu.VMEM)


def smem_spec():
    return pl.BlockSpec(memory_space=pltpu.SMEM)


def hbm_spec():
    return pl.BlockSpec(memory_space=pltpu.HBM)


def in_hbm(values):
    return pltpu.with_memory_space_constraint(values, pltpu.HBM)


def exchange(chunks, order):
    return lax.all_to_all(chunks, "freq", 0, 0, axis_index_groups=[order], tiled=True)


def local(gathers, operator, filters, tile_of, slice_len):
    devices = lax.axis_size("freq")
    traces, length = gathers.shape
    slots, _, receivers, _ = operator.shape
    band_bins = slots * devices
    rows = 2 * band_bins
    group_rows = 2 * slots
    kept_bins = 5 * devices // 4
    offsets, lags = filters.shape[2], filters.shape[3]
    chunk = length
    params = pltpu.CompilerParams(vmem_limit_bytes=VMEM_LIMIT)
    bins_out = bins_in_order(order_out(devices), slots)
    bins_back = bins_in_order(order_back(devices), slots)
    forward = row_tables(bins_out, length) / math.sqrt(length)
    forward_table = np.concatenate(split_halves(forward), axis=0)
    back_high, back_low = split_halves(row_tables(bins_back, length))
    back_table = np.concatenate([back_high, back_high, back_low], axis=0)
    tables = lag_tables(bins_back, lags, length)
    with jax.named_scope("spectrum"):
        outgoing = pl.pallas_call(
            functools.partial(spectrum_kernel, chunk),
            out_shape=jax.ShapeDtypeStruct((devices, group_rows, traces), jnp.float32),
            in_specs=[hbm_spec()] * 2,
            out_specs=vmem_spec(),
            scratch_shapes=[
                pltpu.VMEM((traces, length), jnp.float32),
                pltpu.VMEM((2 * rows, length), jnp.bfloat16),
                pltpu.SemaphoreType.DMA((2, length // chunk)),
            ],
            compiler_params=params,
            cost_estimate=pl.CostEstimate(flops=COST[0], bytes_accessed=COST[1], transcendentals=0),
            name="spectrum",
        )(in_hbm(gathers), in_hbm(jnp.asarray(forward_table)))
    incoming = exchange(outgoing, order_out(devices))
    stacked = operator.reshape(slots, 2, receivers // 8, 8, receivers // traces, traces)
    stacked = jnp.swapaxes(stacked, 3, 4).reshape(slots, 2, receivers // 8, -1, 16, traces)
    with jax.named_scope("predict"):
        sending, coefficients = pl.pallas_call(
            functools.partial(predict_kernel, kept_bins),
            out_shape=[
                jax.ShapeDtypeStruct((devices, 2 * group_rows, traces), jnp.bfloat16),
                jax.ShapeDtypeStruct((offsets, 2 * rows), jnp.float32),
            ],
            in_specs=[smem_spec()] * 2 + [vmem_spec()] * 4,
            out_specs=[vmem_spec()] * 2,
            scratch_shapes=[pltpu.SMEM((2, devices), jnp.int32)],
            compiler_params=params,
            name="predict",
        )(
            tile_of,
            slice_len,
            jnp.transpose(filters[0], (1, 0, 2)),
            jnp.asarray(tables),
            incoming,
            stacked,
        )
    returned = exchange(sending, order_back(devices))
    with jax.named_scope("subtract"):
        return pl.pallas_call(
            functools.partial(subtract_kernel, length // 4),
            out_shape=jax.ShapeDtypeStruct((traces, length), jnp.float32),
            in_specs=[vmem_spec()] * 4,
            out_specs=hbm_spec(),
            scratch_shapes=[
                pltpu.VMEM((traces + 16, 2 * rows), jnp.float32),
                pltpu.VMEM((traces, length), jnp.float32),
                pltpu.SemaphoreType.DMA((4,)),
            ],
            compiler_params=params,
            name="subtract",
        )(returned, coefficients, jnp.asarray(back_table), gathers)


def solution(mesh):
    placed = (
        P(("survey", "freq"), None),
        P(("survey", "freq"), None, None, None),
        P(("survey", "freq"), None, None, None),
        P("survey"),
        P("survey"),
    )
    return jax.shard_map(
        local, mesh=mesh, in_specs=placed, out_specs=P(("survey", "freq"), None), check_vma=False
    )
```

```python
import functools
import math

import jax
import jax.numpy as jnp
import ml_dtypes
import numpy as np
from jax import lax
from jax.experimental import pallas as pl
from jax.experimental.pallas import tpu as pltpu
from jax.sharding import PartitionSpec as P

FIRST = 40
REACH = 4
COST = (10**11, 40_000_000)
VMEM_LIMIT = 32 * 1024 * 1024


def split_halves(values):
    values = values.astype(np.float32)
    high = values.astype(ml_dtypes.bfloat16)
    low = (values - high.astype(np.float32)).astype(ml_dtypes.bfloat16)
    return high, low


def group_order(root, devices):
    return [root] + [device for device in range(devices)[::-1] if device != root]


def order_out(devices):
    return group_order(3 * devices // 4 - 1, devices)


def order_back(devices):
    return group_order(3 * devices // 4 - 1, devices)


def bins_in_order(order, slots):
    return (FIRST + np.array(order)[:, None] * slots + np.arange(slots)).reshape(-1)


def row_tables(bin_ids, length):
    band_bins = len(bin_ids)
    angles = 2.0 * np.pi / length * (bin_ids[:, None] * np.arange(length)[None, :] % length)
    return np.stack([np.cos(angles), -np.sin(angles)], axis=1).reshape(2 * band_bins, length)


def lag_tables(bin_ids, lags, length):
    band_bins = len(bin_ids)
    lag_ids = np.arange(lags) - lags // 2
    angles = 2.0 * np.pi / length * (bin_ids[:, None] * lag_ids[None, :] % length)
    cosine, sine = np.cos(angles), np.sin(angles)
    weight = (bin_ids / (FIRST + band_bins))[:, None]
    real = np.stack([cosine, sine, -weight * sine, weight * cosine])
    imag = np.stack([sine, -cosine, weight * cosine, weight * sine])
    own = np.stack([real, real], axis=2).reshape(4, 2 * band_bins, lags)
    partner = np.stack([-imag, imag], axis=2).reshape(4, 2 * band_bins, lags)
    both = np.concatenate([own, partner], axis=1)
    return np.swapaxes(both, 1, 2).reshape(4 * lags, 4 * band_bins).astype(np.float32)


def split_array(values):
    high = values.astype(jnp.bfloat16)
    low = (values - high.astype(jnp.float32)).astype(jnp.bfloat16)
    return high, low


def swap_pairs(values):
    rows = values.shape[0]
    parity = lax.broadcasted_iota(jnp.int32, values.shape, 0) % 2
    return jnp.where(
        parity == 0, pltpu.roll(values, rows - 1, 0), pltpu.roll(values, 1, 0)
    )


def filter_lanes(kept_bins, slots, slice_ref, filters_ref, lag_ref):
    _, components, _ = filters_ref.shape
    lanes = lag_ref.shape[1]
    rows = lanes // 2
    flat = jnp.concatenate([filters_ref[:, part] for part in range(components)], axis=1)
    total = jnp.dot(
        flat, lag_ref[...], precision=lax.Precision.HIGHEST, preferred_element_type=jnp.float32
    )
    lane_ids = lax.broadcasted_iota(jnp.int32, (1, lanes), 1) % rows
    group = lane_ids // (2 * slots)
    slot = lane_ids // 2 % slots
    count = jnp.zeros((1, lanes), jnp.int32)
    devices = rows // (2 * slots)
    for place, device in enumerate(order_back(devices)):
        count = jnp.where(group == place, slice_ref[device], count)
    return total * jnp.where(slot < count, math.sqrt(2.0 / kept_bins), 0.0)


def spectrum_kernel(
    kept_bins,
    slots,
    slice_ref,
    filters_ref,
    lag_ref,
    gathers_ref,
    table_ref,
    out_ref,
    coefficient_ref,
    counts,
    filters,
    lags,
    held,
    table,
    sems,
):
    traces = gathers_ref.shape[0]
    rows = table_ref.shape[0] // 2
    parts = [pl.ds(0, traces // 2), pl.ds(traces // 2, traces // 2)]
    pairs = [(gathers_ref.at[part], held.at[part]) for part in parts]
    pairs += [(table_ref, table), (slice_ref, counts), (filters_ref, filters), (lag_ref, lags)]
    copies = [
        pltpu.make_async_copy(source, target, sems.at[i])
        for i, (source, target) in enumerate(pairs)
    ]
    for copy in copies:
        copy.start()
    for copy in copies[3:]:
        copy.wait()
    coefficient_ref[...] = filter_lanes(kept_bins, slots, counts, filters, lags)
    for copy in copies[:3]:
        copy.wait()
    dot = functools.partial(
        lax.dot_general,
        dimension_numbers=(((1,), (1,)), ((), ())),
        preferred_element_type=jnp.float32,
    )
    high, low = split_array(held[...])
    both = dot(table[...], high)
    total = both[:rows] + (both[rows:] + dot(table[:rows], low))
    out_ref[...] = total.astype(jnp.bfloat16).astype(out_ref.dtype).reshape(out_ref.shape)


def predict_kernel(tile_ref, incoming_ref, operator_ref, out_ref, holder):
    devices, group_rows, traces = incoming_ref.shape
    slots, _, receivers, _ = operator_ref.shape
    per_shot = receivers // traces
    shots = devices // per_shot
    rows = shots * group_rows
    for place, device in enumerate(order_out(devices)):
        holder[0, tile_ref[device]] = place
    for place, device in enumerate(order_back(devices)):
        holder[1, tile_ref[device]] = place
    columns = []
    for q in range(per_shot):
        parts = [
            incoming_ref[holder[0, s * per_shot + q]].astype(jnp.float32) for s in range(shots)
        ]
        columns.append(jnp.concatenate(parts, axis=0))
    spectrum = jnp.concatenate(columns, axis=1).astype(jnp.bfloat16)
    row_ids = lax.broadcasted_iota(jnp.int32, (rows, receivers), 0)
    dot = functools.partial(
        lax.dot_general,
        dimension_numbers=(((1,), (1,)), ((), ())),
        preferred_element_type=jnp.float32,
    )
    predicted = jnp.zeros((rows, receivers), jnp.float32)
    for slot in range(slots):
        by_real = dot(spectrum, operator_ref[slot, 0])
        by_imag = swap_pairs(dot(spectrum, operator_ref[slot, 1]))
        product = jnp.where(row_ids % 2 == 0, by_real - by_imag, by_real + by_imag)
        predicted = jnp.where(row_ids // 2 % slots == slot, product, predicted)
    lane_ids = lax.broadcasted_iota(jnp.int32, (rows, receivers), 1) % traces
    edge = jnp.zeros((rows, traces), jnp.float32)
    after = jnp.concatenate([predicted[:, traces:], edge], axis=1)
    before = jnp.concatenate([edge, predicted[:, :-traces]], axis=1)
    halo = jnp.where(lane_ids < REACH, after, jnp.where(lane_ids >= traces - REACH, before, 0.0))
    for s in range(shots):
        for q in range(per_shot):
            where = (slice(s * group_rows, (s + 1) * group_rows), slice(q * traces, (q + 1) * traces))
            both = jnp.concatenate([predicted[where], halo[where]], axis=0)
            out_ref[holder[1, s * per_shot + q]] = both.astype(jnp.bfloat16)


def subtract_kernel(
    chunk, returned_ref, coefficient_ref, table_ref, gathers_ref, out_ref, spread, result, sems
):
    devices, group_rows, _ = returned_ref.shape
    group_rows = group_rows // 2
    rows = devices * group_rows
    traces, length = gathers_ref.shape
    offsets = coefficient_ref.shape[0]
    came = returned_ref[...].astype(jnp.float32)
    own = came[:, :group_rows].reshape(rows, traces)
    edges = came[:, group_rows:].reshape(rows, traces)
    halo = jnp.transpose(jnp.concatenate([edges, swap_pairs(edges)], axis=0))
    spread[0:8] = halo[traces - 8 :]
    spread[8 : 8 + traces] = jnp.transpose(jnp.concatenate([own, swap_pairs(own)], axis=0))
    spread[8 + traces : 16 + traces] = halo[:8]
    total = jnp.zeros((traces, 2 * rows), jnp.float32)
    for offset in range(offsets):
        first = 8 + offset - offsets // 2
        total = total + spread[first : first + traces] * coefficient_ref[offset : offset + 1]
    total = total + pltpu.roll(total, rows, 1)
    high = total.astype(jnp.bfloat16).astype(jnp.float32)
    lane_ids = lax.broadcasted_iota(jnp.int32, total.shape, 1)
    mixed = jnp.where(lane_ids < rows, high, total - high)
    stacked = jnp.concatenate([mixed, high[:, :rows]], axis=1).astype(jnp.bfloat16)
    copies = []
    for step in range(length // chunk):
        part = pl.ds(step * chunk, chunk)
        response = jnp.dot(stacked, table_ref[:, part], preferred_element_type=jnp.float32)
        result[:, part] = gathers_ref[:, part] - response
        copy = pltpu.make_async_copy(result.at[:, part], out_ref.at[:, part], sems.at[step])
        copy.start()
        copies.append(copy)
    for copy in copies:
        copy.wait()


def vmem_spec():
    return pl.BlockSpec(memory_space=pltpu.VMEM)


def smem_spec():
    return pl.BlockSpec(memory_space=pltpu.SMEM)


def hbm_spec():
    return pl.BlockSpec(memory_space=pltpu.HBM)


def in_hbm(values):
    return pltpu.with_memory_space_constraint(values, pltpu.HBM)


def exchange(chunks, order):
    return lax.all_to_all(chunks, "freq", 0, 0, axis_index_groups=[order], tiled=True)


def local(gathers, operator, filters, tile_of, slice_len):
    devices = lax.axis_size("freq")
    traces, length = gathers.shape
    slots, _, receivers, _ = operator.shape
    band_bins = slots * devices
    rows = 2 * band_bins
    group_rows = 2 * slots
    kept_bins = 5 * devices // 4
    offsets, lags = filters.shape[2], filters.shape[3]
    params = pltpu.CompilerParams(vmem_limit_bytes=VMEM_LIMIT)
    bins_out = bins_in_order(order_out(devices), slots)
    bins_back = bins_in_order(order_back(devices), slots)
    forward = row_tables(bins_out, length) / math.sqrt(length)
    forward_table = np.concatenate(split_halves(forward), axis=0)
    back_high, back_low = split_halves(row_tables(bins_back, length))
    back_table = np.concatenate([back_high, back_high, back_low], axis=0)
    tables = lag_tables(bins_back, lags, length)
    with jax.named_scope("spectrum"):
        outgoing, coefficients = pl.pallas_call(
            functools.partial(spectrum_kernel, kept_bins, slots),
            out_shape=[
                jax.ShapeDtypeStruct((devices, group_rows, traces), jnp.float32),
                jax.ShapeDtypeStruct((offsets, 2 * rows), jnp.float32),
            ],
            in_specs=[hbm_spec()] * 5,
            out_specs=[vmem_spec()] * 2,
            scratch_shapes=[
                pltpu.SMEM(slice_len.shape, jnp.int32),
                pltpu.VMEM((offsets, filters.shape[1], lags), jnp.float32),
                pltpu.VMEM(tables.shape, jnp.float32),
                pltpu.VMEM((traces, length), jnp.float32),
                pltpu.VMEM((2 * rows, length), jnp.bfloat16),
                pltpu.SemaphoreType.DMA((6,)),
            ],
            compiler_params=params,
            cost_estimate=pl.CostEstimate(flops=COST[0], bytes_accessed=COST[1], transcendentals=0),
            name="spectrum",
        )(
            in_hbm(slice_len),
            in_hbm(jnp.transpose(filters[0], (1, 0, 2))),
            in_hbm(jnp.asarray(tables)),
            in_hbm(gathers),
            in_hbm(jnp.asarray(forward_table)),
        )
    incoming = exchange(outgoing, order_out(devices))
    with jax.named_scope("predict"):
        sending = pl.pallas_call(
            predict_kernel,
            out_shape=jax.ShapeDtypeStruct((devices, 2 * group_rows, traces), jnp.bfloat16),
            in_specs=[smem_spec(), vmem_spec(), vmem_spec()],
            out_specs=vmem_spec(),
            scratch_shapes=[pltpu.SMEM((2, devices), jnp.int32)],
            compiler_params=params,
            name="predict",
        )(tile_of, incoming, operator)
    returned = exchange(sending, order_back(devices))
    with jax.named_scope("subtract"):
        return pl.pallas_call(
            functools.partial(subtract_kernel, length // 4),
            out_shape=jax.ShapeDtypeStruct((traces, length), jnp.float32),
            in_specs=[vmem_spec()] * 4,
            out_specs=hbm_spec(),
            scratch_shapes=[
                pltpu.VMEM((traces + 16, 2 * rows), jnp.float32),
                pltpu.VMEM((traces, length), jnp.float32),
                pltpu.SemaphoreType.DMA((4,)),
            ],
            compiler_params=params,
            name="subtract",
        )(returned, coefficients, jnp.asarray(back_table), gathers)


def solution(mesh):
    placed = (
        P(("survey", "freq"), None),
        P(("survey", "freq"), None, None, None),
        P(("survey", "freq"), None, None, None),
        P("survey"),
        P("survey"),
    )
    return jax.shard_map(
        local, mesh=mesh, in_specs=placed, out_specs=P(("survey", "freq"), None), check_vma=False
    )
```

```python
import functools
import math

import jax
import jax.numpy as jnp
import ml_dtypes
import numpy as np
from jax import lax
from jax.experimental import pallas as pl
from jax.experimental.pallas import tpu as pltpu
from jax.sharding import PartitionSpec as P

FIRST = 40
REACH = 4
COST = (10**11, 40_000_000)
VMEM_LIMIT = 32 * 1024 * 1024


def split_halves(values):
    values = values.astype(np.float32)
    high = values.astype(ml_dtypes.bfloat16)
    low = (values - high.astype(np.float32)).astype(ml_dtypes.bfloat16)
    return high, low


def group_order(root, devices):
    return [root] + [device for device in range(devices)[::-1] if device != root]


def order_out(devices):
    return group_order(3 * devices // 4 - 1, devices)


def order_back(devices):
    return group_order(devices - 1, devices)


def bins_in_order(order, slots):
    return (FIRST + np.array(order)[:, None] * slots + np.arange(slots)).reshape(-1)


def row_tables(bin_ids, length):
    band_bins = len(bin_ids)
    angles = 2.0 * np.pi / length * (bin_ids[:, None] * np.arange(length)[None, :] % length)
    return np.stack([np.cos(angles), -np.sin(angles)], axis=1).reshape(2 * band_bins, length)


def lag_tables(bin_ids, lags, length):
    band_bins = len(bin_ids)
    lag_ids = np.arange(lags) - lags // 2
    angles = 2.0 * np.pi / length * (bin_ids[:, None] * lag_ids[None, :] % length)
    cosine, sine = np.cos(angles), np.sin(angles)
    weight = (bin_ids / (FIRST + band_bins))[:, None]
    real = np.stack([cosine, sine, -weight * sine, weight * cosine])
    imag = np.stack([sine, -cosine, weight * cosine, weight * sine])
    own = np.stack([real, real], axis=2).reshape(4, 2 * band_bins, lags)
    partner = np.stack([-imag, imag], axis=2).reshape(4, 2 * band_bins, lags)
    both = np.concatenate([own, partner], axis=1)
    return np.swapaxes(both, 1, 2).reshape(4 * lags, 4 * band_bins).astype(np.float32)


def split_array(values):
    high = values.astype(jnp.bfloat16)
    low = (values - high.astype(jnp.float32)).astype(jnp.bfloat16)
    return high, low


def swap_pairs(values):
    rows = values.shape[0]
    parity = lax.broadcasted_iota(jnp.int32, values.shape, 0) % 2
    return jnp.where(
        parity == 0, pltpu.roll(values, rows - 1, 0), pltpu.roll(values, 1, 0)
    )


def filter_lanes(kept_bins, slots, slice_ref, filters_ref, lag_ref):
    _, components, _ = filters_ref.shape
    lanes = lag_ref.shape[1]
    rows = lanes // 2
    flat = jnp.concatenate([filters_ref[:, part] for part in range(components)], axis=1)
    total = jnp.dot(
        flat, lag_ref[...], precision=lax.Precision.HIGHEST, preferred_element_type=jnp.float32
    )
    lane_ids = lax.broadcasted_iota(jnp.int32, (1, lanes), 1) % rows
    group = lane_ids // (2 * slots)
    slot = lane_ids // 2 % slots
    count = jnp.zeros((1, lanes), jnp.int32)
    devices = rows // (2 * slots)
    for place, device in enumerate(order_back(devices)):
        count = jnp.where(group == place, slice_ref[device], count)
    return total * jnp.where(slot < count, math.sqrt(2.0 / kept_bins), 0.0)


def spectrum_kernel(chunk, gathers_ref, table_ref, out_ref, held, table, sems):
    length = gathers_ref.shape[1]
    rows = table_ref.shape[0] // 2
    copies = []
    for step in range(length // chunk):
        part = pl.ds(step * chunk, chunk)
        copies.append(
            (
                pltpu.make_async_copy(gathers_ref.at[:, part], held.at[:, part], sems.at[0, step]),
                pltpu.make_async_copy(table_ref.at[:, part], table.at[:, part], sems.at[1, step]),
            )
        )
    for pair in copies:
        for copy in pair:
            copy.start()
    dot = functools.partial(
        lax.dot_general,
        dimension_numbers=(((1,), (1,)), ((), ())),
        preferred_element_type=jnp.float32,
    )
    total = jnp.zeros((rows, held.shape[0]), jnp.float32)
    for step, pair in enumerate(copies):
        for copy in pair:
            copy.wait()
        part = pl.ds(step * chunk, chunk)
        high, low = split_array(held[:, part])
        weights = table[:, part]
        both = dot(weights, high)
        total = total + both[:rows] + (both[rows:] + dot(weights[:rows], low))
    out_ref[...] = total.astype(jnp.bfloat16).astype(out_ref.dtype).reshape(out_ref.shape)


def predict_kernel(
    kept_bins,
    tile_ref,
    slice_ref,
    filters_ref,
    lag_ref,
    incoming_ref,
    operator_ref,
    out_ref,
    coefficient_ref,
    holder,
):
    devices, group_rows, traces = incoming_ref.shape
    slots, _, receivers, _ = operator_ref.shape
    per_shot = receivers // traces
    shots = devices // per_shot
    rows = shots * group_rows
    for place, device in enumerate(order_out(devices)):
        holder[0, tile_ref[device]] = place
    for place, device in enumerate(order_back(devices)):
        holder[1, tile_ref[device]] = place
    columns = []
    for q in range(per_shot):
        parts = [
            incoming_ref[holder[0, s * per_shot + q]].astype(jnp.float32) for s in range(shots)
        ]
        columns.append(jnp.concatenate(parts, axis=0))
    spectrum = jnp.concatenate(columns, axis=1).astype(jnp.bfloat16)
    row_ids = lax.broadcasted_iota(jnp.int32, (rows, receivers), 0)
    dot = functools.partial(
        lax.dot_general,
        dimension_numbers=(((1,), (1,)), ((), ())),
        preferred_element_type=jnp.float32,
    )
    predicted = jnp.zeros((rows, receivers), jnp.float32)
    for slot in range(slots):
        by_real = dot(spectrum, operator_ref[slot, 0])
        by_imag = swap_pairs(dot(spectrum, operator_ref[slot, 1]))
        product = jnp.where(row_ids % 2 == 0, by_real - by_imag, by_real + by_imag)
        predicted = jnp.where(row_ids // 2 % slots == slot, product, predicted)
    lane_ids = lax.broadcasted_iota(jnp.int32, (rows, receivers), 1) % traces
    edge = jnp.zeros((rows, traces), jnp.float32)
    after = jnp.concatenate([predicted[:, traces:], edge], axis=1)
    before = jnp.concatenate([edge, predicted[:, :-traces]], axis=1)
    halo = jnp.where(lane_ids < REACH, after, jnp.where(lane_ids >= traces - REACH, before, 0.0))
    for s in range(shots):
        for q in range(per_shot):
            where = (slice(s * group_rows, (s + 1) * group_rows), slice(q * traces, (q + 1) * traces))
            both = jnp.concatenate([predicted[where], halo[where]], axis=0)
            out_ref[holder[1, s * per_shot + q]] = both.astype(jnp.bfloat16)
    coefficient_ref[...] = filter_lanes(kept_bins, slots, slice_ref, filters_ref, lag_ref)


def subtract_kernel(
    chunk, returned_ref, coefficient_ref, table_ref, gathers_ref, out_ref, spread, result, sems
):
    devices, group_rows, _ = returned_ref.shape
    group_rows = group_rows // 2
    rows = devices * group_rows
    traces, length = gathers_ref.shape
    offsets = coefficient_ref.shape[0]
    came = returned_ref[...].astype(jnp.float32)
    own = came[:, :group_rows].reshape(rows, traces)
    edges = came[:, group_rows:].reshape(rows, traces)
    halo = jnp.transpose(jnp.concatenate([edges, swap_pairs(edges)], axis=0))
    spread[0:8] = halo[traces - 8 :]
    spread[8 : 8 + traces] = jnp.transpose(jnp.concatenate([own, swap_pairs(own)], axis=0))
    spread[8 + traces : 16 + traces] = halo[:8]
    total = jnp.zeros((traces, 2 * rows), jnp.float32)
    for offset in range(offsets):
        first = 8 + offset - offsets // 2
        total = total + spread[first : first + traces] * coefficient_ref[offset : offset + 1]
    total = total + pltpu.roll(total, rows, 1)
    high = total.astype(jnp.bfloat16).astype(jnp.float32)
    lane_ids = lax.broadcasted_iota(jnp.int32, total.shape, 1)
    mixed = jnp.where(lane_ids < rows, high, total - high)
    stacked = jnp.concatenate([mixed, high[:, :rows]], axis=1).astype(jnp.bfloat16)
    copies = []
    for step in range(length // chunk):
        part = pl.ds(step * chunk, chunk)
        response = jnp.dot(stacked, table_ref[:, part], preferred_element_type=jnp.float32)
        result[:, part] = gathers_ref[:, part] - response
        copy = pltpu.make_async_copy(result.at[:, part], out_ref.at[:, part], sems.at[step])
        copy.start()
        copies.append(copy)
    for copy in copies:
        copy.wait()


def vmem_spec():
    return pl.BlockSpec(memory_space=pltpu.VMEM)


def smem_spec():
    return pl.BlockSpec(memory_space=pltpu.SMEM)


def hbm_spec():
    return pl.BlockSpec(memory_space=pltpu.HBM)


def in_hbm(values):
    return pltpu.with_memory_space_constraint(values, pltpu.HBM)


def exchange(chunks, order):
    return lax.all_to_all(chunks, "freq", 0, 0, axis_index_groups=[order], tiled=True)


def local(gathers, operator, filters, tile_of, slice_len):
    devices = lax.axis_size("freq")
    traces, length = gathers.shape
    slots, _, receivers, _ = operator.shape
    band_bins = slots * devices
    rows = 2 * band_bins
    group_rows = 2 * slots
    kept_bins = 5 * devices // 4
    offsets, lags = filters.shape[2], filters.shape[3]
    chunk = length
    params = pltpu.CompilerParams(vmem_limit_bytes=VMEM_LIMIT)
    bins_out = bins_in_order(order_out(devices), slots)
    bins_back = bins_in_order(order_back(devices), slots)
    forward = row_tables(bins_out, length) / math.sqrt(length)
    forward_table = np.concatenate(split_halves(forward), axis=0)
    back_high, back_low = split_halves(row_tables(bins_back, length))
    back_table = np.concatenate([back_high, back_high, back_low], axis=0)
    tables = lag_tables(bins_back, lags, length)
    with jax.named_scope("spectrum"):
        outgoing = pl.pallas_call(
            functools.partial(spectrum_kernel, chunk),
            out_shape=jax.ShapeDtypeStruct((devices, group_rows, traces), jnp.float32),
            in_specs=[hbm_spec()] * 2,
            out_specs=vmem_spec(),
            scratch_shapes=[
                pltpu.VMEM((traces, length), jnp.float32),
                pltpu.VMEM((2 * rows, length), jnp.bfloat16),
                pltpu.SemaphoreType.DMA((2, length // chunk)),
            ],
            compiler_params=params,
            cost_estimate=pl.CostEstimate(flops=COST[0], bytes_accessed=COST[1], transcendentals=0),
            name="spectrum",
        )(in_hbm(gathers), in_hbm(jnp.asarray(forward_table)))
    incoming = exchange(outgoing, order_out(devices))
    with jax.named_scope("predict"):
        sending, coefficients = pl.pallas_call(
            functools.partial(predict_kernel, kept_bins),
            out_shape=[
                jax.ShapeDtypeStruct((devices, 2 * group_rows, traces), jnp.bfloat16),
                jax.ShapeDtypeStruct((offsets, 2 * rows), jnp.float32),
            ],
            in_specs=[smem_spec()] * 2 + [vmem_spec()] * 4,
            out_specs=[vmem_spec()] * 2,
            scratch_shapes=[pltpu.SMEM((2, devices), jnp.int32)],
            compiler_params=params,
            name="predict",
        )(
            tile_of,
            slice_len,
            jnp.transpose(filters[0], (1, 0, 2)),
            jnp.asarray(tables),
            incoming,
            operator,
        )
    returned = exchange(sending, order_back(devices))
    with jax.named_scope("subtract"):
        return pl.pallas_call(
            functools.partial(subtract_kernel, length // 4),
            out_shape=jax.ShapeDtypeStruct((traces, length), jnp.float32),
            in_specs=[vmem_spec()] * 4,
            out_specs=hbm_spec(),
            scratch_shapes=[
                pltpu.VMEM((traces + 16, 2 * rows), jnp.float32),
                pltpu.VMEM((traces, length), jnp.float32),
                pltpu.SemaphoreType.DMA((4,)),
            ],
            compiler_params=params,
            name="subtract",
        )(returned, coefficients, jnp.asarray(back_table), gathers)


def solution(mesh):
    placed = (
        P(("survey", "freq"), None),
        P(("survey", "freq"), None, None, None),
        P(("survey", "freq"), None, None, None),
        P("survey"),
        P("survey"),
    )
    return jax.shard_map(
        local, mesh=mesh, in_specs=placed, out_specs=P(("survey", "freq"), None), check_vma=False
    )
```

```python
import functools
import math

import jax
import jax.numpy as jnp
import ml_dtypes
import numpy as np
from jax import lax
from jax.experimental import pallas as pl
from jax.experimental.pallas import tpu as pltpu
from jax.sharding import PartitionSpec as P

FIRST = 40
REACH = 4
COST = (10**11, 40_000_000)
VMEM_LIMIT = 32 * 1024 * 1024


def split_halves(values):
    values = values.astype(np.float32)
    high = values.astype(ml_dtypes.bfloat16)
    low = (values - high.astype(np.float32)).astype(ml_dtypes.bfloat16)
    return high, low


def group_order(root, devices):
    return [root] + [device for device in range(devices)[::-1] if device != root]


def order_out(devices):
    return group_order(3 * devices // 4 - 1, devices)


def order_back(devices):
    return group_order(devices - 1, devices)


def bins_in_order(order, slots):
    return (FIRST + np.array(order)[:, None] * slots + np.arange(slots)).reshape(-1)


def row_tables(bin_ids, length):
    band_bins = len(bin_ids)
    angles = 2.0 * np.pi / length * (bin_ids[:, None] * np.arange(length)[None, :] % length)
    return np.stack([np.cos(angles), -np.sin(angles)], axis=1).reshape(2 * band_bins, length)


def lag_tables(bin_ids, lags, length):
    band_bins = len(bin_ids)
    lag_ids = np.arange(lags) - lags // 2
    angles = 2.0 * np.pi / length * (bin_ids[:, None] * lag_ids[None, :] % length)
    cosine, sine = np.cos(angles), np.sin(angles)
    weight = (bin_ids / (FIRST + band_bins))[:, None]
    real = np.stack([cosine, sine, -weight * sine, weight * cosine])
    imag = np.stack([sine, -cosine, weight * cosine, weight * sine])
    own = np.stack([real, real], axis=2).reshape(4, 2 * band_bins, lags)
    partner = np.stack([-imag, imag], axis=2).reshape(4, 2 * band_bins, lags)
    both = np.concatenate([own, partner], axis=1)
    return np.swapaxes(both, 1, 2).reshape(4 * lags, 4 * band_bins).astype(np.float32)


def split_array(values):
    high = values.astype(jnp.bfloat16)
    low = (values - high.astype(jnp.float32)).astype(jnp.bfloat16)
    return high, low


def swap_pairs(values):
    rows = values.shape[0]
    parity = lax.broadcasted_iota(jnp.int32, values.shape, 0) % 2
    return jnp.where(
        parity == 0, pltpu.roll(values, rows - 1, 0), pltpu.roll(values, 1, 0)
    )


def filter_lanes(kept_bins, slots, slice_ref, filters_ref, lag_ref):
    _, components, _ = filters_ref.shape
    lanes = lag_ref.shape[1]
    rows = lanes // 2
    flat = jnp.concatenate([filters_ref[:, part] for part in range(components)], axis=1)
    total = jnp.dot(
        flat, lag_ref[...], precision=lax.Precision.HIGHEST, preferred_element_type=jnp.float32
    )
    lane_ids = lax.broadcasted_iota(jnp.int32, (1, lanes), 1) % rows
    group = lane_ids // (2 * slots)
    slot = lane_ids // 2 % slots
    count = jnp.zeros((1, lanes), jnp.int32)
    devices = rows // (2 * slots)
    for place, device in enumerate(order_back(devices)):
        count = jnp.where(group == place, slice_ref[device], count)
    return total * jnp.where(slot < count, math.sqrt(2.0 / kept_bins), 0.0)


def spectrum_kernel(gathers_ref, table_ref, out_ref, held, table, sems):
    traces, length = gathers_ref.shape
    rows = table_ref.shape[0] // 2
    devices, group_rows, _ = out_ref.shape
    copies = [
        pltpu.make_async_copy(gathers_ref, held, sems.at[0]),
        pltpu.make_async_copy(table_ref, table, sems.at[1]),
    ]
    for copy in copies:
        copy.start()
    for copy in copies:
        copy.wait()
    dot = functools.partial(
        lax.dot_general,
        dimension_numbers=(((1,), (1,)), ((), ())),
        preferred_element_type=jnp.float32,
    )
    early, late = held[:, : length // 2], held[:, length // 2 :]
    pieces = []
    for parity, folded in enumerate((early + late, early - late)):
        high, low = split_array(folded)
        weights = table[parity * rows : (parity + 1) * rows]
        both = dot(weights, high)
        total = both[: rows // 2] + (both[rows // 2 :] + dot(weights[: rows // 2], low))
        total = total.astype(jnp.bfloat16).astype(out_ref.dtype)
        pieces.append(total.reshape(devices, group_rows // 2, traces))
    out_ref[...] = jnp.concatenate(pieces, axis=1)


def predict_kernel(
    kept_bins,
    tile_ref,
    slice_ref,
    filters_ref,
    lag_ref,
    incoming_ref,
    operator_ref,
    out_ref,
    coefficient_ref,
    holder,
):
    devices, group_rows, traces = incoming_ref.shape
    slots, _, receivers, _ = operator_ref.shape
    per_shot = receivers // traces
    shots = devices // per_shot
    rows = shots * group_rows
    for place, device in enumerate(order_out(devices)):
        holder[0, tile_ref[device]] = place
    for place, device in enumerate(order_back(devices)):
        holder[1, tile_ref[device]] = place
    columns = []
    for q in range(per_shot):
        parts = [
            incoming_ref[holder[0, s * per_shot + q]].astype(jnp.float32) for s in range(shots)
        ]
        columns.append(jnp.concatenate(parts, axis=0))
    spectrum = jnp.concatenate(columns, axis=1).astype(jnp.bfloat16)
    row_ids = lax.broadcasted_iota(jnp.int32, (rows, receivers), 0)
    dot = functools.partial(
        lax.dot_general,
        dimension_numbers=(((1,), (1,)), ((), ())),
        preferred_element_type=jnp.float32,
    )
    predicted = jnp.zeros((rows, receivers), jnp.float32)
    for slot in range(slots):
        by_real = dot(spectrum, operator_ref[slot, 0])
        by_imag = swap_pairs(dot(spectrum, operator_ref[slot, 1]))
        product = jnp.where(row_ids % 2 == 0, by_real - by_imag, by_real + by_imag)
        predicted = jnp.where(row_ids // 2 % slots == slot, product, predicted)
    lane_ids = lax.broadcasted_iota(jnp.int32, (rows, receivers), 1) % traces
    edge = jnp.zeros((rows, traces), jnp.float32)
    after = jnp.concatenate([predicted[:, traces:], edge], axis=1)
    before = jnp.concatenate([edge, predicted[:, :-traces]], axis=1)
    halo = jnp.where(lane_ids < REACH, after, jnp.where(lane_ids >= traces - REACH, before, 0.0))
    for s in range(shots):
        for q in range(per_shot):
            where = (slice(s * group_rows, (s + 1) * group_rows), slice(q * traces, (q + 1) * traces))
            both = jnp.concatenate([predicted[where], halo[where]], axis=0)
            out_ref[holder[1, s * per_shot + q]] = both.astype(jnp.bfloat16)
    coefficient_ref[...] = filter_lanes(kept_bins, slots, slice_ref, filters_ref, lag_ref)


def subtract_kernel(
    chunk, returned_ref, coefficient_ref, table_ref, gathers_ref, out_ref, spread, result, sems
):
    devices, group_rows, _ = returned_ref.shape
    group_rows = group_rows // 2
    rows = devices * group_rows
    traces, length = gathers_ref.shape
    offsets = coefficient_ref.shape[0]
    came = returned_ref[...].astype(jnp.float32)
    own = came[:, :group_rows].reshape(rows, traces)
    edges = came[:, group_rows:].reshape(rows, traces)
    halo = jnp.transpose(jnp.concatenate([edges, swap_pairs(edges)], axis=0))
    spread[0:8] = halo[traces - 8 :]
    spread[8 : 8 + traces] = jnp.transpose(jnp.concatenate([own, swap_pairs(own)], axis=0))
    spread[8 + traces : 16 + traces] = halo[:8]
    total = jnp.zeros((traces, 2 * rows), jnp.float32)
    for offset in range(offsets):
        first = 8 + offset - offsets // 2
        total = total + spread[first : first + traces] * coefficient_ref[offset : offset + 1]
    total = total + pltpu.roll(total, rows, 1)
    high = total.astype(jnp.bfloat16).astype(jnp.float32)
    lane_ids = lax.broadcasted_iota(jnp.int32, total.shape, 1)
    mixed = jnp.where(lane_ids < rows, high, total - high)
    stacked = jnp.concatenate([mixed, high[:, :rows]], axis=1).astype(jnp.bfloat16)
    copies = []
    start = 0
    for step, width in enumerate((3 * chunk, 2 * chunk, 2 * chunk, chunk)):
        part = pl.ds(start, width)
        start += width
        response = jnp.dot(stacked, table_ref[:, part], preferred_element_type=jnp.float32)
        result[:, part] = gathers_ref[:, part] - response
        copy = pltpu.make_async_copy(result.at[:, part], out_ref.at[:, part], sems.at[step])
        copy.start()
        copies.append(copy)
    for copy in copies:
        copy.wait()


def vmem_spec():
    return pl.BlockSpec(memory_space=pltpu.VMEM)


def smem_spec():
    return pl.BlockSpec(memory_space=pltpu.SMEM)


def hbm_spec():
    return pl.BlockSpec(memory_space=pltpu.HBM)


def in_hbm(values):
    return pltpu.with_memory_space_constraint(values, pltpu.HBM)


def exchange(chunks, order):
    return lax.all_to_all(chunks, "freq", 0, 0, axis_index_groups=[order], tiled=True)


def local(gathers, operator, filters, tile_of, slice_len):
    devices = lax.axis_size("freq")
    traces, length = gathers.shape
    slots, _, receivers, _ = operator.shape
    band_bins = slots * devices
    rows = 2 * band_bins
    group_rows = 2 * slots
    kept_bins = 5 * devices // 4
    offsets, lags = filters.shape[2], filters.shape[3]
    params = pltpu.CompilerParams(vmem_limit_bytes=VMEM_LIMIT)
    bins_out = bins_in_order(order_out(devices), slots)
    bins_back = bins_in_order(order_back(devices), slots)
    forward_table = np.concatenate([
        half
        for parity in range(2)
        for half in split_halves(
            row_tables(bins_out[bins_out % 2 == parity], length)[:, : length // 2]
            / math.sqrt(length)
        )
    ])
    back_high, back_low = split_halves(row_tables(bins_back, length))
    back_table = np.concatenate([back_high, back_high, back_low], axis=0)
    tables = lag_tables(bins_back, lags, length)
    with jax.named_scope("spectrum"):
        outgoing = pl.pallas_call(
            spectrum_kernel,
            out_shape=jax.ShapeDtypeStruct((devices, group_rows, traces), jnp.float32),
            in_specs=[hbm_spec()] * 2,
            out_specs=vmem_spec(),
            scratch_shapes=[
                pltpu.VMEM((traces, length), jnp.float32),
                pltpu.VMEM((2 * rows, length // 2), jnp.bfloat16),
                pltpu.SemaphoreType.DMA((2,)),
            ],
            compiler_params=params,
            cost_estimate=pl.CostEstimate(flops=COST[0], bytes_accessed=COST[1], transcendentals=0),
            name="spectrum",
        )(in_hbm(gathers), in_hbm(jnp.asarray(forward_table)))
    incoming = exchange(outgoing, order_out(devices))
    with jax.named_scope("predict"):
        sending, coefficients = pl.pallas_call(
            functools.partial(predict_kernel, kept_bins),
            out_shape=[
                jax.ShapeDtypeStruct((devices, 2 * group_rows, traces), jnp.bfloat16),
                jax.ShapeDtypeStruct((offsets, 2 * rows), jnp.float32),
            ],
            in_specs=[smem_spec()] * 2 + [vmem_spec()] * 4,
            out_specs=[vmem_spec()] * 2,
            scratch_shapes=[pltpu.SMEM((2, devices), jnp.int32)],
            compiler_params=params,
            name="predict",
        )(
            tile_of,
            slice_len,
            jnp.transpose(filters[0], (1, 0, 2)),
            jnp.asarray(tables),
            incoming,
            operator,
        )
    returned = exchange(sending, order_back(devices))
    with jax.named_scope("subtract"):
        return pl.pallas_call(
            functools.partial(subtract_kernel, length // 8),
            out_shape=jax.ShapeDtypeStruct((traces, length), jnp.float32),
            in_specs=[vmem_spec()] * 4,
            out_specs=hbm_spec(),
            scratch_shapes=[
                pltpu.VMEM((traces + 16, 2 * rows), jnp.float32),
                pltpu.VMEM((traces, length), jnp.float32),
                pltpu.SemaphoreType.DMA((4,)),
            ],
            compiler_params=params,
            name="subtract",
        )(returned, coefficients, jnp.asarray(back_table), gathers)


def solution(mesh):
    placed = (
        P(("survey", "freq"), None),
        P(("survey", "freq"), None, None, None),
        P(("survey", "freq"), None, None, None),
        P("survey"),
        P("survey"),
    )
    return jax.shard_map(
        local, mesh=mesh, in_specs=placed, out_specs=P(("survey", "freq"), None), check_vma=False
    )
```

```python
import functools
import math

import jax
import jax.numpy as jnp
import ml_dtypes
import numpy as np
from jax import lax
from jax.experimental import pallas as pl
from jax.experimental.pallas import tpu as pltpu
from jax.sharding import PartitionSpec as P

FIRST = 40
REACH = 4
COST = (10**11, 40_000_000)
VMEM_LIMIT = 32 * 1024 * 1024


def split_halves(values):
    values = values.astype(np.float32)
    high = values.astype(ml_dtypes.bfloat16)
    low = (values - high.astype(np.float32)).astype(ml_dtypes.bfloat16)
    return high, low


def group_order(root, devices):
    return [root] + [device for device in range(devices)[::-1] if device != root]


def order_out(devices):
    return group_order(3 * devices // 4 - 1, devices)


def order_back(devices):
    return group_order(devices - 1, devices)


def bins_in_order(order, slots):
    return (FIRST + np.array(order)[:, None] * slots + np.arange(slots)).reshape(-1)


def row_tables(bin_ids, length):
    band_bins = len(bin_ids)
    angles = 2.0 * np.pi / length * (bin_ids[:, None] * np.arange(length)[None, :] % length)
    return np.stack([np.cos(angles), -np.sin(angles)], axis=1).reshape(2 * band_bins, length)


def lag_tables(bin_ids, lags, length):
    band_bins = len(bin_ids)
    lag_ids = np.arange(lags) - lags // 2
    angles = 2.0 * np.pi / length * (bin_ids[:, None] * lag_ids[None, :] % length)
    cosine, sine = np.cos(angles), np.sin(angles)
    weight = (bin_ids / (FIRST + band_bins))[:, None]
    real = np.stack([cosine, sine, -weight * sine, weight * cosine])
    imag = np.stack([sine, -cosine, weight * cosine, weight * sine])
    own = np.stack([real, real], axis=2).reshape(4, 2 * band_bins, lags)
    partner = np.stack([-imag, imag], axis=2).reshape(4, 2 * band_bins, lags)
    both = np.concatenate([own, partner], axis=1)
    return np.swapaxes(both, 1, 2).reshape(4 * lags, 4 * band_bins).astype(np.float32)


def split_array(values):
    high = values.astype(jnp.bfloat16)
    low = (values - high.astype(jnp.float32)).astype(jnp.bfloat16)
    return high, low


def swap_pairs(values):
    rows = values.shape[0]
    parity = lax.broadcasted_iota(jnp.int32, values.shape, 0) % 2
    return jnp.where(
        parity == 0, pltpu.roll(values, rows - 1, 0), pltpu.roll(values, 1, 0)
    )


def filter_lanes(kept_bins, slots, slice_ref, filters_ref, lag_ref):
    _, components, _ = filters_ref.shape
    lanes = lag_ref.shape[1]
    rows = lanes // 2
    flat = jnp.concatenate([filters_ref[:, part] for part in range(components)], axis=1)
    total = jnp.dot(
        flat, lag_ref[...], precision=lax.Precision.HIGHEST, preferred_element_type=jnp.float32
    )
    lane_ids = lax.broadcasted_iota(jnp.int32, (1, lanes), 1) % rows
    group = lane_ids // (2 * slots)
    slot = lane_ids // 2 % slots
    count = jnp.zeros((1, lanes), jnp.int32)
    devices = rows // (2 * slots)
    for place, device in enumerate(order_back(devices)):
        count = jnp.where(group == place, slice_ref[device], count)
    return total * jnp.where(slot < count, math.sqrt(2.0 / kept_bins), 0.0)


def spectrum_kernel(gathers_ref, table_ref, out_ref, held, table, sems):
    traces, length = gathers_ref.shape
    rows = table_ref.shape[0] // 2
    devices, group_rows, _ = out_ref.shape
    copies = [
        pltpu.make_async_copy(gathers_ref, held, sems.at[0]),
        pltpu.make_async_copy(table_ref, table, sems.at[1]),
    ]
    for copy in copies:
        copy.start()
    for copy in copies:
        copy.wait()
    dot = functools.partial(
        lax.dot_general,
        dimension_numbers=(((1,), (1,)), ((), ())),
        preferred_element_type=jnp.float32,
    )
    early, late = held[:, : length // 2], held[:, length // 2 :]
    pieces = []
    for parity, folded in enumerate((early + late, early - late)):
        high, low = split_array(folded)
        weights = table[parity * rows : (parity + 1) * rows]
        both = dot(weights, high)
        total = both[: rows // 2] + (both[rows // 2 :] + dot(weights[: rows // 2], low))
        total = total.astype(jnp.bfloat16).astype(out_ref.dtype)
        pieces.append(total.reshape(devices, group_rows // 2, traces))
    out_ref[...] = jnp.concatenate(pieces, axis=1)


def predict_kernel(
    kept_bins,
    tile_ref,
    slice_ref,
    filters_ref,
    lag_ref,
    incoming_ref,
    operator_ref,
    out_ref,
    coefficient_ref,
    holder,
):
    devices, group_rows, traces = incoming_ref.shape
    slots, _, receivers, _ = operator_ref.shape
    per_shot = receivers // traces
    shots = devices // per_shot
    rows = shots * group_rows
    for place, device in enumerate(order_out(devices)):
        holder[0, tile_ref[device]] = place
    for place, device in enumerate(order_back(devices)):
        holder[1, tile_ref[device]] = place
    columns = []
    for q in range(per_shot):
        parts = [
            incoming_ref[holder[0, s * per_shot + q]].astype(jnp.float32) for s in range(shots)
        ]
        columns.append(jnp.concatenate(parts, axis=0))
    spectrum = jnp.concatenate(columns, axis=1).astype(jnp.bfloat16)
    row_ids = lax.broadcasted_iota(jnp.int32, (rows, receivers), 0)
    dot = functools.partial(
        lax.dot_general,
        dimension_numbers=(((1,), (1,)), ((), ())),
        preferred_element_type=jnp.float32,
    )
    predicted = jnp.zeros((rows, receivers), jnp.float32)
    products = dot(spectrum, operator_ref[...].reshape(2 * slots * receivers, receivers))
    for slot in range(slots):
        by_real, by_imag = (
            products[:, (2 * slot + part) * receivers : (2 * slot + part + 1) * receivers]
            for part in range(2)
        )
        by_imag = swap_pairs(by_imag)
        product = jnp.where(row_ids % 2 == 0, by_real - by_imag, by_real + by_imag)
        predicted = jnp.where(row_ids // 2 % slots == slot, product, predicted)
    lane_ids = lax.broadcasted_iota(jnp.int32, (rows, receivers), 1) % traces
    edge = jnp.zeros((rows, traces), jnp.float32)
    after = jnp.concatenate([predicted[:, traces:], edge], axis=1)
    before = jnp.concatenate([edge, predicted[:, :-traces]], axis=1)
    halo = jnp.where(lane_ids < REACH, after, jnp.where(lane_ids >= traces - REACH, before, 0.0))
    for s in range(shots):
        for q in range(per_shot):
            where = (slice(s * group_rows, (s + 1) * group_rows), slice(q * traces, (q + 1) * traces))
            both = jnp.concatenate([predicted[where], halo[where]], axis=0)
            out_ref[holder[1, s * per_shot + q]] = both.astype(jnp.bfloat16)
    coefficient_ref[...] = filter_lanes(kept_bins, slots, slice_ref, filters_ref, lag_ref)


def subtract_kernel(
    chunk, returned_ref, coefficient_ref, table_ref, gathers_ref, out_ref, spread, result, sems
):
    devices, group_rows, _ = returned_ref.shape
    group_rows = group_rows // 2
    rows = devices * group_rows
    traces, length = gathers_ref.shape
    offsets = coefficient_ref.shape[0]
    came = returned_ref[...].astype(jnp.float32)
    own = came[:, :group_rows].reshape(rows, traces)
    edges = came[:, group_rows:].reshape(rows, traces)
    halo = jnp.transpose(jnp.concatenate([edges, swap_pairs(edges)], axis=0))
    spread[0:8] = halo[traces - 8 :]
    spread[8 : 8 + traces] = jnp.transpose(jnp.concatenate([own, swap_pairs(own)], axis=0))
    spread[8 + traces : 16 + traces] = halo[:8]
    total = jnp.zeros((traces, 2 * rows), jnp.float32)
    for offset in range(offsets):
        first = 8 + offset - offsets // 2
        total = total + spread[first : first + traces] * coefficient_ref[offset : offset + 1]
    total = total + pltpu.roll(total, rows, 1)
    high = total.astype(jnp.bfloat16).astype(jnp.float32)
    lane_ids = lax.broadcasted_iota(jnp.int32, total.shape, 1)
    mixed = jnp.where(lane_ids < rows, high, total - high)
    stacked = jnp.concatenate([mixed, high[:, :rows]], axis=1).astype(jnp.bfloat16)
    copies = []
    start = 0
    for step, width in enumerate((3 * chunk, 2 * chunk, 2 * chunk, chunk)):
        part = pl.ds(start, width)
        start += width
        response = jnp.dot(stacked, table_ref[:, part], preferred_element_type=jnp.float32)
        result[:, part] = gathers_ref[:, part] - response
        copy = pltpu.make_async_copy(result.at[:, part], out_ref.at[:, part], sems.at[step])
        copy.start()
        copies.append(copy)
    for copy in copies:
        copy.wait()


def vmem_spec():
    return pl.BlockSpec(memory_space=pltpu.VMEM)


def smem_spec():
    return pl.BlockSpec(memory_space=pltpu.SMEM)


def hbm_spec():
    return pl.BlockSpec(memory_space=pltpu.HBM)


def in_hbm(values):
    return pltpu.with_memory_space_constraint(values, pltpu.HBM)


def exchange(chunks, order):
    return lax.all_to_all(chunks, "freq", 0, 0, axis_index_groups=[order], tiled=True)


def local(gathers, operator, filters, tile_of, slice_len):
    devices = lax.axis_size("freq")
    traces, length = gathers.shape
    slots, _, receivers, _ = operator.shape
    band_bins = slots * devices
    rows = 2 * band_bins
    group_rows = 2 * slots
    kept_bins = 5 * devices // 4
    offsets, lags = filters.shape[2], filters.shape[3]
    params = pltpu.CompilerParams(vmem_limit_bytes=VMEM_LIMIT)
    bins_out = bins_in_order(order_out(devices), slots)
    bins_back = bins_in_order(order_back(devices), slots)
    forward_table = np.concatenate([
        half
        for parity in range(2)
        for half in split_halves(
            row_tables(bins_out[bins_out % 2 == parity], length)[:, : length // 2]
            / math.sqrt(length)
        )
    ])
    back_high, back_low = split_halves(row_tables(bins_back, length))
    back_table = np.concatenate([back_high, back_high, back_low], axis=0)
    tables = lag_tables(bins_back, lags, length)
    with jax.named_scope("spectrum"):
        outgoing = pl.pallas_call(
            spectrum_kernel,
            out_shape=jax.ShapeDtypeStruct((devices, group_rows, traces), jnp.float32),
            in_specs=[hbm_spec()] * 2,
            out_specs=vmem_spec(),
            scratch_shapes=[
                pltpu.VMEM((traces, length), jnp.float32),
                pltpu.VMEM((2 * rows, length // 2), jnp.bfloat16),
                pltpu.SemaphoreType.DMA((2,)),
            ],
            compiler_params=params,
            cost_estimate=pl.CostEstimate(flops=COST[0], bytes_accessed=COST[1], transcendentals=0),
            name="spectrum",
        )(in_hbm(gathers), in_hbm(jnp.asarray(forward_table)))
    incoming = exchange(outgoing, order_out(devices))
    with jax.named_scope("predict"):
        sending, coefficients = pl.pallas_call(
            functools.partial(predict_kernel, kept_bins),
            out_shape=[
                jax.ShapeDtypeStruct((devices, 2 * group_rows, traces), jnp.bfloat16),
                jax.ShapeDtypeStruct((offsets, 2 * rows), jnp.float32),
            ],
            in_specs=[smem_spec()] * 2 + [vmem_spec()] * 4,
            out_specs=[vmem_spec()] * 2,
            scratch_shapes=[pltpu.SMEM((2, devices), jnp.int32)],
            compiler_params=params,
            name="predict",
        )(
            tile_of,
            slice_len,
            jnp.transpose(filters[0], (1, 0, 2)),
            jnp.asarray(tables),
            incoming,
            operator,
        )
    returned = exchange(sending, order_back(devices))
    with jax.named_scope("subtract"):
        return pl.pallas_call(
            functools.partial(subtract_kernel, length // 8),
            out_shape=jax.ShapeDtypeStruct((traces, length), jnp.float32),
            in_specs=[vmem_spec()] * 4,
            out_specs=hbm_spec(),
            scratch_shapes=[
                pltpu.VMEM((traces + 16, 2 * rows), jnp.float32),
                pltpu.VMEM((traces, length), jnp.float32),
                pltpu.SemaphoreType.DMA((4,)),
            ],
            compiler_params=params,
            name="subtract",
        )(returned, coefficients, jnp.asarray(back_table), gathers)


def solution(mesh):
    placed = (
        P(("survey", "freq"), None),
        P(("survey", "freq"), None, None, None),
        P(("survey", "freq"), None, None, None),
        P("survey"),
        P("survey"),
    )
    return jax.shard_map(
        local, mesh=mesh, in_specs=placed, out_specs=P(("survey", "freq"), None), check_vma=False
    )
```

```python
import functools
import math

import jax
import jax.numpy as jnp
import ml_dtypes
import numpy as np
from jax import lax
from jax.experimental import pallas as pl
from jax.experimental.pallas import tpu as pltpu
from jax.sharding import PartitionSpec as P

FIRST = 40
REACH = 4
COST = (10**11, 40_000_000)
VMEM_LIMIT = 32 * 1024 * 1024


def split_halves(values):
    values = values.astype(np.float32)
    high = values.astype(ml_dtypes.bfloat16)
    low = (values - high.astype(np.float32)).astype(ml_dtypes.bfloat16)
    return high, low


def group_order(root, devices):
    return [root] + [device for device in range(devices)[::-1] if device != root]


def order_out(devices):
    return group_order(3 * devices // 4 - 1, devices)


def order_back(devices):
    return group_order(devices - 1, devices)


def bins_in_order(order, slots):
    return (FIRST + np.array(order)[:, None] * slots + np.arange(slots)).reshape(-1)


def row_tables(bin_ids, length):
    band_bins = len(bin_ids)
    angles = 2.0 * np.pi / length * (bin_ids[:, None] * np.arange(length)[None, :] % length)
    return np.stack([np.cos(angles), -np.sin(angles)], axis=1).reshape(2 * band_bins, length)


def lag_tables(bin_ids, lags, length):
    band_bins = len(bin_ids)
    lag_ids = np.arange(lags) - lags // 2
    angles = 2.0 * np.pi / length * (bin_ids[:, None] * lag_ids[None, :] % length)
    cosine, sine = np.cos(angles), np.sin(angles)
    weight = (bin_ids / (FIRST + band_bins))[:, None]
    real = np.stack([cosine, sine, -weight * sine, weight * cosine])
    imag = np.stack([sine, -cosine, weight * cosine, weight * sine])
    own = np.stack([real, real], axis=2).reshape(4, 2 * band_bins, lags)
    partner = np.stack([-imag, imag], axis=2).reshape(4, 2 * band_bins, lags)
    both = np.concatenate([own, partner], axis=1)
    return np.swapaxes(both, 1, 2).reshape(4 * lags, 4 * band_bins).astype(np.float32)


def split_array(values):
    high = values.astype(jnp.bfloat16)
    low = (values - high.astype(jnp.float32)).astype(jnp.bfloat16)
    return high, low


def swap_pairs(values):
    rows = values.shape[0]
    parity = lax.broadcasted_iota(jnp.int32, values.shape, 0) % 2
    return jnp.where(
        parity == 0, pltpu.roll(values, rows - 1, 0), pltpu.roll(values, 1, 0)
    )


def filter_lanes(kept_bins, slots, slice_ref, filters_ref, lag_ref):
    _, components, _ = filters_ref.shape
    lanes = lag_ref.shape[1]
    rows = lanes // 2
    flat = jnp.concatenate([filters_ref[:, part] for part in range(components)], axis=1)
    total = jnp.dot(
        flat, lag_ref[...], precision=lax.Precision.HIGHEST, preferred_element_type=jnp.float32
    )
    lane_ids = lax.broadcasted_iota(jnp.int32, (1, lanes), 1) % rows
    group = lane_ids // (2 * slots)
    slot = lane_ids // 2 % slots
    count = jnp.zeros((1, lanes), jnp.int32)
    devices = rows // (2 * slots)
    for place, device in enumerate(order_back(devices)):
        count = jnp.where(group == place, slice_ref[device], count)
    return total * jnp.where(slot < count, math.sqrt(2.0 / kept_bins), 0.0)


def spectrum_kernel(gathers_ref, table_ref, out_ref, held, table, sems):
    traces, length = gathers_ref.shape
    rows = table_ref.shape[0] // 2
    devices, group_rows, _ = out_ref.shape
    copies = [
        pltpu.make_async_copy(gathers_ref, held, sems.at[0]),
        pltpu.make_async_copy(table_ref, table, sems.at[1]),
    ]
    for copy in copies:
        copy.start()
    for copy in copies:
        copy.wait()
    dot = functools.partial(
        lax.dot_general,
        dimension_numbers=(((1,), (1,)), ((), ())),
        preferred_element_type=jnp.float32,
    )
    early, late = held[:, : length // 2], held[:, length // 2 :]
    pieces = []
    for parity, folded in enumerate((early + late, early - late)):
        high, low = split_array(folded)
        weights = table[parity * rows : (parity + 1) * rows]
        both = dot(weights, high)
        total = both[: rows // 2] + (both[rows // 2 :] + dot(weights[: rows // 2], low))
        total = total.astype(jnp.bfloat16).astype(out_ref.dtype)
        pieces.append(total.reshape(devices, group_rows // 2, traces))
    out_ref[...] = jnp.concatenate(pieces, axis=1)


def predict_kernel(
    kept_bins,
    tile_ref,
    slice_ref,
    filters_ref,
    lag_ref,
    incoming_ref,
    operator_ref,
    out_ref,
    coefficient_ref,
    holder,
):
    devices, group_rows, traces = incoming_ref.shape
    slots, _, receivers, _ = operator_ref.shape
    per_shot = receivers // traces
    shots = devices // per_shot
    rows = shots * group_rows
    for place, device in enumerate(order_out(devices)):
        holder[0, tile_ref[device]] = place
    for place, device in enumerate(order_back(devices)):
        holder[1, tile_ref[device]] = place
    columns = []
    for q in range(per_shot):
        parts = [
            incoming_ref[holder[0, s * per_shot + q]].astype(jnp.float32) for s in range(shots)
        ]
        columns.append(jnp.concatenate(parts, axis=0))
    spectrum = jnp.concatenate(columns, axis=1).astype(jnp.bfloat16)
    row_ids = lax.broadcasted_iota(jnp.int32, (rows, receivers), 0)
    dot = functools.partial(
        lax.dot_general,
        dimension_numbers=(((1,), (1,)), ((), ())),
        preferred_element_type=jnp.float32,
    )
    predicted = jnp.zeros((rows, receivers), jnp.float32)
    for slot in range(slots):
        by_real = dot(spectrum, operator_ref[slot, 0])
        by_imag = swap_pairs(dot(spectrum, operator_ref[slot, 1]))
        product = jnp.where(row_ids % 2 == 0, by_real - by_imag, by_real + by_imag)
        predicted = jnp.where(row_ids // 2 % slots == slot, product, predicted)
    lane_ids = lax.broadcasted_iota(jnp.int32, (rows, receivers), 1) % traces
    edge = jnp.zeros((rows, traces), jnp.float32)
    after = jnp.concatenate([predicted[:, traces:], edge], axis=1)
    before = jnp.concatenate([edge, predicted[:, :-traces]], axis=1)
    halo = jnp.where(lane_ids < REACH, after, jnp.where(lane_ids >= traces - REACH, before, 0.0))
    for s in range(shots):
        for q in range(per_shot):
            where = (slice(s * group_rows, (s + 1) * group_rows), slice(q * traces, (q + 1) * traces))
            both = jnp.concatenate([predicted[where], halo[where]], axis=0)
            out_ref[holder[1, s * per_shot + q]] = both.astype(jnp.bfloat16)
    coefficient_ref[...] = filter_lanes(kept_bins, slots, slice_ref, filters_ref, lag_ref)


def subtract_kernel(
    chunk, returned_ref, coefficient_ref, table_ref, gathers_ref, out_ref, spread, result, sems
):
    devices, group_rows, _ = returned_ref.shape
    group_rows = group_rows // 2
    rows = devices * group_rows
    traces, length = gathers_ref.shape
    offsets = coefficient_ref.shape[0]
    came = returned_ref[...].astype(jnp.float32)
    own = came[:, :group_rows].reshape(rows, traces)
    edges = came[:, group_rows:].reshape(rows, traces)
    halo = jnp.transpose(jnp.concatenate([edges, swap_pairs(edges)], axis=0))
    spread[0:8] = halo[traces - 8 :]
    spread[8 : 8 + traces] = jnp.transpose(jnp.concatenate([own, swap_pairs(own)], axis=0))
    spread[8 + traces : 16 + traces] = halo[:8]
    total = jnp.zeros((traces, 2 * rows), jnp.float32)
    for offset in range(offsets):
        first = 8 + offset - offsets // 2
        total = total + spread[first : first + traces] * coefficient_ref[offset : offset + 1]
    total = total + pltpu.roll(total, rows, 1)
    high = total.astype(jnp.bfloat16).astype(jnp.float32)
    lane_ids = lax.broadcasted_iota(jnp.int32, total.shape, 1)
    mixed = jnp.where(lane_ids < rows, high, total - high)
    stacked = jnp.concatenate([mixed, high[:, :rows]], axis=1).astype(jnp.bfloat16)
    copies = []
    start = 0
    for step, width in enumerate((3 * chunk, 2 * chunk, 2 * chunk, chunk)):
        part = pl.ds(start, width)
        start += width
        response = jnp.dot(stacked, table_ref[:, part], preferred_element_type=jnp.float32)
        result[:, part] = gathers_ref[:, part] - response
        copy = pltpu.make_async_copy(result.at[:, part], out_ref.at[:, part], sems.at[step])
        copy.start()
        copies.append(copy)
    for copy in copies:
        copy.wait()


def vmem_spec():
    return pl.BlockSpec(memory_space=pltpu.VMEM)


def smem_spec():
    return pl.BlockSpec(memory_space=pltpu.SMEM)


def hbm_spec():
    return pl.BlockSpec(memory_space=pltpu.HBM)


def in_hbm(values):
    return pltpu.with_memory_space_constraint(values, pltpu.HBM)


def exchange(chunks, order):
    return lax.all_to_all(chunks, "freq", 0, 0, axis_index_groups=[order], tiled=True)


def local(gathers, operator, filters, tile_of, slice_len):
    devices = lax.axis_size("freq")
    traces, length = gathers.shape
    slots, _, receivers, _ = operator.shape
    band_bins = slots * devices
    rows = 2 * band_bins
    group_rows = 2 * slots
    kept_bins = 5 * devices // 4
    offsets, lags = filters.shape[2], filters.shape[3]
    params = pltpu.CompilerParams(vmem_limit_bytes=VMEM_LIMIT)
    bins_out = bins_in_order(order_out(devices), slots)
    bins_back = bins_in_order(order_back(devices), slots)
    forward_table = np.concatenate([
        half
        for parity in range(2)
        for half in split_halves(
            row_tables(bins_out[bins_out % 2 == parity], length)[:, : length // 2]
            / math.sqrt(length)
        )
    ])
    back_high, back_low = split_halves(row_tables(bins_back, length))
    back_table = np.concatenate([back_high, back_high, back_low], axis=0)
    tables = lag_tables(bins_back, lags, length)
    with jax.named_scope("spectrum"):
        outgoing = pl.pallas_call(
            spectrum_kernel,
            out_shape=jax.ShapeDtypeStruct((devices, group_rows, traces), jnp.bfloat16),
            in_specs=[hbm_spec()] * 2,
            out_specs=vmem_spec(),
            scratch_shapes=[
                pltpu.VMEM((traces, length), jnp.float32),
                pltpu.VMEM((2 * rows, length // 2), jnp.bfloat16),
                pltpu.SemaphoreType.DMA((2,)),
            ],
            compiler_params=params,
            cost_estimate=pl.CostEstimate(flops=COST[0], bytes_accessed=COST[1], transcendentals=0),
            name="spectrum",
        )(in_hbm(gathers), in_hbm(jnp.asarray(forward_table)))
    incoming = exchange(outgoing, order_out(devices))
    with jax.named_scope("predict"):
        sending, coefficients = pl.pallas_call(
            functools.partial(predict_kernel, kept_bins),
            out_shape=[
                jax.ShapeDtypeStruct((devices, 2 * group_rows, traces), jnp.bfloat16),
                jax.ShapeDtypeStruct((offsets, 2 * rows), jnp.float32),
            ],
            in_specs=[smem_spec()] * 2 + [vmem_spec()] * 4,
            out_specs=[vmem_spec()] * 2,
            scratch_shapes=[pltpu.SMEM((2, devices), jnp.int32)],
            compiler_params=params,
            name="predict",
        )(
            tile_of,
            slice_len,
            jnp.transpose(filters[0], (1, 0, 2)),
            jnp.asarray(tables),
            incoming,
            operator,
        )
    returned = exchange(sending, order_back(devices))
    with jax.named_scope("subtract"):
        return pl.pallas_call(
            functools.partial(subtract_kernel, length // 8),
            out_shape=jax.ShapeDtypeStruct((traces, length), jnp.float32),
            in_specs=[vmem_spec()] * 4,
            out_specs=hbm_spec(),
            scratch_shapes=[
                pltpu.VMEM((traces + 16, 2 * rows), jnp.float32),
                pltpu.VMEM((traces, length), jnp.float32),
                pltpu.SemaphoreType.DMA((4,)),
            ],
            compiler_params=params,
            name="subtract",
        )(returned, coefficients, jnp.asarray(back_table), gathers)


def solution(mesh):
    placed = (
        P(("survey", "freq"), None),
        P(("survey", "freq"), None, None, None),
        P(("survey", "freq"), None, None, None),
        P("survey"),
        P("survey"),
    )
    return jax.shard_map(
        local, mesh=mesh, in_specs=placed, out_specs=P(("survey", "freq"), None), check_vma=False
    )
```
